128 devices in a mesh: enc: 4 (over y_lo, core), lon: 32 (over x, z, y_hi).
Axes of the slice: x: 4, y: 4 (y_hi: 2, y_lo: 2; y = y_hi * 2 + y_lo), z: 4, core: 2. Of those that a mesh axis runs over, the one named last changes fastest.
Arguments:
- pixel_field: bfloat16 [52, 24, 100, 384], P('enc', None, None, 'lon'), may hold values from -6 to 6
- level_ids: int32 [52], replicated, may hold values from 0 to 51, each once
- embed_weight: bfloat16 [52, 100, 512], replicated, may hold values from -0.625 to 0.625
- embed_bias: bfloat16 [52, 512], replicated, may hold values from -6 to 6
- latents: bfloat16 [4, 512], replicated, may hold values from -6 to 6
- query_weight: bfloat16 [512, 512], replicated, may hold values from -0.25 to 0.25
- key_weight: bfloat16 [512, 512], replicated, may hold values from -0.25 to 0.25
- value_weight: bfloat16 [512, 512], replicated, may hold values from -0.25 to 0.25
- pool_weight: bfloat16 [512, 512], replicated, may hold values from -0.25 to 0.25
- pool_temp: float32 [16], replicated, may hold values from 0.5 to 6
- first_gain: float32 [512], replicated, may hold values from 0.1 to 1.9
- qkv_weight: bfloat16 [512, 1536], replicated, may hold values from -0.25 to 0.25
- window_temp: float32 [16], replicated, may hold values from 0.5 to 6
- proj_weight: bfloat16 [512, 512], replicated, may hold values from -0.25 to 0.25
- second_gain: float32 [512], replicated, may hold values from 0.1 to 1.9
- up_weight: bfloat16 [512, 2048], replicated, may hold values from -0.25 to 0.25
- down_weight: bfloat16 [2048, 512], replicated, may hold values from -0.125 to 0.125
- cotangent: bfloat16 [4, 24, 384, 512], P(None, 'enc', 'lon'), may hold values from -6 to 6
Outputs:
- layer_out: bfloat16 [4, 24, 384, 512], P(None, 'enc', 'lon')
- up_grad: float32 [512, 2048], replicated
- down_grad: float32 [2048, 512], replicated
The draws below stay inside these ranges and needn't reach their ends.
Inputs may be any that keep to these rules, and one draw needn't show every extreme that they name: A permutation: slot s of pixel_field holds variable-level level_ids[s].
All inputs are finite; a program needn't handle non-finite values.
Results may differ from the reference program's by a relative error of at most 0.023.
Values may be sent and summed in bfloat16 or wider, within the bound.
A program may use at most 192 MiB of HBM per device.

```python
import math
import jax
import jax.numpy as jnp
from jax import lax

D = 512
HEADS = 16
FF = 2048
LATENT = 4
PIX = 100
WD = 2
WH = 6
WW = 12
VLEV = 52
LAT = 24
LONP = 384
NTOK = 36864


def draw_pool_temp(key, part):
    key = jax.random.fold_in(key, 11)
    return jnp.exp(jax.random.uniform(key, (HEADS,), jnp.float32, math.log(0.5), math.log(2.0)))


def draw_window_temp(key, part):
    key = jax.random.fold_in(key, 23)
    return jnp.exp(jax.random.uniform(key, (HEADS,), jnp.float32, math.log(0.5), math.log(2.0)))


def block_scale(rng, extent, cuts, least, top_value):
    def one(axis_at, blocks):
        steps = jax.random.uniform(jax.random.fold_in(jax.random.fold_in(rng, 6), axis_at), (blocks,), jnp.float32, least / len(cuts), top_value / len(cuts))
        return jnp.repeat(jnp.exp(steps), extent[axis_at] // blocks).reshape((-1,) + (1,) * (len(extent) - axis_at - 1))

    loudness = one(*cuts[0])
    for cut in cuts[1:]:
        loudness = loudness * one(*cut)
    return loudness


def bell_draw(own_key, shape, scale, bound, split=(), kind=jnp.bfloat16):
    values = scale * jax.random.normal(own_key, shape, jnp.float32)
    if split:
        values = values * block_scale(own_key, shape, split, -0.22, 0.18)
    return jnp.clip(values, -bound, bound).astype(kind)


def setup_inputs(seed: int = 0) -> dict:
    splits = jax.random.split(jax.random.key(seed), 19)
    return {
        "pixel_field": bell_draw(splits[0], (VLEV, LAT, PIX, LONP), 1.0, 6.0, ((0, 4), (3, 32))),
        "level_ids": jax.random.permutation(splits[1], VLEV).astype(jnp.int32),
        "embed_weight": bell_draw(splits[2], (VLEV, PIX, D), PIX ** -0.5, 0.625),
        "embed_bias": bell_draw(splits[3], (VLEV, D), 1.0, 6.0),
        "latents": bell_draw(splits[4], (LATENT, D), 1.0, 6.0),
        "query_weight": bell_draw(splits[5], (D, D), D ** -0.5, 0.25),
        "key_weight": bell_draw(splits[6], (D, D), D ** -0.5, 0.25),
        "value_weight": bell_draw(splits[7], (D, D), D ** -0.5, 0.25),
        "pool_weight": bell_draw(splits[8], (D, D), D ** -0.5, 0.25),
        "pool_temp": draw_pool_temp(jax.random.fold_in(splits[18], 71), 0),
        "first_gain": jnp.clip(1.0 + 0.18 * jax.random.normal(splits[10], (D,), jnp.float32), 0.1, 1.9),
        "qkv_weight": bell_draw(splits[11], (D, 3 * D), D ** -0.5, 0.25),
        "window_temp": draw_window_temp(jax.random.fold_in(splits[18], 71), 0),
        "proj_weight": bell_draw(splits[13], (D, D), D ** -0.5, 0.25),
        "second_gain": jnp.clip(1.0 + 0.18 * jax.random.normal(splits[14], (D,), jnp.float32), 0.1, 1.9),
        "up_weight": bell_draw(splits[15], (D, FF), D ** -0.5, 0.25),
        "down_weight": bell_draw(splits[16], (FF, D), FF ** -0.5, 0.125),
        "cotangent": bell_draw(splits[17], (LATENT, LAT, LONP, D), 1.0, 6.0, ((1, 4), (2, 32))),
    }


epsilon = 1e-05
highest = lax.Precision.HIGHEST

def layer_norm(values, gain_vector):
    values = values.astype(jnp.float32)
    row_mean = lax.optimization_barrier(jnp.mean(values, axis=-1, keepdims=True))
    centred = values - row_mean
    variance = lax.optimization_barrier(jnp.mean(centred * centred, axis=-1, keepdims=True))
    return centred * lax.rsqrt(variance + epsilon) * gain_vector

def fold_keys(latents, query_weight, key_weight, pool_temp):
    head_count = pool_temp.shape[0]
    model_width = latents.shape[1]
    head_width = model_width // head_count
    queries = jnp.dot(latents, query_weight, preferred_element_type=jnp.float32).astype(jnp.bfloat16)
    folded = jnp.einsum('dhe,lhe->lhd', key_weight.astype(jnp.float32).reshape(model_width, head_count, head_width), queries.astype(jnp.float32).reshape(-1, head_count, head_width), precision=highest)
    return folded * (pool_temp / math.sqrt(head_width))[None, :, None]

def finish_pool(values, pool_weight, latents):
    pooled = values.astype(jnp.bfloat16)
    array_shape = pooled.shape
    projected = jnp.dot(pooled.reshape(-1, array_shape[-1]), pool_weight, preferred_element_type=jnp.float32)
    projected = projected.reshape(array_shape)
    expanded = latents.astype(jnp.float32).reshape((array_shape[0],) + (1,) * (len(array_shape) - 2) + (array_shape[-1],))
    return (projected + expanded).astype(jnp.bfloat16)

def key_mask(levels, padded_rows, first_row, slab_rows):
    level_index = jnp.arange(levels + WD, dtype=jnp.int32)
    level_ok = (level_index >= WD // 2) & (level_index < WD // 2 + levels)
    global_row = first_row - WH // 2 + jnp.arange(padded_rows, dtype=jnp.int32)
    row_ok = (global_row >= 0) & (global_row < slab_rows)
    return level_ok[:, None] & row_ok[None, :]

def window_attention(projected, key_valid, window_temp):
    levels, rows, cols, triple = projected.shape
    model_width = triple // 3
    head_count = window_temp.shape[0]
    head_width = model_width // head_count
    level_wins = levels // WD
    col_wins = cols // WW
    blocks = projected.reshape(level_wins, WD, rows // WH, WH, col_wins, WW, 3, head_count, head_width)
    masks = key_valid.reshape(level_wins, WD, rows // WH, WH)
    factor = window_temp / math.sqrt(head_width)

    def one_band(inputs):
        band_tokens, band_mask = inputs
        windows = jnp.transpose(band_tokens, (0, 3, 1, 2, 4, 5, 6, 7)).reshape(level_wins * col_wins, WD * WH * WW, 3, head_count, head_width)
        key_ok = jnp.broadcast_to(band_mask[:, None, :, :, None], (level_wins, col_wins, WD, WH, WW))
        key_ok = key_ok.reshape(level_wins * col_wins, WD * WH * WW)
        queries = windows[:, :, 0].astype(jnp.float32)
        keys_part = windows[:, :, 1].astype(jnp.float32)
        values = windows[:, :, 2].astype(jnp.float32)
        scores = jnp.einsum('wnhe,wmhe->whnm', queries, keys_part) * factor[None, :, None, None]
        scores = jnp.where(key_ok[:, None, None, :], scores, -jnp.inf)
        peak_score = lax.optimization_barrier(jnp.max(scores, axis=-1, keepdims=True))
        exponent = jnp.exp(scores - peak_score)
        weights = (exponent / lax.optimization_barrier(jnp.sum(exponent, axis=-1, keepdims=True))).astype(jnp.bfloat16)
        result = jnp.einsum('whnm,wmhe->wnhe', weights.astype(jnp.float32), values).astype(jnp.bfloat16)
        result = result.reshape(level_wins, col_wins, WD, WH, WW, model_width)
        return jnp.transpose(result, (0, 2, 3, 1, 4, 5)).reshape(levels, WH, cols, model_width)
    bands = lax.map(one_band, (jnp.moveaxis(blocks, 2, 0), jnp.moveaxis(masks, 2, 0)))
    return jnp.moveaxis(bands, 0, 1).reshape(levels, rows, cols, model_width)

def pool_row(tokens, folded, value_weight, pool_weight, latents):
    head_count = folded.shape[1]
    model_width = tokens.shape[-1]
    head_width = model_width // head_count
    token_values = tokens.astype(jnp.float32)
    scores = jnp.einsum('spd,lhd->lhsp', token_values, folded, precision=highest)
    peak_score = lax.optimization_barrier(jnp.max(scores, axis=2, keepdims=True))
    exponent = jnp.exp(scores - peak_score)
    totals = lax.optimization_barrier(jnp.sum(exponent, axis=2))
    mixture = jnp.einsum('lhsp,spd->lhpd', exponent, token_values, precision=highest)
    values = jnp.einsum('lhpd,dhe->lphe', mixture, value_weight.astype(jnp.float32).reshape(model_width, head_count, head_width), precision=highest)
    values = values / jnp.transpose(totals, (0, 2, 1))[..., None]
    return finish_pool(values.reshape(values.shape[0], values.shape[1], model_width), pool_weight, latents)

def reference(pixel_field, level_ids, embed_weight, embed_bias, latents, query_weight, key_weight, value_weight, pool_weight, pool_temp, first_gain, qkv_weight, window_temp, proj_weight, second_gain, up_weight, down_weight, cotangent):
    slot_table = embed_weight[level_ids].astype(jnp.float32)
    slot_offsets = embed_bias[level_ids].astype(jnp.float32)
    folded = fold_keys(latents, query_weight, key_weight, pool_temp)

    def one_row(pixels):
        tokens = jnp.einsum('spc,spd->scd', pixels.astype(jnp.float32), slot_table) + slot_offsets[:, None, :]
        return pool_row(tokens.astype(jnp.bfloat16), folded, value_weight, pool_weight, latents)
    stream = jnp.moveaxis(lax.map(one_row, jnp.moveaxis(pixel_field, 1, 0)), 0, 1)
    levels, rows, cols, model_width = stream.shape
    half_width = WW // 2
    level_pad = WD // 2
    row_pad = WH // 2
    first_norm = layer_norm(stream, first_gain).astype(jnp.bfloat16)
    projected = jnp.dot(first_norm.reshape(-1, model_width), qkv_weight, preferred_element_type=jnp.float32)
    projected = projected.astype(jnp.bfloat16).reshape(levels, rows, cols, 3 * model_width)
    padded = jnp.pad(projected, ((level_pad, level_pad), (row_pad, row_pad), (0, 0), (0, 0)))
    rolled = jnp.roll(padded, -half_width, axis=2)
    key_valid = key_mask(levels, rows + 2 * row_pad, 0, rows)
    attended = window_attention(rolled, key_valid, window_temp)[level_pad:level_pad + levels, row_pad:row_pad + rows]
    attended = jnp.roll(attended, half_width, axis=2)
    scaling = 1.0 / math.sqrt(NTOK)

    def level_step(carry, inputs):
        up_total, down_total = carry
        stream_part, attended_part, cot_part = inputs
        flat_rows = stream_part.reshape(-1, model_width)
        middle = (flat_rows.astype(jnp.float32) + jnp.dot(attended_part.reshape(-1, model_width), proj_weight, preferred_element_type=jnp.float32)).astype(jnp.bfloat16)
        second_norm = layer_norm(middle, second_gain).astype(jnp.bfloat16)
        pre_act = jnp.dot(second_norm, up_weight, preferred_element_type=jnp.float32)
        hidden = jax.nn.gelu(pre_act).astype(jnp.bfloat16)
        output = (middle.astype(jnp.float32) + jnp.dot(hidden, down_weight, preferred_element_type=jnp.float32)).astype(jnp.bfloat16)
        cot_rows = cot_part.reshape(-1, model_width)
        down_total = down_total + jnp.dot(hidden.T, cot_rows, preferred_element_type=jnp.float32)
        back_grad = jnp.dot(cot_rows, down_weight.T, preferred_element_type=jnp.float32)
        slope_grad = jax.vjp(jax.nn.gelu, pre_act)[1](back_grad)[0].astype(jnp.bfloat16)
        up_total = up_total + jnp.dot(second_norm.T, slope_grad, preferred_element_type=jnp.float32)
        return ((up_total, down_total), output.reshape(stream_part.shape))
    start_carry = (jnp.zeros((model_width, up_weight.shape[1]), jnp.float32), jnp.zeros((up_weight.shape[1], model_width), jnp.float32))
    (up_total, down_total), layer_out = lax.scan(level_step, start_carry, (stream, attended, cotangent))
    return (layer_out, up_total * scaling, down_total * scaling)
```

```python
import functools
import math

import jax
import jax.numpy as jnp
import numpy as np
from jax import lax
from jax.experimental import pallas as pl
from jax.experimental.pallas import tpu as pltpu
from jax.sharding import PartitionSpec as P

SLOTS = 52
HEADS = 16
HEAD_WIDTH = 32
WIDTH = 512
FF = 2048
LEVELS = 4
ROWS = 6
COLS = 12
SPOTS = ROWS * COLS
TOKENS = LEVELS * SPOTS
HALF = TOKENS // 2
PIXELS = 100
EPSILON = 1e-05
NTOK = 36864
PARTS = 4
PART_ROWS = 1024
PART_COLS = 256
MESH = pl.DeviceIdType.MESH

f32 = jnp.float32
bf16 = jnp.bfloat16


def dot(a, b, contract=((1,), (0,))):
    return lax.dot_general(a, b, (contract, ((), ())), preferred_element_type=f32)


def normed(values, gain):
    mean = jnp.mean(values, axis=-1, keepdims=True)
    centred = values - mean
    variance = jnp.mean(centred * centred, axis=-1, keepdims=True)
    return (centred * lax.rsqrt(variance + EPSILON) * gain).astype(bf16)


def head_rows():
    mask = np.zeros((HEADS, WIDTH), np.float32)
    for h in range(HEADS):
        mask[h, h * HEAD_WIDTH : (h + 1) * HEAD_WIDTH] = 1.0
    return mask


def spread_matrix():
    one = np.zeros((LEVELS * HEADS, LEVELS * WIDTH), np.float32)
    for l in range(LEVELS):
        for h in range(HEADS):
            at = l * WIDTH + h * HEAD_WIDTH
            one[l * HEADS + h, at : at + HEAD_WIDTH] = 1.0
    return np.concatenate([one, one], axis=0)


def order_matrix():
    matrix = np.zeros((TOKENS, TOKENS), np.float32)
    for half in range(2):
        for r in range(ROWS):
            for c in range(COLS // 2):
                for l in range(LEVELS):
                    to = half * HALF + (r * (COLS // 2) + c) * LEVELS + l
                    source = l * SPOTS + (half * (COLS // 2) + c) * ROWS + r
                    matrix[to, source] = 1.0
    return matrix


def pool_kernel(
    ids,
    pixels,
    embed_weight,
    embed_bias,
    latents,
    query_weight,
    key_weight,
    value_weight,
    pool_weight,
    temp,
    heads,
    spread,
    order,
    left,
    right,
    tokens,
    scores,
    values,
    sums,
):
    queries = dot(latents[...], query_weight[...]).astype(bf16).astype(f32)
    blocks = [queries[l : l + 1] * heads[...] for l in range(LEVELS)]
    blocks = jnp.concatenate(blocks, axis=0).astype(bf16)
    folded = dot(blocks, key_weight[...], ((1,), (1,))) * temp[...]
    high = folded.astype(bf16)
    low = (folded - high.astype(f32)).astype(bf16)
    keys = jnp.concatenate([high, high, low, low], axis=0)

    def embed(pair, _):
        both = []
        for i in range(2):
            slot = pair * 2 + i
            level = ids[slot]
            both.append(
                dot(pixels[slot], embed_weight[level]) + embed_bias[level].astype(f32)
            )
        tokens[pair] = jnp.concatenate(both, axis=0).astype(bf16)
        return 0

    lax.fori_loop(0, SLOTS // 2, embed, 0, unroll=2)

    def project(four, _):
        block = jnp.concatenate([tokens[four * 2], tokens[four * 2 + 1]], axis=0)
        projected = dot(block, value_weight[...])
        scored = dot(block, keys, ((1,), (1,)))
        scored = scored[:, :128] + scored[:, 128:]
        for i in range(4):
            values[four * 4 + i] = projected[i * SPOTS : (i + 1) * SPOTS]
            scores[four * 4 + i] = scored[i * SPOTS : (i + 1) * SPOTS]
        return 0

    lax.fori_loop(0, SLOTS // 4, project, 0)

    peak = scores[0]
    for s in range(1, SLOTS):
        peak = jnp.maximum(peak, scores[s])
    total = jnp.zeros_like(peak)
    for s in range(SLOTS):
        exponent = jnp.exp(scores[s] - peak)
        scores[s] = exponent
        total = total + exponent
    inverse = 1.0 / total
    first = lax.broadcasted_iota(jnp.int32, (4 * SPOTS, 128), 1) < 64
    sums[...] = jnp.zeros_like(sums)

    def mix(four, _):
        probs = jnp.concatenate([scores[four * 4 + i] * inverse for i in range(4)], axis=0)
        high = probs.astype(bf16).astype(f32)
        split = jnp.where(first, high, probs - high).astype(bf16)
        for l in range(LEVELS):
            wide = dot(split, spread[:, l * WIDTH : (l + 1) * WIDTH])
            part = sums[l]
            for i in range(4):
                part = part + wide[i * SPOTS : (i + 1) * SPOTS] * values[four * 4 + i]
            sums[l] = part
        return 0

    lax.fori_loop(0, SLOTS // 4, mix, 0)

    pooled = jnp.concatenate([sums[l] for l in range(LEVELS)], axis=0).astype(bf16)
    projected = dot(pooled, pool_weight[...])
    stream = jnp.concatenate(
        [
            projected[l * SPOTS : (l + 1) * SPOTS] + latents[l : l + 1].astype(f32)
            for l in range(LEVELS)
        ],
        axis=0,
    ).astype(bf16)
    ordered = dot(order[...], stream).astype(bf16)
    left[...] = ordered[:HALF]
    right[...] = ordered[HALF:]


def pool(pixels, ids, embed_weight, embed_bias, latents, wq, wk, wv, wp, pool_temp):
    temp = jnp.tile(pool_temp / math.sqrt(HEAD_WIDTH), LEVELS)[:, None]
    vmem = pl.BlockSpec(memory_space=pltpu.VMEM)
    half = jax.ShapeDtypeStruct((HALF, WIDTH), bf16)
    return pl.pallas_call(
        pool_kernel,
        out_shape=(half, half),
        in_specs=[pl.BlockSpec(memory_space=pltpu.SMEM)] + [vmem] * 12,
        out_specs=(vmem, vmem),
        scratch_shapes=[
            pltpu.VMEM((SLOTS // 2, 2 * SPOTS, WIDTH), bf16),
            pltpu.VMEM((SLOTS, SPOTS, 128), f32),
            pltpu.VMEM((SLOTS, SPOTS, WIDTH), f32),
            pltpu.VMEM((LEVELS, SPOTS, WIDTH), f32),
        ],
        compiler_params=pltpu.CompilerParams(vmem_limit_bytes=56 * 1024 * 1024),
        cost_estimate=pl.CostEstimate(
            flops=20_000_000_000, bytes_accessed=12_000_000, transcendentals=500_000
        ),
        name="pool",
    )(
        ids,
        pixels,
        embed_weight,
        embed_bias[:, None, :],
        latents,
        wq,
        wk,
        wv,
        wp,
        temp,
        jnp.asarray(head_rows(), f32),
        jnp.asarray(spread_matrix(), bf16),
        jnp.asarray(order_matrix(), bf16),
    )


def layer_kernel(
    place,
    factor,
    own,
    above,
    below,
    cotangent,
    first_gain,
    qkv_weight,
    proj_weight,
    second_gain,
    up_weight,
    down_weight,
    output,
    grads,
    qs,
    ks,
    vs,
    attended,
    normed2,
    normed2_t,
    total,
):
    stream = own[...]
    wide = jnp.concatenate([above[...], stream, below[...]], axis=0).astype(f32)
    norm = normed(wide, first_gain[...])
    queries = dot(norm[HALF : HALF + TOKENS], qkv_weight[:, :WIDTH]).astype(bf16)
    keys = dot(norm, qkv_weight[:, WIDTH : 2 * WIDTH]).astype(bf16)
    values = dot(norm, qkv_weight[:, 2 * WIDTH :]).astype(bf16)
    for win in range(2):
        for g in range(4):
            lanes = slice(g * 128, (g + 1) * 128)
            qs[win * 4 + g] = queries[win * HALF : (win + 1) * HALF, lanes]
            ks[win * 4 + g] = keys[win * TOKENS : (win + 1) * TOKENS, lanes]
            vs[win * 4 + g] = values[win * TOKENS : (win + 1) * TOKENS, lanes]

    row = lax.broadcasted_iota(jnp.int32, (HALF, TOKENS), 0)
    col = lax.broadcasted_iota(jnp.int32, (HALF, TOKENS), 1)
    same = (((row & 3) + 1) >> 1) == (((col & 3) + 1) >> 1)
    lane = lax.broadcasted_iota(jnp.int32, (HALF, 128), 1) // HEAD_WIDTH
    enc = place[0]

    def attend(index, _):
        win = index // 4
        group = lax.rem(index, 4)
        first_key = jnp.where((win == 0) & (enc == 0), HALF, 0)
        last_key = jnp.where((win == 1) & (enc == 3), HALF, TOKENS)
        valid = same & (col >= first_key) & (col < last_key)
        query = qs[index]
        key = ks[index]
        value = vs[index]
        result = jnp.zeros((HALF, 128), f32)
        for h in range(4):
            mine = lane == h
            part = jnp.where(mine, query, jnp.zeros_like(query))
            scores = dot(part, key, ((1,), (1,))) * factor[group * 4 + h]
            scores = jnp.where(valid, scores, -1e30)
            exponent = jnp.exp(scores - jnp.max(scores, axis=-1, keepdims=True))
            weights = exponent / jnp.sum(exponent, axis=-1, keepdims=True)
            result = jnp.where(mine, dot(weights.astype(bf16), value), result)
        attended[index] = result.astype(bf16)
        return 0

    lax.fori_loop(0, 8, attend, 0)

    rows = [
        jnp.concatenate([attended[win * 4 + g] for g in range(4)], axis=1) for win in range(2)
    ]
    middle = stream.astype(f32) + dot(jnp.concatenate(rows, axis=0), proj_weight[...])
    middle = middle.astype(bf16).astype(f32)
    norm = normed(middle, second_gain[...])
    normed2[...] = norm
    normed2_t[...] = norm.T
    total[...] = middle

    def mlp(j, _):
        at = pl.ds(pl.multiple_of(j * 512, 512), 512)
        x = dot(normed2[...], up_weight[:, at])
        cubic = 0.044715 * (x * x)
        scale = math.sqrt(2.0 / math.pi)
        bend = jnp.tanh(scale * (x * (1.0 + cubic)))
        hidden = (0.5 * x * (1.0 + bend)).astype(bf16)
        slope = 0.5 * (1.0 + bend) + 0.5 * x * (1.0 - bend * bend) * (
            scale * (1.0 + 3.0 * cubic)
        )
        down = down_weight[at, :]
        total[...] += dot(hidden, down)
        down_grad = dot(hidden, cotangent[...], ((0,), (0,))).astype(bf16)
        back = dot(cotangent[...], down, ((1,), (1,)))
        slope = (slope * back).astype(bf16)
        up_grad = dot(normed2_t[...], slope).astype(bf16)
        for i in range(2):
            lanes = slice(i * PART_COLS, (i + 1) * PART_COLS)
            grads[0, j, i * 512 : (i + 1) * 512] = up_grad[:, lanes]
            grads[1, j, i * 512 : (i + 1) * 512] = down_grad[:, lanes]
        return 0

    lax.fori_loop(0, FF // 512, mlp, 0)
    output[...] = total[...].astype(bf16)


def layer(place, own, above, below, cot, g1, wqkv, window_temp, wproj, g2, wup, wdown):
    vmem = pl.BlockSpec(memory_space=pltpu.VMEM)
    smem = pl.BlockSpec(memory_space=pltpu.SMEM)
    return pl.pallas_call(
        layer_kernel,
        out_shape=(
            jax.ShapeDtypeStruct((TOKENS, WIDTH), bf16),
            jax.ShapeDtypeStruct((2, PARTS, PART_ROWS, PART_COLS), bf16),
        ),
        in_specs=[smem, smem] + [vmem] * 10,
        out_specs=(vmem, vmem),
        scratch_shapes=[
            pltpu.VMEM((8, HALF, 128), bf16),
            pltpu.VMEM((8, TOKENS, 128), bf16),
            pltpu.VMEM((8, TOKENS, 128), bf16),
            pltpu.VMEM((8, HALF, 128), bf16),
            pltpu.VMEM((TOKENS, WIDTH), bf16),
            pltpu.VMEM((WIDTH, TOKENS), bf16),
            pltpu.VMEM((TOKENS, WIDTH), f32),
        ],
        compiler_params=pltpu.CompilerParams(vmem_limit_bytes=56 * 1024 * 1024),
        cost_estimate=pl.CostEstimate(
            flops=10_000_000_000, bytes_accessed=12_000_000, transcendentals=2_000_000
        ),
        name="layer",
    )(
        place,
        window_temp / math.sqrt(HEAD_WIDTH),
        own,
        above,
        below,
        cot,
        g1[None, :],
        wqkv,
        wproj,
        g2[None, :],
        wup,
        wdown,
    )


def mesh_id(x, y, z, core):
    return (lax.rem(y, 2) * 2 + core, x * 8 + z * 2 + y // 2)


def sum_kernel(
    grads, result, pair, work, got1, got2, got3, send, recv, send_pair, recv_pair
):
    enc = lax.axis_index("enc")
    lon = lax.axis_index("lon")
    core = lax.rem(enc, 2)
    x = lon // 8
    y = lax.rem(lon, 2) * 2 + enc // 2
    z = lax.rem(lon // 2, 4)
    partner = mesh_id(x, y, z, 1 - core)

    def along(dim, by):
        is_x = (2 - dim) * (1 - dim) // 2
        is_y = dim * (2 - dim)
        is_z = dim * (dim - 1) // 2
        return mesh_id(
            lax.rem(x + by * is_x, 4),
            lax.rem(y + by * is_y, 4),
            lax.rem(z + by * is_z, 4),
            core,
        )

    def where_along(dim):
        is_x = (2 - dim) * (1 - dim) // 2
        is_y = dim * (2 - dim)
        is_z = dim * (dim - 1) // 2
        return x * is_x + y * is_y + z * is_z

    barrier = pltpu.get_barrier_semaphore()
    pl.semaphore_signal(barrier, inc=1, device_id=partner, device_id_type=MESH)
    for dim in range(3):
        for by in range(1, 4):
            pl.semaphore_signal(barrier, inc=1, device_id=along(dim, by), device_id_type=MESH)
    pl.semaphore_wait(barrier, 10)

    pair_copies = []
    for p in range(PARTS):
        copy = pltpu.make_async_remote_copy(
            src_ref=grads.at[1 - core, p],
            dst_ref=pair.at[p],
            send_sem=send_pair.at[p],
            recv_sem=recv_pair.at[p],
            device_id=partner,
            device_id_type=MESH,
        )
        copy.start()
        pair_copies.append(copy)

    sizes = (PART_ROWS // 4, PART_ROWS // 16, PART_ROWS // 64)
    slots = (got1, got2, got3)
    dims = [[lax.rem(p + core + phase, 3) for phase in range(3)] for p in range(PARTS)]
    mine = [[where_along(dims[p][phase]) for phase in range(3)] for p in range(PARTS)]
    starts = []
    for p in range(PARTS):
        at = [0]
        for phase in range(3):
            at.append(at[-1] + mine[p][phase] * sizes[phase])
        starts.append(at)

    copies = {}

    def scatter(p, phase):
        size = sizes[phase]
        for by in range(1, 4):
            target = lax.rem(mine[p][phase] + by, 4)
            first = pl.multiple_of(starts[p][phase] + target * size, 16)
            copy = pltpu.make_async_remote_copy(
                src_ref=work.at[p, pl.ds(first, size)],
                dst_ref=slots[phase].at[p, by - 1],
                send_sem=send.at[0, p, phase, by - 1],
                recv_sem=recv.at[0, p, phase, by - 1],
                device_id=along(dims[p][phase], by),
                device_id_type=MESH,
            )
            copy.start()
            copies[0, p, phase, by] = copy

    def add_up(p, phase):
        for by in range(1, 4):
            copies[0, p, phase, by].wait_recv()
        size = sizes[phase]
        first = pl.multiple_of(starts[p][phase + 1], 16)
        held = work[p, pl.ds(first, size), :].astype(f32)
        for k in range(3):
            held = held + slots[phase][p, k].astype(f32)
        if phase < 2:
            work[p, pl.ds(first, size), :] = held.astype(bf16)
        else:
            result[core, p, pl.ds(first, size), :] = held.astype(bf16)

    def gather(p, phase):
        size = sizes[phase]
        first = pl.multiple_of(starts[p][phase + 1], 16)
        piece = result.at[core, p, pl.ds(first, size)]
        for by in range(1, 4):
            copy = pltpu.make_async_remote_copy(
                src_ref=piece,
                dst_ref=piece,
                send_sem=send.at[1, p, phase, by - 1],
                recv_sem=recv.at[1, p, phase, by - 1],
                device_id=along(dims[p][phase], by),
                device_id_type=MESH,
            )
            copy.start()
            copies[1, p, phase, by] = copy

    def gathered(p, phase):
        size = sizes[phase]
        for by in range(1, 4):
            source = lax.rem(mine[p][phase] + 4 - by, 4)
            first = pl.multiple_of(starts[p][phase] + source * size, 16)
            piece = result.at[core, p, pl.ds(first, size)]
            pltpu.make_async_remote_copy(
                src_ref=piece,
                dst_ref=piece,
                send_sem=send.at[1, p, phase, by - 1],
                recv_sem=recv.at[1, p, phase, by - 1],
                device_id=along(dims[p][phase], by),
                device_id_type=MESH,
            ).wait_recv()

    for p in range(PARTS):
        pair_copies[p].wait_recv()
        work[p] = (grads[core, p].astype(f32) + pair[p].astype(f32)).astype(bf16)
        scatter(p, 0)
    for phase in range(3):
        for p in range(PARTS):
            add_up(p, phase)
            if phase < 2:
                scatter(p, phase + 1)
            else:
                gather(p, 2)
    for phase in (2, 1, 0):
        for p in range(PARTS):
            gathered(p, phase)
            if phase > 0:
                gather(p, phase - 1)
            else:
                copy = pltpu.make_async_remote_copy(
                    src_ref=result.at[core, p],
                    dst_ref=result.at[core, p],
                    send_sem=send_pair.at[PARTS + p],
                    recv_sem=recv_pair.at[PARTS + p],
                    device_id=partner,
                    device_id_type=MESH,
                )
                copy.start()
                pair_copies.append(copy)
    for p in range(PARTS):
        pltpu.make_async_remote_copy(
            src_ref=result.at[1 - core, p],
            dst_ref=result.at[1 - core, p],
            send_sem=send_pair.at[PARTS + p],
            recv_sem=recv_pair.at[PARTS + p],
            device_id=partner,
            device_id_type=MESH,
        ).wait_recv()
    for copy in pair_copies:
        copy.wait_send()
    for copy in copies.values():
        copy.wait_send()


def sum_grads(grads):
    vmem = pl.BlockSpec(memory_space=pltpu.VMEM)
    return pl.pallas_call(
        sum_kernel,
        out_shape=jax.ShapeDtypeStruct(grads.shape, bf16),
        in_specs=[vmem],
        out_specs=vmem,
        scratch_shapes=[
            pltpu.VMEM((PARTS, PART_ROWS, PART_COLS), bf16),
            pltpu.VMEM((PARTS, PART_ROWS, PART_COLS), bf16),
            pltpu.VMEM((PARTS, 3, PART_ROWS // 4, PART_COLS), bf16),
            pltpu.VMEM((PARTS, 3, PART_ROWS // 16, PART_COLS), bf16),
            pltpu.VMEM((PARTS, 3, PART_ROWS // 64, PART_COLS), bf16),
            pltpu.SemaphoreType.DMA((2, PARTS, 3, 3)),
            pltpu.SemaphoreType.DMA((2, PARTS, 3, 3)),
            pltpu.SemaphoreType.DMA((2 * PARTS,)),
            pltpu.SemaphoreType.DMA((2 * PARTS,)),
        ],
        compiler_params=pltpu.CompilerParams(
            collective_id=1, has_side_effects=True, vmem_limit_bytes=48 * 1024 * 1024
        ),
        name="sum_grads",
    )(grads)


def shifted(value, axis, by):
    count = lax.axis_size(axis)
    return lax.ppermute(value, axis, [(i, (i + by) % count) for i in range(count)])


def per_device(
    pixel_field,
    level_ids,
    embed_weight,
    embed_bias,
    latents,
    query_weight,
    key_weight,
    value_weight,
    pool_weight,
    pool_temp,
    first_gain,
    qkv_weight,
    window_temp,
    proj_weight,
    second_gain,
    up_weight,
    down_weight,
    cotangent,
):
    groups = 4
    half_cols = COLS // 2
    cot = jnp.transpose(cotangent, (1, 2, 0, 3))
    cot = jnp.concatenate([cot[:, half_cols:], shifted(cot[:, :half_cols], "lon", -1)], axis=1)
    cot = cot.reshape(TOKENS, WIDTH)

    mine = SLOTS // groups
    pixels = jnp.transpose(pixel_field, (0, 3, 1, 2)).reshape(mine, COLS, groups, ROWS, PIXELS)
    pixels = jnp.transpose(pixels, (2, 0, 1, 3, 4)).reshape(SLOTS, SPOTS, PIXELS)
    pixels = lax.all_to_all(pixels, "enc", split_axis=0, concat_axis=0, tiled=True)
    left, right = pool(
        pixels,
        level_ids,
        embed_weight,
        embed_bias,
        latents,
        query_weight,
        key_weight,
        value_weight,
        pool_weight,
        pool_temp,
    )
    east = shifted(left, "lon", -1)
    own = jnp.concatenate(
        [v.reshape(ROWS, half_cols * LEVELS, WIDTH) for v in (right, east)], axis=1
    ).reshape(TOKENS, WIDTH)
    forward = [(i, i + 1) for i in range(groups - 1)]
    backward = [(i + 1, i) for i in range(groups - 1)]
    above = lax.ppermute(own[HALF:], "enc", forward)
    below = lax.ppermute(own[:HALF], "enc", backward)
    place = lax.axis_index("enc").astype(jnp.int32)[None]
    output, grads = layer(
        place,
        own,
        above,
        below,
        cot,
        first_gain,
        qkv_weight,
        window_temp,
        proj_weight,
        second_gain,
        up_weight,
        down_weight,
    )
    output = output.reshape(ROWS, COLS, LEVELS, WIDTH)
    back = shifted(output[:, half_cols:], "lon", 1)
    output = jnp.concatenate([back, output[:, :half_cols]], axis=1)
    output = jnp.transpose(output, (2, 0, 1, 3))

    sums = sum_grads(grads)
    scaling = 1.0 / math.sqrt(NTOK)
    up_grad = sums[0].reshape(PARTS, 2, WIDTH, PART_COLS)
    up_grad = jnp.transpose(up_grad, (2, 0, 1, 3)).reshape(WIDTH, FF)
    down_grad = sums[1].reshape(PARTS, 2, 512, PART_COLS)
    down_grad = jnp.transpose(down_grad, (0, 2, 1, 3)).reshape(FF, WIDTH)
    return (output, up_grad.astype(f32) * scaling, down_grad.astype(f32) * scaling)


def solution(mesh):
    placed = (P("enc", None, None, "lon"),) + (P(),) * 16 + (P(None, "enc", "lon", None),)
    return jax.shard_map(
        per_device,
        mesh=mesh,
        in_specs=placed,
        out_specs=(P(None, "enc", "lon", None), P(), P()),
        check_vma=False,
    )
```

```python
import functools
import math

import jax
import jax.numpy as jnp
import numpy as np
from jax import lax
from jax.experimental import pallas as pl
from jax.experimental.pallas import tpu as pltpu
from jax.sharding import PartitionSpec as P

SLOTS = 52
HEADS = 16
HEAD_WIDTH = 32
WIDTH = 512
FF = 2048
LEVELS = 4
ROWS = 6
COLS = 12
SPOTS = ROWS * COLS
TOKENS = LEVELS * SPOTS
HALF = TOKENS // 2
PIXELS = 100
PER = SLOTS // 4
EPSILON = 1e-05
NTOK = 36864
PARTS = 4
PART_ROWS = 1024
PART_COLS = 256
MESH = pl.DeviceIdType.MESH

f32 = jnp.float32
bf16 = jnp.bfloat16


def dot(a, b, contract=((1,), (0,))):
    return lax.dot_general(a, b, (contract, ((), ())), preferred_element_type=f32)


def normed(values, gain):
    mean = jnp.mean(values, axis=-1, keepdims=True)
    centred = values - mean
    variance = jnp.mean(centred * centred, axis=-1, keepdims=True)
    return (centred * lax.rsqrt(variance + EPSILON) * gain).astype(bf16)


def head_rows():
    mask = np.zeros((HEADS, WIDTH), np.float32)
    for h in range(HEADS):
        mask[h, h * HEAD_WIDTH : (h + 1) * HEAD_WIDTH] = 1.0
    return mask


def spread_matrix():
    one = np.zeros((LEVELS * HEADS, LEVELS * WIDTH), np.float32)
    for l in range(LEVELS):
        for h in range(HEADS):
            at = l * WIDTH + h * HEAD_WIDTH
            one[l * HEADS + h, at : at + HEAD_WIDTH] = 1.0
    return np.concatenate([one, one], axis=0)


def shift_matrices():
    half = COLS // 2
    left_of_stream = np.zeros((HALF, TOKENS), np.float32)
    right_of_stream = np.zeros((TOKENS, TOKENS), np.float32)
    left_of_natural = np.zeros((HALF, TOKENS), np.float32)
    right_of_natural = np.zeros((TOKENS, TOKENS), np.float32)
    east_part = np.zeros((TOKENS, HALF), np.float32)
    for r in range(ROWS):
        for c in range(half):
            for l in range(LEVELS):
                piece = (r * half + c) * LEVELS + l
                low = (r * COLS + c) * LEVELS + l
                high = (r * COLS + half + c) * LEVELS + l
                left_of_stream[piece, l * SPOTS + c * ROWS + r] = 1.0
                right_of_stream[low, l * SPOTS + (half + c) * ROWS + r] = 1.0
                left_of_natural[piece, low] = 1.0
                right_of_natural[low, high] = 1.0
                east_part[high, piece] = 1.0
    return left_of_stream, right_of_stream, left_of_natural, right_of_natural, east_part


def pool_kernel(
    ids,
    pixels,
    embed_weight,
    embed_bias,
    latents,
    query_weight,
    key_weight,
    value_weight,
    pool_weight,
    temp,
    heads,
    spread,
    left_of_stream,
    right_of_stream,
    left_of_natural,
    right_of_natural,
    east_part,
    cotangent,
    wide,
    cot_shifted,
    tokens,
    scores,
    values,
    sums,
    arrived,
    cot_left,
    cot_east,
    left,
    east,
    send,
    recv,
):
    enc = lax.axis_index("enc")
    lon = lax.axis_index("lon")
    mate = enc + 1 - 2 * lax.rem(enc, 2)
    peers = (mate, lax.rem(enc + 2, 4), lax.rem(mate + 2, 4))
    west_id = (enc, lax.rem(lon + 31, 32))
    east_id = (enc, lax.rem(lon + 1, 32))
    barrier = pltpu.get_barrier_semaphore()
    for peer in peers:
        pl.semaphore_signal(barrier, inc=1, device_id=(peer, lon), device_id_type=MESH)
    for other in (west_id, east_id):
        pl.semaphore_signal(barrier, inc=1, device_id=other, device_id_type=MESH)
    pl.semaphore_wait(barrier, 5)

    def remote(source, target, index, device):
        copy = pltpu.make_async_remote_copy(
            src_ref=source,
            dst_ref=target,
            send_sem=send.at[index],
            recv_sem=recv.at[index],
            device_id=device,
            device_id_type=MESH,
        )
        copy.start()
        return copy

    copies = []
    for k in (1, 2, 0):
        copies.append(remote(pixels.at[peers[k]], arrived.at[k], k, (peers[k], lon)))
    copy_far, copy_other, copy_mate = copies
    cot_left[...] = dot(left_of_natural[...], cotangent[...]).astype(bf16)
    copy_cot = remote(cot_left, cot_east, 3, west_id)

    queries = dot(latents[...], query_weight[...]).astype(bf16).astype(f32)
    blocks = [queries[l : l + 1] * heads[...] for l in range(LEVELS)]
    blocks = jnp.concatenate(blocks, axis=0).astype(bf16)
    folded = dot(blocks, key_weight[...], ((1,), (1,))) * temp[...]
    high = folded.astype(bf16)
    low = (folded - high.astype(f32)).astype(bf16)
    keys = jnp.concatenate([high, high, low, low], axis=0)

    def token_of(block, slot):
        level = ids[slot]
        return dot(block, embed_weight[level]) + embed_bias[level].astype(f32)

    def project(stage):
        def one(four, _):
            block = jnp.concatenate([tokens[four * 2], tokens[four * 2 + 1]], axis=0)
            projected = dot(block, value_weight[...])
            scored = dot(block, keys, ((1,), (1,)))
            scored = scored[:, :128] + scored[:, 128:]
            for i in range(4):
                values[four * 4 + i] = projected[i * SPOTS : (i + 1) * SPOTS]
                scores[four * 4 + i] = scored[i * SPOTS : (i + 1) * SPOTS]
            return 0

        lax.fori_loop(6 * stage, 6 + 7 * stage, one, 0)

    def embed_near(i, _):
        near = token_of(pixels[enc, i], enc * PER + i)
        far = token_of(arrived[0, i], mate * PER + i)
        tokens[i] = jnp.concatenate([near, far], axis=0).astype(bf16)
        return 0

    def embed_far(i, _):
        near = token_of(arrived[1, i], peers[1] * PER + i)
        far = token_of(arrived[2, i], peers[2] * PER + i)
        tokens[PER + i] = jnp.concatenate([near, far], axis=0).astype(bf16)
        return 0

    copy_mate.wait_recv()
    lax.fori_loop(0, PER, embed_near, 0)
    project(0)
    copy_far.wait_recv()
    copy_other.wait_recv()
    lax.fori_loop(0, PER, embed_far, 0)
    project(1)

    peak = scores[0]
    for s in range(1, SLOTS):
        peak = jnp.maximum(peak, scores[s])
    total = jnp.zeros_like(peak)
    for s in range(SLOTS):
        exponent = jnp.exp(scores[s] - peak)
        scores[s] = exponent
        total = total + exponent
    inverse = 1.0 / total
    first = lax.broadcasted_iota(jnp.int32, (4 * SPOTS, 128), 1) < 64
    sums[...] = jnp.zeros_like(sums)

    def mix(four, _):
        probs = jnp.concatenate([scores[four * 4 + i] * inverse for i in range(4)], axis=0)
        high = probs.astype(bf16).astype(f32)
        split = jnp.where(first, high, probs - high).astype(bf16)
        for l in range(LEVELS):
            spread_out = dot(split, spread[:, l * WIDTH : (l + 1) * WIDTH])
            part = sums[l]
            for i in range(4):
                part = part + spread_out[i * SPOTS : (i + 1) * SPOTS] * values[four * 4 + i]
            sums[l] = part
        return 0

    lax.fori_loop(0, SLOTS // 4, mix, 0)

    pooled = jnp.concatenate([sums[l] for l in range(LEVELS)], axis=0).astype(bf16)
    projected = dot(pooled, pool_weight[...])
    stream = jnp.concatenate(
        [
            projected[l * SPOTS : (l + 1) * SPOTS] + latents[l : l + 1].astype(f32)
            for l in range(LEVELS)
        ],
        axis=0,
    ).astype(bf16)
    left[...] = dot(left_of_stream[...], stream).astype(bf16)
    copy_left = remote(left, east, 4, west_id)
    kept = dot(right_of_stream[...], stream)
    copy_cot.wait_recv()
    cot_shifted[...] = (
        dot(right_of_natural[...], cotangent[...]) + dot(east_part[...], cot_east[...])
    ).astype(bf16)
    copy_left.wait_recv()
    wide[HALF : HALF + TOKENS] = (kept + dot(east_part[...], east[...])).astype(bf16)
    copy_up = remote(
        wide.at[pl.ds(HALF, HALF)],
        wide.at[pl.ds(HALF + TOKENS, HALF)],
        5,
        (lax.rem(enc + 3, 4), lon),
    )
    copy_down = remote(
        wide.at[pl.ds(TOKENS, HALF)], wide.at[pl.ds(0, HALF)], 6, (lax.rem(enc + 1, 4), lon)
    )
    copy_up.wait_recv()
    copy_down.wait_recv()
    for copy in (copy_far, copy_other, copy_mate, copy_cot, copy_left, copy_up, copy_down):
        copy.wait_send()


def pool(pixels, cot, ids, embed_weight, embed_bias, latents, wq, wk, wv, wp, pool_temp):
    temp = jnp.tile(pool_temp / math.sqrt(HEAD_WIDTH), LEVELS)[:, None]
    vmem = pl.BlockSpec(memory_space=pltpu.VMEM)
    return pl.pallas_call(
        pool_kernel,
        out_shape=(
            jax.ShapeDtypeStruct((2 * TOKENS, WIDTH), bf16),
            jax.ShapeDtypeStruct((TOKENS, WIDTH), bf16),
        ),
        in_specs=[pl.BlockSpec(memory_space=pltpu.SMEM)] + [vmem] * 17,
        out_specs=(vmem, vmem),
        scratch_shapes=[
            pltpu.VMEM((SLOTS // 2, 2 * SPOTS, WIDTH), bf16),
            pltpu.VMEM((SLOTS, SPOTS, 128), f32),
            pltpu.VMEM((SLOTS, SPOTS, WIDTH), f32),
            pltpu.VMEM((LEVELS, SPOTS, WIDTH), f32),
            pltpu.VMEM((3, PER, SPOTS, PIXELS), bf16),
            pltpu.VMEM((HALF, WIDTH), bf16),
            pltpu.VMEM((HALF, WIDTH), bf16),
            pltpu.VMEM((HALF, WIDTH), bf16),
            pltpu.VMEM((HALF, WIDTH), bf16),
            pltpu.SemaphoreType.DMA((7,)),
            pltpu.SemaphoreType.DMA((7,)),
        ],
        compiler_params=pltpu.CompilerParams(
            collective_id=2, has_side_effects=True, vmem_limit_bytes=56 * 1024 * 1024
        ),
        cost_estimate=pl.CostEstimate(
            flops=20_000_000_000, bytes_accessed=12_000_000, transcendentals=500_000
        ),
        name="pool",
    )(
        ids,
        pixels,
        embed_weight,
        embed_bias[:, None, :],
        latents,
        wq,
        wk,
        wv,
        wp,
        temp,
        jnp.asarray(head_rows(), f32),
        jnp.asarray(spread_matrix(), bf16),
        *[jnp.asarray(matrix, bf16) for matrix in shift_matrices()],
        cot,
    )


def layer_kernel(
    place,
    factor,
    wide,
    cotangent,
    first_gain,
    qkv_weight,
    proj_weight,
    second_gain,
    up_weight,
    down_weight,
    back_part,
    left_part,
    stay,
    leave,
    grads,
    qs,
    ks,
    vs,
    attended,
    normed2,
    normed2_t,
    total,
):
    stream = wide[HALF : HALF + TOKENS]
    norm = normed(wide[...].astype(f32), first_gain[...])
    queries = dot(norm[HALF : HALF + TOKENS], qkv_weight[:, :WIDTH]).astype(bf16)
    keys = dot(norm, qkv_weight[:, WIDTH : 2 * WIDTH]).astype(bf16)
    values = dot(norm, qkv_weight[:, 2 * WIDTH :]).astype(bf16)
    for win in range(2):
        for g in range(4):
            lanes = slice(g * 128, (g + 1) * 128)
            qs[win * 4 + g] = queries[win * HALF : (win + 1) * HALF, lanes]
            ks[win * 4 + g] = keys[win * TOKENS : (win + 1) * TOKENS, lanes]
            vs[win * 4 + g] = values[win * TOKENS : (win + 1) * TOKENS, lanes]

    row = lax.broadcasted_iota(jnp.int32, (HALF, TOKENS), 0)
    col = lax.broadcasted_iota(jnp.int32, (HALF, TOKENS), 1)
    same = (((row & 3) + 1) >> 1) == (((col & 3) + 1) >> 1)
    lane = lax.broadcasted_iota(jnp.int32, (HALF, 128), 1) // HEAD_WIDTH
    enc = place[0]

    def attend(index, _):
        win = index // 4
        group = lax.rem(index, 4)
        first_key = jnp.where((win == 0) & (enc == 0), HALF, 0)
        last_key = jnp.where((win == 1) & (enc == 3), HALF, TOKENS)
        valid = same & (col >= first_key) & (col < last_key)
        query = qs[index]
        key = ks[index]
        value = vs[index]
        result = jnp.zeros((HALF, 128), f32)
        for h in range(4):
            mine = lane == h
            part = jnp.where(mine, query, jnp.zeros_like(query))
            scores = dot(part, key, ((1,), (1,))) * factor[group * 4 + h]
            scores = jnp.where(valid, scores, -1e30)
            exponent = jnp.exp(scores - jnp.max(scores, axis=-1, keepdims=True))
            weights = exponent / jnp.sum(exponent, axis=-1, keepdims=True)
            result = jnp.where(mine, dot(weights.astype(bf16), value), result)
        attended[index] = result.astype(bf16)
        return 0

    lax.fori_loop(0, 8, attend, 0)

    rows = [
        jnp.concatenate([attended[win * 4 + g] for g in range(4)], axis=1) for win in range(2)
    ]
    middle = stream.astype(f32) + dot(jnp.concatenate(rows, axis=0), proj_weight[...])
    middle = middle.astype(bf16).astype(f32)
    norm = normed(middle, second_gain[...])
    normed2[...] = norm
    normed2_t[...] = norm.T
    total[...] = middle

    def mlp(j, _):
        at = pl.ds(pl.multiple_of(j * 512, 512), 512)
        x = dot(normed2[...], up_weight[:, at])
        cubic = 0.044715 * (x * x)
        scale = math.sqrt(2.0 / math.pi)
        bend = jnp.tanh(scale * (x * (1.0 + cubic)))
        hidden = (0.5 * x * (1.0 + bend)).astype(bf16)
        slope = 0.5 * (1.0 + bend) + 0.5 * x * (1.0 - bend * bend) * (
            scale * (1.0 + 3.0 * cubic)
        )
        down = down_weight[at, :]
        total[...] += dot(hidden, down)
        down_grad = dot(hidden, cotangent[...], ((0,), (0,))).astype(bf16)
        back = dot(cotangent[...], down, ((1,), (1,)))
        slope = (slope * back).astype(bf16)
        up_grad = dot(normed2_t[...], slope).astype(bf16)
        for i in range(2):
            lanes = slice(i * PART_COLS, (i + 1) * PART_COLS)
            grads[0, j, i * 512 : (i + 1) * 512] = up_grad[:, lanes]
            grads[1, j, i * 512 : (i + 1) * 512] = down_grad[:, lanes]
        return 0

    lax.fori_loop(0, FF // 512, mlp, 0)
    output = total[...].astype(bf16)
    stay[...] = dot(left_part[...], output).astype(bf16)
    leave[...] = dot(back_part[...], output).astype(bf16)


def layer(place, wide, cot, g1, wqkv, window_temp, wproj, g2, wup, wdown):
    vmem = pl.BlockSpec(memory_space=pltpu.VMEM)
    smem = pl.BlockSpec(memory_space=pltpu.SMEM)
    return pl.pallas_call(
        layer_kernel,
        out_shape=(
            jax.ShapeDtypeStruct((HALF, WIDTH), bf16),
            jax.ShapeDtypeStruct((HALF, WIDTH), bf16),
            jax.ShapeDtypeStruct((2, PARTS, PART_ROWS, PART_COLS), bf16),
        ),
        in_specs=[smem, smem] + [vmem] * 10,
        out_specs=(vmem, vmem, vmem),
        scratch_shapes=[
            pltpu.VMEM((8, HALF, 128), bf16),
            pltpu.VMEM((8, TOKENS, 128), bf16),
            pltpu.VMEM((8, TOKENS, 128), bf16),
            pltpu.VMEM((8, HALF, 128), bf16),
            pltpu.VMEM((TOKENS, WIDTH), bf16),
            pltpu.VMEM((WIDTH, TOKENS), bf16),
            pltpu.VMEM((TOKENS, WIDTH), f32),
        ],
        compiler_params=pltpu.CompilerParams(vmem_limit_bytes=56 * 1024 * 1024),
        cost_estimate=pl.CostEstimate(
            flops=10_000_000_000, bytes_accessed=12_000_000, transcendentals=2_000_000
        ),
        name="layer",
    )(
        place,
        window_temp / math.sqrt(HEAD_WIDTH),
        wide,
        cot,
        g1[None, :],
        wqkv,
        wproj,
        g2[None, :],
        wup,
        wdown,
        jnp.asarray(shift_matrices()[4].T, bf16),
        jnp.asarray(shift_matrices()[2], bf16),
    )


def mesh_id(x, y, z, core):
    return (lax.rem(y, 2) * 2 + core, x * 8 + z * 2 + y // 2)


def sum_kernel(
    grads, leave, result, back, pair, work, got1, got2, got3, send, recv, send_pair, recv_pair
):
    enc = lax.axis_index("enc")
    lon = lax.axis_index("lon")
    core = lax.rem(enc, 2)
    x = lon // 8
    y = lax.rem(lon, 2) * 2 + enc // 2
    z = lax.rem(lon // 2, 4)
    partner = mesh_id(x, y, z, 1 - core)

    def along(dim, by):
        is_x = (2 - dim) * (1 - dim) // 2
        is_y = dim * (2 - dim)
        is_z = dim * (dim - 1) // 2
        return mesh_id(
            lax.rem(x + by * is_x, 4),
            lax.rem(y + by * is_y, 4),
            lax.rem(z + by * is_z, 4),
            core,
        )

    def where_along(dim):
        is_x = (2 - dim) * (1 - dim) // 2
        is_y = dim * (2 - dim)
        is_z = dim * (dim - 1) // 2
        return x * is_x + y * is_y + z * is_z

    west_id = (enc, lax.rem(lon + 31, 32))
    east_id = (enc, lax.rem(lon + 1, 32))
    barrier = pltpu.get_barrier_semaphore()
    for other in (partner, west_id, east_id):
        pl.semaphore_signal(barrier, inc=1, device_id=other, device_id_type=MESH)
    for dim in range(3):
        for by in range(1, 4):
            pl.semaphore_signal(barrier, inc=1, device_id=along(dim, by), device_id_type=MESH)
    pl.semaphore_wait(barrier, 12)

    pair_copies = []
    for p in range(PARTS):
        copy = pltpu.make_async_remote_copy(
            src_ref=grads.at[1 - core, p],
            dst_ref=pair.at[p],
            send_sem=send_pair.at[p],
            recv_sem=recv_pair.at[p],
            device_id=partner,
            device_id_type=MESH,
        )
        copy.start()
        pair_copies.append(copy)
    copy_back = pltpu.make_async_remote_copy(
        src_ref=leave,
        dst_ref=back,
        send_sem=send_pair.at[2 * PARTS],
        recv_sem=recv_pair.at[2 * PARTS],
        device_id=east_id,
        device_id_type=MESH,
    )
    copy_back.start()

    sizes = (PART_ROWS // 4, PART_ROWS // 16, PART_ROWS // 64)
    slots = (got1, got2, got3)
    dims = [[lax.rem(p + core + phase, 3) for phase in range(3)] for p in range(PARTS)]
    mine = [[where_along(dims[p][phase]) for phase in range(3)] for p in range(PARTS)]
    starts = []
    for p in range(PARTS):
        at = [0]
        for phase in range(3):
            at.append(at[-1] + mine[p][phase] * sizes[phase])
        starts.append(at)

    copies = {}

    def scatter(p, phase):
        size = sizes[phase]
        for by in range(1, 4):
            target = lax.rem(mine[p][phase] + by, 4)
            first = pl.multiple_of(starts[p][phase] + target * size, 16)
            copy = pltpu.make_async_remote_copy(
                src_ref=work.at[p, pl.ds(first, size)],
                dst_ref=slots[phase].at[p, by - 1],
                send_sem=send.at[0, p, phase, by - 1],
                recv_sem=recv.at[0, p, phase, by - 1],
                device_id=along(dims[p][phase], by),
                device_id_type=MESH,
            )
            copy.start()
            copies[0, p, phase, by] = copy

    def add_up(p, phase):
        for by in range(1, 4):
            copies[0, p, phase, by].wait_recv()
        size = sizes[phase]
        first = pl.multiple_of(starts[p][phase + 1], 16)
        held = work[p, pl.ds(first, size), :].astype(f32)
        for k in range(3):
            held = held + slots[phase][p, k].astype(f32)
        if phase < 2:
            work[p, pl.ds(first, size), :] = held.astype(bf16)
        else:
            result[core, p, pl.ds(first, size), :] = held.astype(bf16)

    def gather(p, phase):
        size = sizes[phase]
        first = pl.multiple_of(starts[p][phase + 1], 16)
        piece = result.at[core, p, pl.ds(first, size)]
        for by in range(1, 4):
            copy = pltpu.make_async_remote_copy(
                src_ref=piece,
                dst_ref=piece,
                send_sem=send.at[1, p, phase, by - 1],
                recv_sem=recv.at[1, p, phase, by - 1],
                device_id=along(dims[p][phase], by),
                device_id_type=MESH,
            )
            copy.start()
            copies[1, p, phase, by] = copy

    def gathered(p, phase):
        size = sizes[phase]
        for by in range(1, 4):
            source = lax.rem(mine[p][phase] + 4 - by, 4)
            first = pl.multiple_of(starts[p][phase] + source * size, 16)
            piece = result.at[core, p, pl.ds(first, size)]
            pltpu.make_async_remote_copy(
                src_ref=piece,
                dst_ref=piece,
                send_sem=send.at[1, p, phase, by - 1],
                recv_sem=recv.at[1, p, phase, by - 1],
                device_id=along(dims[p][phase], by),
                device_id_type=MESH,
            ).wait_recv()

    for p in range(PARTS):
        pair_copies[p].wait_recv()
        work[p] = (grads[core, p].astype(f32) + pair[p].astype(f32)).astype(bf16)
        scatter(p, 0)
    for phase in range(3):
        for p in range(PARTS):
            add_up(p, phase)
            if phase < 2:
                scatter(p, phase + 1)
            else:
                gather(p, 2)
    for phase in (2, 1, 0):
        for p in range(PARTS):
            gathered(p, phase)
            if phase > 0:
                gather(p, phase - 1)
            else:
                copy = pltpu.make_async_remote_copy(
                    src_ref=result.at[core, p],
                    dst_ref=result.at[core, p],
                    send_sem=send_pair.at[PARTS + p],
                    recv_sem=recv_pair.at[PARTS + p],
                    device_id=partner,
                    device_id_type=MESH,
                )
                copy.start()
                pair_copies.append(copy)
    for p in range(PARTS):
        pltpu.make_async_remote_copy(
            src_ref=result.at[1 - core, p],
            dst_ref=result.at[1 - core, p],
            send_sem=send_pair.at[PARTS + p],
            recv_sem=recv_pair.at[PARTS + p],
            device_id=partner,
            device_id_type=MESH,
        ).wait_recv()
    copy_back.wait_recv()
    copy_back.wait_send()
    for copy in pair_copies:
        copy.wait_send()
    for copy in copies.values():
        copy.wait_send()


def sum_grads(grads, leave):
    vmem = pl.BlockSpec(memory_space=pltpu.VMEM)
    return pl.pallas_call(
        sum_kernel,
        out_shape=(
            jax.ShapeDtypeStruct(grads.shape, bf16),
            jax.ShapeDtypeStruct(leave.shape, bf16),
        ),
        in_specs=[vmem, vmem],
        out_specs=(vmem, vmem),
        scratch_shapes=[
            pltpu.VMEM((PARTS, PART_ROWS, PART_COLS), bf16),
            pltpu.VMEM((PARTS, PART_ROWS, PART_COLS), bf16),
            pltpu.VMEM((PARTS, 3, PART_ROWS // 4, PART_COLS), bf16),
            pltpu.VMEM((PARTS, 3, PART_ROWS // 16, PART_COLS), bf16),
            pltpu.VMEM((PARTS, 3, PART_ROWS // 64, PART_COLS), bf16),
            pltpu.SemaphoreType.DMA((2, PARTS, 3, 3)),
            pltpu.SemaphoreType.DMA((2, PARTS, 3, 3)),
            pltpu.SemaphoreType.DMA((2 * PARTS + 1,)),
            pltpu.SemaphoreType.DMA((2 * PARTS + 1,)),
        ],
        compiler_params=pltpu.CompilerParams(
            collective_id=1, has_side_effects=True, vmem_limit_bytes=48 * 1024 * 1024
        ),
        name="sum_grads",
    )(grads, leave)


def finish_kernel(sums, stay, back, east_part, west_part, output, up_grad, down_grad):
    scaling = 1.0 / math.sqrt(NTOK)

    @pl.when(pl.program_id(0) == 0)
    def _():
        whole = dot(west_part[...], back[...]) + dot(east_part[...], stay[...])
        output[...] = whole.astype(bf16)

    for i in range(2):
        lanes = slice(i * PART_COLS, (i + 1) * PART_COLS)
        rows = slice(i * 512, (i + 1) * 512)
        up_grad[:, lanes] = sums[0, 0, rows].astype(f32) * scaling
        down_grad[:, lanes] = sums[1, 0, rows].astype(f32) * scaling


def finish(sums, stay, back):
    matrices = shift_matrices()
    fixed = lambda *shape: pl.BlockSpec(shape, lambda p: (0, 0))
    return pl.pallas_call(
        finish_kernel,
        grid=(PARTS,),
        out_shape=(
            jax.ShapeDtypeStruct((TOKENS, WIDTH), bf16),
            jax.ShapeDtypeStruct((WIDTH, FF), f32),
            jax.ShapeDtypeStruct((FF, WIDTH), f32),
        ),
        in_specs=[
            pl.BlockSpec((2, 1, PART_ROWS, PART_COLS), lambda p: (0, p, 0, 0)),
            fixed(HALF, WIDTH),
            fixed(HALF, WIDTH),
            fixed(TOKENS, HALF),
            fixed(TOKENS, HALF),
        ],
        out_specs=(
            fixed(TOKENS, WIDTH),
            pl.BlockSpec((WIDTH, 512), lambda p: (0, p)),
            pl.BlockSpec((512, WIDTH), lambda p: (p, 0)),
        ),
        compiler_params=pltpu.CompilerParams(vmem_limit_bytes=32 * 1024 * 1024),
        name="finish",
    )(
        sums,
        stay,
        back,
        jnp.asarray(matrices[4], bf16),
        jnp.asarray(matrices[2].T, bf16),
    )


def per_device(
    pixel_field,
    level_ids,
    embed_weight,
    embed_bias,
    latents,
    query_weight,
    key_weight,
    value_weight,
    pool_weight,
    pool_temp,
    first_gain,
    qkv_weight,
    window_temp,
    proj_weight,
    second_gain,
    up_weight,
    down_weight,
    cotangent,
):
    groups = 4
    cot = jnp.transpose(cotangent, (1, 2, 0, 3)).reshape(TOKENS, WIDTH)
    pixels = jnp.transpose(pixel_field, (0, 3, 1, 2)).reshape(PER, COLS, groups, ROWS, PIXELS)
    pixels = jnp.transpose(pixels, (2, 0, 1, 3, 4)).reshape(groups, PER, SPOTS, PIXELS)
    wide, cot = pool(
        pixels,
        cot,
        level_ids,
        embed_weight,
        embed_bias,
        latents,
        query_weight,
        key_weight,
        value_weight,
        pool_weight,
        pool_temp,
    )
    place = lax.axis_index("enc").astype(jnp.int32)[None]
    stay, leave, grads = layer(
        place,
        wide,
        cot,
        first_gain,
        qkv_weight,
        window_temp,
        proj_weight,
        second_gain,
        up_weight,
        down_weight,
    )
    sums, back = sum_grads(grads, leave)
    output, up_grad, down_grad = finish(sums, stay, back)
    output = output.reshape(ROWS, COLS, LEVELS, WIDTH)
    return (jnp.transpose(output, (2, 0, 1, 3)), up_grad, down_grad)


def solution(mesh):
    placed = (P("enc", None, None, "lon"),) + (P(),) * 16 + (P(None, "enc", "lon", None),)
    return jax.shard_map(
        per_device,
        mesh=mesh,
        in_specs=placed,
        out_specs=(P(None, "enc", "lon", None), P(), P()),
        check_vma=False,
    )
```

```python
import functools
import math

import jax
import jax.numpy as jnp
import numpy as np
from jax import lax
from jax.experimental import pallas as pl
from jax.experimental.pallas import tpu as pltpu
from jax.sharding import PartitionSpec as P

SLOTS = 52
HEADS = 16
HEAD_WIDTH = 32
WIDTH = 512
FF = 2048
LEVELS = 4
ROWS = 6
COLS = 12
SPOTS = ROWS * COLS
TOKENS = LEVELS * SPOTS
HALF = TOKENS // 2
PIXELS = 100
PER = SLOTS // 4
EPSILON = 1e-05
NTOK = 36864
PARTS = 4
PART_ROWS = 1024
PART_COLS = 256
HALO = HALF // 2
MESH = pl.DeviceIdType.MESH

f32 = jnp.float32
bf16 = jnp.bfloat16


def dot(a, b, contract=((1,), (0,))):
    return lax.dot_general(a, b, (contract, ((), ())), preferred_element_type=f32)


def normed(values, gain):
    mean = jnp.mean(values, axis=-1, keepdims=True)
    centred = values - mean
    variance = jnp.mean(centred * centred, axis=-1, keepdims=True)
    return (centred * lax.rsqrt(variance + EPSILON) * gain).astype(bf16)


def pooled_at(r, c, l):
    return l * SPOTS + c * ROWS + r


def piece_at(r, c, l):
    return (r * (COLS // 2) + c) * LEVELS + l


def natural_at(r, c, l):
    return (r * COLS + c) * LEVELS + l


def shifted_at(r, c, l):
    pair, place = ((1, 0), (0, 0), (0, 1), (1, 1))[l]
    return (r // 3) * HALF + pair * HALO + ((r % 3) * COLS + c) * 2 + place


def matrix_of(rows, cols, entries):
    matrix = np.zeros((rows, cols), np.float32)
    for r in range(ROWS):
        for c in range(COLS // 2):
            for l in range(LEVELS):
                matrix[entries(r, c, l)] = 1.0
    return matrix


def order_matrices():
    half = COLS // 2
    return (
        matrix_of(HALF, TOKENS, lambda r, c, l: (piece_at(r, c, l), pooled_at(r, c, l))),
        matrix_of(TOKENS, TOKENS, lambda r, c, l: (shifted_at(r, c, l), pooled_at(r, half + c, l))),
        matrix_of(HALF, TOKENS, lambda r, c, l: (piece_at(r, c, l), natural_at(r, c, l))),
        matrix_of(TOKENS, TOKENS, lambda r, c, l: (shifted_at(r, c, l), natural_at(r, half + c, l))),
        matrix_of(TOKENS, HALF, lambda r, c, l: (shifted_at(r, half + c, l), piece_at(r, c, l))),
        matrix_of(HALF, TOKENS, lambda r, c, l: (piece_at(r, c, l), shifted_at(r, half + c, l))),
    )


def final_matrices():
    half = COLS // 2
    return (
        matrix_of(TOKENS, TOKENS, lambda r, c, l: (natural_at(r, half + c, l), shifted_at(r, c, l))),
        matrix_of(TOKENS, HALF, lambda r, c, l: (natural_at(r, c, l), piece_at(r, c, l))),
    )


def pixel_matrix():
    matrix = np.zeros((4 * SPOTS, 4 * SPOTS), np.float32)
    for owner in range(4):
        for c in range(COLS):
            for r in range(ROWS):
                matrix[owner * SPOTS + c * ROWS + r, c * 4 * ROWS + owner * ROWS + r] = 1.0
    return matrix


def head_rows():
    mask = np.zeros((HEADS, WIDTH), np.float32)
    for h in range(HEADS):
        mask[h, h * HEAD_WIDTH : (h + 1) * HEAD_WIDTH] = 1.0
    return mask


def spread_matrix():
    one = np.zeros((LEVELS * HEADS, LEVELS * WIDTH), np.float32)
    for l in range(LEVELS):
        for h in range(HEADS):
            at = l * WIDTH + h * HEAD_WIDTH
            one[l * HEADS + h, at : at + HEAD_WIDTH] = 1.0
    return np.concatenate([one, one], axis=0)


def mesh_id(x, y, z, core):
    return (lax.rem(y, 2) * 2 + core, x * 8 + z * 2 + y // 2)


def split_parts(values):
    first = lax.broadcasted_iota(jnp.int32, values.shape, 1) < 64
    high = values.astype(bf16).astype(f32)
    return jnp.where(first, high, values - high).astype(bf16)


def main_kernel(
    ids,
    pool_temp,
    window_temp,
    pixels,
    pixel_order,
    latents,
    query_weight,
    key_weight,
    heads,
    first_gain,
    second_gain,
    embed_bias,
    embed_hbm,
    value_hbm,
    pool_hbm,
    spread_hbm,
    qkv_hbm,
    proj_hbm,
    up_hbm,
    down_hbm,
    cot_hbm,
    mat0_hbm,
    mat1_hbm,
    mat2_hbm,
    mat3_hbm,
    mat4_hbm,
    mat5_hbm,
    output,
    back,
    result,
    embed_weight,
    value_weight,
    pool_weight,
    spread,
    qkv_weight,
    proj_weight,
    up_weight,
    down_weight,
    cotangent,
    mat0,
    mat1,
    mat2,
    mat3,
    mat4,
    mat5,
    bias,
    outgoing,
    arrived,
    tokens,
    scores,
    values,
    sums,
    cot_left,
    cot_east,
    left,
    east,
    wide,
    cot_shifted,
    back_grad,
    qs,
    ks,
    vs,
    masks,
    attended,
    norm2,
    norm2_t,
    total,
    leave,
    grads,
    pair,
    work,
    got1,
    got2,
    got3,
    load_sem,
    send,
    recv,
    ring_send,
    ring_recv,
    pair_send,
    pair_recv,
):
    enc = lax.axis_index("enc")
    lon = lax.axis_index("lon")
    mate = enc + 1 - 2 * lax.rem(enc, 2)
    peers = (mate, lax.rem(enc + 2, 4), lax.rem(mate + 2, 4))
    west_id = (enc, lax.rem(lon + 31, 32))
    east_id = (enc, lax.rem(lon + 1, 32))
    core = lax.rem(enc, 2)
    x_at = lon // 8
    y_at = lax.rem(lon, 2) * 2 + enc // 2
    z_at = lax.rem(lon // 2, 4)

    def along(dim, by):
        is_x = (2 - dim) * (1 - dim) // 2
        is_y = dim * (2 - dim)
        is_z = dim * (dim - 1) // 2
        return mesh_id(
            lax.rem(x_at + by * is_x, 4),
            lax.rem(y_at + by * is_y, 4),
            lax.rem(z_at + by * is_z, 4),
            core,
        )

    def place_along(dim):
        is_x = (2 - dim) * (1 - dim) // 2
        is_y = dim * (2 - dim)
        is_z = dim * (dim - 1) // 2
        return x_at * is_x + y_at * is_y + z_at * is_z

    barrier = pltpu.get_barrier_semaphore()
    for peer in peers:
        pl.semaphore_signal(barrier, inc=1, device_id=(peer, lon), device_id_type=MESH)
    for other in (west_id, east_id):
        pl.semaphore_signal(barrier, inc=1, device_id=other, device_id_type=MESH)
    for dim in range(3):
        for by in range(1, 4):
            pl.semaphore_signal(barrier, inc=1, device_id=along(dim, by), device_id_type=MESH)

    loads = {}
    for index, (name, source, target) in enumerate(
        (
            ("embed", embed_hbm, embed_weight),
            ("value", value_hbm, value_weight),
            ("spread", spread_hbm, spread),
            ("pool", pool_hbm, pool_weight),
            ("cot", cot_hbm, cotangent),
            ("mat2", mat2_hbm, mat2),
            ("mat0", mat0_hbm, mat0),
            ("mat1", mat1_hbm, mat1),
            ("mat3", mat3_hbm, mat3),
            ("mat4", mat4_hbm, mat4),
            ("mat5", mat5_hbm, mat5),
            ("down", down_hbm, down_weight),
            ("qkv", qkv_hbm, qkv_weight),
            ("proj", proj_hbm, proj_weight),
            ("up", up_hbm, up_weight),
        )
    ):
        loads[name] = pltpu.make_async_copy(source, target, load_sem.at[index])
        loads[name].start()

    def remote(source, target, index, device):
        copy = pltpu.make_async_remote_copy(
            src_ref=source,
            dst_ref=target,
            send_sem=send.at[index],
            recv_sem=recv.at[index],
            device_id=device,
            device_id_type=MESH,
        )
        copy.start()
        return copy

    def sort_pixels(slot, _):
        block = pixels[slot].astype(f32).reshape(4 * SPOTS, PIXELS).astype(bf16)
        block = dot(pixel_order[...], block).astype(bf16).astype(f32)
        for owner in range(4):
            outgoing[owner, slot] = block[owner * SPOTS : (owner + 1) * SPOTS].astype(bf16)
        return 0

    lax.fori_loop(0, PER, sort_pixels, 0)
    pl.semaphore_wait(barrier, 14)
    copy_far = remote(outgoing.at[peers[1]], arrived.at[1], 1, (peers[1], lon))
    copy_other = remote(outgoing.at[peers[2]], arrived.at[2], 2, (peers[2], lon))
    copy_mate = remote(outgoing.at[peers[0]], arrived.at[0], 0, (peers[0], lon))

    bias[...] = embed_bias[...].astype(f32)
    queries = dot(latents[...], query_weight[...]).astype(bf16).astype(f32)
    blocks = [queries[l : l + 1] * heads[...] for l in range(LEVELS)]
    blocks = jnp.concatenate(blocks, axis=0).astype(bf16)
    head_of = lax.rem(lax.broadcasted_iota(jnp.int32, (LEVELS * HEADS, 1), 0), HEADS)
    temp = jnp.zeros((LEVELS * HEADS, 1), f32)
    for h in range(HEADS):
        temp = jnp.where(head_of == h, pool_temp[h] * (1.0 / math.sqrt(HEAD_WIDTH)), temp)
    folded = dot(blocks, key_weight[...], ((1,), (1,))) * temp
    high = folded.astype(bf16)
    low = (folded - high.astype(f32)).astype(bf16)
    keys = jnp.concatenate([high, high, low, low], axis=0)

    def token_of(block, slot):
        level = ids[slot]
        return dot(block, embed_weight[level]) + bias[pl.ds(level, 1), :]

    def embed_near(i, _):
        near = token_of(outgoing[enc, i], enc * PER + i)
        far = token_of(arrived[0, i], mate * PER + i)
        tokens[i] = jnp.concatenate([near, far], axis=0).astype(bf16)
        return 0

    def embed_far(i, _):
        near = token_of(arrived[1, i], peers[1] * PER + i)
        far = token_of(arrived[2, i], peers[2] * PER + i)
        tokens[i] = jnp.concatenate([near, far], axis=0).astype(bf16)
        return 0

    def project(first, count):
        block = jnp.concatenate([tokens[first + i] for i in range(count)], axis=0)
        projected = dot(block, value_weight[...])
        scored = dot(block, keys, ((1,), (1,)))
        scored = scored[:, :128] + scored[:, 128:]
        for i in range(2 * count):
            values[first * 2 + i] = projected[i * SPOTS : (i + 1) * SPOTS]
            scores[first * 2 + i] = scored[i * SPOTS : (i + 1) * SPOTS]

    def project_two(i, _):
        project(2 * i, 2)
        return 0

    def mix(stage, first, count):
        probs = jnp.concatenate([scores[first + i] for i in range(count)], axis=0)
        split = split_parts(probs)
        for l in range(LEVELS):
            wider = dot(split, spread[:, l * WIDTH : (l + 1) * WIDTH])
            part = sums[stage, l]
            for i in range(count):
                part = part + wider[i * SPOTS : (i + 1) * SPOTS] * values[first + i]
            sums[stage, l] = part

    def pool_stage(stage, embed):
        lax.fori_loop(0, PER, embed, 0)
        if stage == 0:
            loads["value"].wait()
        lax.fori_loop(0, PER // 2, project_two, 0)
        project(PER - 1, 1)
        peak = scores[0]
        for s in range(1, 2 * PER):
            peak = jnp.maximum(peak, scores[s])
        weight = jnp.zeros_like(peak)
        for s in range(2 * PER):
            exponent = jnp.exp(scores[s] - peak)
            scores[s] = exponent
            weight = weight + exponent
        sums[stage] = jnp.zeros((LEVELS, SPOTS, WIDTH), f32)
        if stage == 0:
            loads["spread"].wait()

        def mix_four(i, _):
            mix(stage, 4 * i, 4)
            return 0

        lax.fori_loop(0, 2 * PER // 4, mix_four, 0)
        mix(stage, 2 * PER - 2, 2)
        return peak, weight

    loads["embed"].wait()
    copy_mate.wait_recv()
    peak_near, weight_near = pool_stage(0, embed_near)
    copy_far.wait_recv()
    copy_other.wait_recv()
    loads["cot"].wait()
    loads["mat2"].wait()
    cot_left[...] = dot(mat2[...], cotangent[...]).astype(bf16)
    copy_cot = remote(cot_left, cot_east, 3, west_id)
    peak_far, weight_far = pool_stage(1, embed_far)

    peak = jnp.maximum(peak_near, peak_far)
    near = jnp.exp(peak_near - peak)
    far = jnp.exp(peak_far - peak)
    inverse = 1.0 / (weight_near * near + weight_far * far)
    shares = split_parts(jnp.concatenate([near * inverse, far * inverse], axis=0))
    pooled = []
    for l in range(LEVELS):
        share = dot(shares, spread[:, l * WIDTH : (l + 1) * WIDTH])
        pooled.append(share[:SPOTS] * sums[0, l] + share[SPOTS:] * sums[1, l])
    pooled = jnp.concatenate(pooled, axis=0).astype(bf16)
    loads["pool"].wait()
    projected = dot(pooled, pool_weight[...])
    stream = jnp.concatenate(
        [
            projected[l * SPOTS : (l + 1) * SPOTS] + latents[l : l + 1].astype(f32)
            for l in range(LEVELS)
        ],
        axis=0,
    ).astype(bf16)
    loads["mat0"].wait()
    left[...] = dot(mat0[...], stream).astype(bf16)
    copy_left = remote(left, east, 4, west_id)
    loads["mat1"].wait()
    kept = dot(mat1[...], stream)
    copy_cot.wait_recv()
    loads["mat3"].wait()
    loads["mat4"].wait()
    cot = (dot(mat3[...], cotangent[...]) + dot(mat4[...], cot_east[...])).astype(bf16)
    cot_shifted[...] = cot
    loads["down"].wait()
    for j in range(4):
        back_grad[j] = dot(cot, down_weight[j * 512 : (j + 1) * 512], ((1,), (1,)))
    copy_left.wait_recv()
    own = (kept + dot(mat4[...], east[...])).astype(bf16)
    wide[HALF : HALF + TOKENS] = own
    copy_up = remote(
        wide.at[pl.ds(HALF, HALF)],
        wide.at[pl.ds(HALF + TOKENS, HALF)],
        5,
        (lax.rem(enc + 3, 4), lon),
    )
    copy_down = remote(
        wide.at[pl.ds(TOKENS, HALF)], wide.at[pl.ds(0, HALF)], 6, (lax.rem(enc + 1, 4), lon)
    )

    loads["qkv"].wait()
    norm = normed(own.astype(f32), first_gain[...])
    own_q = dot(norm, qkv_weight[:, :WIDTH])
    own_k = dot(norm, qkv_weight[:, WIDTH : 2 * WIDTH])
    own_v = dot(norm, qkv_weight[:, 2 * WIDTH :])
    row = lax.broadcasted_iota(jnp.int32, (HALO, HALF), 0)
    col = lax.broadcasted_iota(jnp.int32, (HALO, HALF), 1)
    same = lax.rem(row, 2) == lax.rem(col, 2)
    first_key = jnp.where(enc == 0, HALO, 0)
    last_key = jnp.where(enc == 3, HALO, HALF)
    ones = jnp.ones((HALF, 128), f32)
    for win in range(2):
        inside = (col >= first_key) if win == 0 else (col < last_key)
        masks[win * 2] = jnp.where(inside, 0.0, -1e30)
        masks[win * 2 + 1] = jnp.where(inside & same, 0.0, -1e30)
    copy_up.wait_recv()
    copy_down.wait_recv()
    halo = jnp.concatenate([wide[:HALF], wide[HALF + TOKENS :]], axis=0).astype(f32)
    norm = normed(halo, first_gain[...])
    halo_k = dot(norm, qkv_weight[:, WIDTH : 2 * WIDTH])
    halo_v = dot(norm, qkv_weight[:, 2 * WIDTH :])
    for win in range(2):
        for two in range(2):
            at = win * HALF + two * HALO
            rows = slice(at, at + HALO)
            for g in range(4):
                lanes = slice(g * 128, (g + 1) * 128)
                index = (win * 2 + two) * 4 + g
                qs[index] = own_q[rows, lanes]
                key = (halo_k[rows, lanes], own_k[rows, lanes])
                value = (halo_v[rows, lanes], own_v[rows, lanes])
                if win == 1:
                    key, value = key[::-1], value[::-1]
                ks[index] = jnp.concatenate(key, axis=0).astype(bf16)
                value = jnp.concatenate(value, axis=0)
                vs[index] = jnp.concatenate([value, ones], axis=1).astype(bf16)

    lane = lax.broadcasted_iota(jnp.int32, (HALO, 128), 1) // HEAD_WIDTH

    def attend(index, _):
        group = lax.rem(index, 4)
        query = qs[index]
        mask = masks[index // 4]
        stacked = [jnp.where(lane == h, query, 0.0) for h in range(4)]
        raw = dot(jnp.concatenate(stacked, axis=0).astype(bf16), ks[index], ((1,), (1,)))
        exponents = []
        for h in range(4):
            masked = raw[h * HALO : (h + 1) * HALO] + mask
            top = jnp.max(masked, axis=-1, keepdims=True)
            factor = window_temp[group * 4 + h] * (1.0 / math.sqrt(HEAD_WIDTH))
            exponents.append(jnp.exp((masked - top) * factor).astype(bf16).astype(f32))
        exponent = jnp.concatenate(exponents, axis=0).astype(bf16)
        mixed = dot(exponent, vs[index])
        above = mixed[:HALO, :128]
        under = mixed[:HALO, 128:]
        for h in range(1, 4):
            rows = slice(h * HALO, (h + 1) * HALO)
            above = jnp.where(lane == h, mixed[rows, :128], above)
            under = jnp.where(lane == h, mixed[rows, 128:], under)
        attended[index] = above / under
        return 0

    lax.fori_loop(0, 16, attend, 0, unroll=2)

    rows = [
        jnp.concatenate([attended[block * 4 + g] for g in range(4)], axis=1) for block in range(4)
    ]
    loads["proj"].wait()
    mixed = dot(jnp.concatenate(rows, axis=0).astype(bf16), proj_weight[...])
    middle = (own.astype(f32) + mixed).astype(bf16).astype(f32)
    norm = normed(middle, second_gain[...])
    norm2[...] = norm
    norm2_t[...] = norm.T
    total[...] = middle

    sizes = (PART_ROWS // 4, PART_ROWS // 16, PART_ROWS // 64)
    slots = (got1, got2, got3)
    dims = [[lax.rem(p + core + phase, 3) for phase in range(3)] for p in range(PARTS)]
    mine = [[place_along(dims[p][phase]) for phase in range(3)] for p in range(PARTS)]
    starts = []
    for p in range(PARTS):
        at = [0]
        for phase in range(3):
            at.append(at[-1] + mine[p][phase] * sizes[phase])
        starts.append(at)
    pair_id = (mate, lon)
    pair_copies = []
    copies = {}

    def give_pair(index, source, target):
        copy = pltpu.make_async_remote_copy(
            src_ref=source,
            dst_ref=target,
            send_sem=pair_send.at[index],
            recv_sem=pair_recv.at[index],
            device_id=pair_id,
            device_id_type=MESH,
        )
        copy.start()
        pair_copies.append(copy)
        return copy

    def ring_copy(way, p, phase, by, source, target):
        return pltpu.make_async_remote_copy(
            src_ref=source,
            dst_ref=target,
            send_sem=ring_send.at[way, p, phase, by - 1],
            recv_sem=ring_recv.at[way, p, phase, by - 1],
            device_id=along(dims[p][phase], by),
            device_id_type=MESH,
        )

    def scatter(p, phase):
        size = sizes[phase]
        for by in range(1, 4):
            target = lax.rem(mine[p][phase] + by, 4)
            first = pl.multiple_of(starts[p][phase] + target * size, 16)
            source = work.at[p, pl.ds(first, size)]
            copy = ring_copy(0, p, phase, by, source, slots[phase].at[p, by - 1])
            copy.start()
            copies[0, p, phase, by] = copy

    def add_up(p, phase):
        for by in range(1, 4):
            copies[0, p, phase, by].wait_recv()
        size = sizes[phase]
        first = pl.multiple_of(starts[p][phase + 1], 16)
        held = work[p, pl.ds(first, size), :].astype(f32)
        for k in range(3):
            held = held + slots[phase][p, k].astype(f32)
        if phase < 2:
            work[p, pl.ds(first, size), :] = held.astype(bf16)
        else:
            result[core, p, pl.ds(first, size), :] = held.astype(bf16)

    def gather(p, phase):
        size = sizes[phase]
        first = pl.multiple_of(starts[p][phase + 1], 16)
        piece = result.at[core, p, pl.ds(first, size)]
        for by in range(1, 4):
            copy = ring_copy(1, p, phase, by, piece, piece)
            copy.start()
            copies[1, p, phase, by] = copy

    def gathered(p, phase):
        size = sizes[phase]
        for by in range(1, 4):
            source = lax.rem(mine[p][phase] + 4 - by, 4)
            first = pl.multiple_of(starts[p][phase] + source * size, 16)
            piece = result.at[core, p, pl.ds(first, size)]
            ring_copy(1, p, phase, by, piece, piece).wait_recv()

    def mlp(j):
        columns = slice(j * 512, (j + 1) * 512)
        x = dot(norm2[...], up_weight[:, columns])
        cubic = 0.044715 * (x * x)
        scale = math.sqrt(2.0 / math.pi)
        bend = jnp.tanh(scale * (x * (1.0 + cubic)))
        hidden = (0.5 * x * (1.0 + bend)).astype(bf16)
        slope = 0.5 * (1.0 + bend) + 0.5 * x * (1.0 - bend * bend) * (scale * (1.0 + 3.0 * cubic))
        slope = (slope * back_grad[j]).astype(bf16)
        down_grad = dot(hidden, cot_shifted[...], ((0,), (0,))).astype(bf16)
        up_grad = dot(norm2_t[...], slope).astype(bf16)
        for i in range(2):
            lanes = slice(i * PART_COLS, (i + 1) * PART_COLS)
            grads[0, j, i * 512 : (i + 1) * 512] = up_grad[:, lanes]
            grads[1, j, i * 512 : (i + 1) * 512] = down_grad[:, lanes]
        total[...] += dot(hidden, down_weight[columns])

    def reduce_pair(p):
        pair_copies[p].wait_recv()
        work[p] = (grads[core, p].astype(f32) + pair[p].astype(f32)).astype(bf16)
        scatter(p, 0)

    loads["up"].wait()
    for j in range(PARTS):
        mlp(j)
        give_pair(j, grads.at[1 - core, j], pair.at[j])
        if j > 0:
            reduce_pair(j - 1)
    reduce_pair(PARTS - 1)
    done = total[...].astype(bf16)
    output[...] = done
    loads["mat5"].wait()
    leave[...] = dot(mat5[...], done).astype(bf16)
    copy_back = remote(leave, back, 7, east_id)
    for phase in range(3):
        for p in range(PARTS):
            add_up(p, phase)
            if phase < 2:
                scatter(p, phase + 1)
            else:
                gather(p, 2)
    for phase in (2, 1, 0):
        for p in range(PARTS):
            gathered(p, phase)
            if phase > 0:
                gather(p, phase - 1)
            else:
                whole = result.at[core, p]
                give_pair(PARTS + p, whole, whole)
    for p in range(PARTS):
        whole = result.at[1 - core, p]
        pltpu.make_async_remote_copy(
            src_ref=whole,
            dst_ref=whole,
            send_sem=pair_send.at[PARTS + p],
            recv_sem=pair_recv.at[PARTS + p],
            device_id=pair_id,
            device_id_type=MESH,
        ).wait_recv()
    copy_back.wait_recv()
    for copy in (copy_far, copy_other, copy_mate, copy_cot, copy_left, copy_up, copy_down):
        copy.wait_send()
    copy_back.wait_send()
    for copy in pair_copies:
        copy.wait_send()
    for copy in copies.values():
        copy.wait_send()


def main_call(
    pixels,
    ids,
    embed_weight,
    embed_bias,
    latents,
    query_weight,
    key_weight,
    value_weight,
    pool_weight,
    pool_temp,
    first_gain,
    qkv_weight,
    window_temp,
    proj_weight,
    second_gain,
    up_weight,
    down_weight,
    cot,
):
    vmem = pl.BlockSpec(memory_space=pltpu.VMEM)
    smem = pl.BlockSpec(memory_space=pltpu.SMEM)
    anywhere = pl.BlockSpec(memory_space=pl.ANY)
    matrices = [jnp.asarray(matrix, bf16) for matrix in order_matrices()]
    spread = jnp.asarray(spread_matrix(), bf16)
    loaded = (
        embed_weight,
        value_weight,
        pool_weight,
        spread,
        qkv_weight,
        proj_weight,
        up_weight,
        down_weight,
        cot,
        *matrices,
    )
    piece = pltpu.VMEM((HALF, WIDTH), bf16)
    part = pltpu.VMEM((PARTS, PART_ROWS, PART_COLS), bf16)
    return pl.pallas_call(
        main_kernel,
        out_shape=(
            jax.ShapeDtypeStruct((TOKENS, WIDTH), bf16),
            jax.ShapeDtypeStruct((HALF, WIDTH), bf16),
            jax.ShapeDtypeStruct((2, PARTS, PART_ROWS, PART_COLS), bf16),
        ),
        in_specs=[smem] * 3 + [vmem] * 9 + [anywhere] * len(loaded),
        out_specs=(vmem, vmem, vmem),
        scratch_shapes=[pltpu.VMEM(value.shape, bf16) for value in loaded]
        + [
            pltpu.VMEM((SLOTS, WIDTH), f32),
            pltpu.VMEM((4, PER, SPOTS, PIXELS), bf16),
            pltpu.VMEM((3, PER, SPOTS, PIXELS), bf16),
            pltpu.VMEM((PER, 2 * SPOTS, WIDTH), bf16),
            pltpu.VMEM((2 * PER, SPOTS, 128), f32),
            pltpu.VMEM((2 * PER, SPOTS, WIDTH), f32),
            pltpu.VMEM((2, LEVELS, SPOTS, WIDTH), f32),
            piece,
            piece,
            piece,
            piece,
            pltpu.VMEM((2 * TOKENS, WIDTH), bf16),
            pltpu.VMEM((TOKENS, WIDTH), bf16),
            pltpu.VMEM((4, TOKENS, 512), f32),
            pltpu.VMEM((16, HALO, 128), f32),
            pltpu.VMEM((16, HALF, 128), bf16),
            pltpu.VMEM((16, HALF, 256), bf16),
            pltpu.VMEM((4, HALO, HALF), f32),
            pltpu.VMEM((16, HALO, 128), f32),
            pltpu.VMEM((TOKENS, WIDTH), bf16),
            pltpu.VMEM((WIDTH, TOKENS), bf16),
            pltpu.VMEM((TOKENS, WIDTH), f32),
            piece,
            pltpu.VMEM((2, PARTS, PART_ROWS, PART_COLS), bf16),
            part,
            part,
            pltpu.VMEM((PARTS, 3, PART_ROWS // 4, PART_COLS), bf16),
            pltpu.VMEM((PARTS, 3, PART_ROWS // 16, PART_COLS), bf16),
            pltpu.VMEM((PARTS, 3, PART_ROWS // 64, PART_COLS), bf16),
            pltpu.SemaphoreType.DMA((len(loaded),)),
            pltpu.SemaphoreType.DMA((8,)),
            pltpu.SemaphoreType.DMA((8,)),
            pltpu.SemaphoreType.DMA((2, PARTS, 3, 3)),
            pltpu.SemaphoreType.DMA((2, PARTS, 3, 3)),
            pltpu.SemaphoreType.DMA((2 * PARTS,)),
            pltpu.SemaphoreType.DMA((2 * PARTS,)),
        ],
        compiler_params=pltpu.CompilerParams(
            collective_id=1, has_side_effects=True, vmem_limit_bytes=60 * 1024 * 1024
        ),
        name="main",
    )(
        ids,
        pool_temp,
        window_temp,
        pixels,
        jnp.asarray(pixel_matrix(), bf16),
        latents,
        query_weight,
        key_weight,
        jnp.asarray(head_rows(), f32),
        first_gain[None, :],
        second_gain[None, :],
        embed_bias,
        *loaded,
    )


def finish_kernel(sums, shifted, back, keep, take, output, up_grad, down_grad):
    scaling = 1.0 / math.sqrt(NTOK)

    @pl.when(pl.program_id(0) == 0)
    def _():
        whole = dot(keep[...], shifted[...]) + dot(take[...], back[...])
        output[...] = whole.astype(bf16)

    for i in range(2):
        lanes = slice(i * PART_COLS, (i + 1) * PART_COLS)
        rows = slice(i * 512, (i + 1) * 512)
        up_grad[:, lanes] = sums[0, 0, rows].astype(f32) * scaling
        down_grad[:, lanes] = sums[1, 0, rows].astype(f32) * scaling


def finish(sums, shifted, back):
    keep, take = final_matrices()
    fixed = lambda *shape: pl.BlockSpec(shape, lambda p: (0, 0))
    return pl.pallas_call(
        finish_kernel,
        grid=(PARTS,),
        out_shape=(
            jax.ShapeDtypeStruct((TOKENS, WIDTH), bf16),
            jax.ShapeDtypeStruct((WIDTH, FF), f32),
            jax.ShapeDtypeStruct((FF, WIDTH), f32),
        ),
        in_specs=[
            pl.BlockSpec((2, 1, PART_ROWS, PART_COLS), lambda p: (0, p, 0, 0)),
            fixed(TOKENS, WIDTH),
            fixed(HALF, WIDTH),
            fixed(TOKENS, TOKENS),
            fixed(TOKENS, HALF),
        ],
        out_specs=(
            fixed(TOKENS, WIDTH),
            pl.BlockSpec((WIDTH, 512), lambda p: (0, p)),
            pl.BlockSpec((512, WIDTH), lambda p: (p, 0)),
        ),
        compiler_params=pltpu.CompilerParams(vmem_limit_bytes=32 * 1024 * 1024),
        name="finish",
    )(
        sums,
        shifted,
        back,
        jnp.asarray(keep, bf16),
        jnp.asarray(take, bf16),
    )


def per_device(
    pixel_field,
    level_ids,
    embed_weight,
    embed_bias,
    latents,
    query_weight,
    key_weight,
    value_weight,
    pool_weight,
    pool_temp,
    first_gain,
    qkv_weight,
    window_temp,
    proj_weight,
    second_gain,
    up_weight,
    down_weight,
    cotangent,
):
    cot = jnp.transpose(cotangent, (1, 2, 0, 3)).reshape(TOKENS, WIDTH)
    shifted, back, sums = main_call(
        jnp.transpose(pixel_field, (0, 3, 1, 2)),
        level_ids,
        embed_weight,
        embed_bias,
        latents,
        query_weight,
        key_weight,
        value_weight,
        pool_weight,
        pool_temp,
        first_gain,
        qkv_weight,
        window_temp,
        proj_weight,
        second_gain,
        up_weight,
        down_weight,
        cot,
    )
    output, up_grad, down_grad = finish(sums, shifted, back)
    output = output.reshape(ROWS, COLS, LEVELS, WIDTH)
    return (jnp.transpose(output, (2, 0, 1, 3)), up_grad, down_grad)


def solution(mesh):
    placed = (P("enc", None, None, "lon"),) + (P(),) * 16 + (P(None, "enc", "lon", None),)
    return jax.shard_map(
        per_device,
        mesh=mesh,
        in_specs=placed,
        out_specs=(P(None, "enc", "lon", None), P(), P()),
        check_vma=False,
    )
```

```python
import itertools
import math

import jax
import jax.numpy as jnp
import numpy as np
from jax import lax
from jax.experimental import pallas as pl
from jax.experimental.pallas import tpu as pltpu
from jax.sharding import PartitionSpec as P

SLOTS = 52
HEADS = 16
HEAD_WIDTH = 32
WIDTH = 512
FF = 2048
LEVELS = 4
ROWS = 6
COLS = 12
SPOTS = ROWS * COLS
TOKENS = LEVELS * SPOTS
HALF = TOKENS // 2
PIXELS = 100
PER = SLOTS // 4
FAR = 7
EPSILON = 1e-05
NTOK = 36864
PARTS = 4
PART_ROWS = 1024
PART_COLS = 256
HALO = HALF // 2
LEAD = 40
STAGES = 3
PHASES = ((0,), (1, 2))
MESH = pl.DeviceIdType.MESH

f32 = jnp.float32
bf16 = jnp.bfloat16


def dot(a, b, contract=((1,), (0,))):
    return lax.dot_general(a, b, (contract, ((), ())), preferred_element_type=f32)


def normed(values, gain):
    mean = jnp.mean(values, axis=-1, keepdims=True)
    centred = values - mean
    variance = jnp.mean(centred * centred, axis=-1, keepdims=True)
    return (centred * lax.rsqrt(variance + EPSILON) * gain).astype(bf16)


def pooled_at(r, c, l):
    spot = c * ROWS + r
    if spot < LEAD:
        return l * LEAD + spot
    return LEVELS * LEAD + l * (SPOTS - LEAD) + spot - LEAD


def piece_at(r, c, l):
    return (r * (COLS // 2) + c) * LEVELS + l


def natural_at(r, c, l):
    return (r * COLS + c) * LEVELS + l


def shifted_at(r, c, l):
    pair, place = ((1, 0), (0, 0), (0, 1), (1, 1))[l]
    return (r // 3) * HALF + pair * HALO + ((r % 3) * COLS + c) * 2 + place


def matrix_of(rows, cols, entries):
    matrix = np.zeros((rows, cols), np.float32)
    for r in range(ROWS):
        for c in range(COLS // 2):
            for l in range(LEVELS):
                matrix[entries(r, c, l)] = 1.0
    return matrix


def order_matrices():
    half = COLS // 2
    return (
        matrix_of(HALF, LEVELS * LEAD, lambda r, c, l: (piece_at(r, c, l), pooled_at(r, c, l))),
        matrix_of(TOKENS, TOKENS, lambda r, c, l: (shifted_at(r, c, l), pooled_at(r, half + c, l))),
        matrix_of(HALF, TOKENS, lambda r, c, l: (piece_at(r, c, l), natural_at(r, c, l))),
        matrix_of(TOKENS, TOKENS, lambda r, c, l: (shifted_at(r, c, l), natural_at(r, half + c, l))),
        matrix_of(TOKENS, HALF, lambda r, c, l: (shifted_at(r, half + c, l), piece_at(r, c, l))),
        matrix_of(HALF, TOKENS, lambda r, c, l: (piece_at(r, c, l), shifted_at(r, half + c, l))),
    )


def final_matrices():
    half = COLS // 2
    return (
        matrix_of(TOKENS, TOKENS, lambda r, c, l: (natural_at(r, half + c, l), shifted_at(r, c, l))),
        matrix_of(TOKENS, HALF, lambda r, c, l: (natural_at(r, c, l), piece_at(r, c, l))),
    )


def pixel_matrix():
    matrix = np.zeros((4 * SPOTS, 4 * SPOTS), np.float32)
    for owner in range(4):
        for c in range(COLS):
            for r in range(ROWS):
                matrix[owner * SPOTS + c * ROWS + r, c * 4 * ROWS + owner * ROWS + r] = 1.0
    return matrix


def head_rows():
    mask = np.zeros((HEADS, WIDTH), np.float32)
    for h in range(HEADS):
        mask[h, h * HEAD_WIDTH : (h + 1) * HEAD_WIDTH] = 1.0
    return mask


def spread_matrix():
    one = np.zeros((LEVELS * HEADS, LEVELS * WIDTH), np.float32)
    for l in range(LEVELS):
        for h in range(HEADS):
            at = l * WIDTH + h * HEAD_WIDTH
            one[l * HEADS + h, at : at + HEAD_WIDTH] = 1.0
    return np.concatenate([one, one], axis=0)


def mesh_id(x, y, z, core):
    return (lax.rem(y, 2) * 2 + core, x * 8 + z * 2 + y // 2)


def split_parts(values):
    first = lax.broadcasted_iota(jnp.int32, values.shape, 1) < 64
    high = values.astype(bf16).astype(f32)
    return jnp.where(first, high, values - high).astype(bf16)


def main_kernel(
    ids,
    pool_temp,
    window_temp,
    pixels,
    pixel_order,
    latents,
    query_weight,
    key_weight,
    heads,
    first_gain,
    second_gain,
    embed_bias,
    embed_hbm,
    value_hbm,
    pool_hbm,
    spread_hbm,
    qkv_hbm,
    proj_hbm,
    up_hbm,
    down_hbm,
    cot_hbm,
    mat0_hbm,
    mat1_hbm,
    mat2_hbm,
    mat3_hbm,
    mat4_hbm,
    mat5_hbm,
    output,
    back,
    whole,
    result,
    embed_weight,
    value_weight,
    pool_weight,
    spread,
    qkv_weight,
    proj_weight,
    up_weight,
    down_weight,
    cotangent,
    mat0,
    mat1,
    mat2,
    mat3,
    mat4,
    mat5,
    bias,
    outgoing,
    arrived,
    tokens,
    scores,
    values,
    sums,
    cot_left,
    cot_east,
    left,
    east,
    wide,
    cot_shifted,
    back_grad,
    qs,
    ks,
    vs,
    masks,
    attended,
    norm2,
    norm2_t,
    total,
    leave,
    grads,
    pair,
    work,
    got1,
    got2,
    load_sem,
    store_sem,
    send,
    recv,
    ring_send,
    ring_recv,
    pair_send,
    pair_recv,
):
    enc = lax.axis_index("enc")
    lon = lax.axis_index("lon")
    mate = enc + 1 - 2 * lax.rem(enc, 2)
    peers = (mate, lax.rem(enc + 2, 4), lax.rem(mate + 2, 4))
    west_id = (enc, lax.rem(lon + 31, 32))
    east_id = (enc, lax.rem(lon + 1, 32))
    core = lax.rem(enc, 2)
    x_at = lon // 8
    y_at = lax.rem(lon, 2) * 2 + enc // 2
    z_at = lax.rem(lon // 2, 4)

    position = (x_at, y_at, z_at)

    def is_axis(dim):
        return ((2 - dim) * (1 - dim) // 2, dim * (2 - dim), dim * (dim - 1) // 2)

    def moved(steps):
        at = list(position)
        for dim, by in steps:
            at = [place + by * axis for place, axis in zip(at, is_axis(dim))]
        return mesh_id(*[lax.rem(place, 4) for place in at], core)

    def place_along(dim):
        return sum(place * axis for place, axis in zip(position, is_axis(dim)))

    combos = [
        [by for by in itertools.product(range(4), repeat=len(phase)) if any(by)]
        for phase in PHASES
    ]
    others = set()
    for turn in range(3):
        for phase, bys in zip(PHASES, combos):
            for by in bys:
                step = [0, 0, 0]
                for dim, count in zip(phase, by):
                    step[(turn + dim) % 3] += count
                others.add(tuple(step))
    others = sorted(others)
    barrier = pltpu.get_barrier_semaphore()
    for peer in peers:
        pl.semaphore_signal(barrier, inc=1, device_id=(peer, lon), device_id_type=MESH)
    for other in (west_id, east_id):
        pl.semaphore_signal(barrier, inc=1, device_id=other, device_id_type=MESH)
    for step in others:
        device = moved(list(enumerate(step)))
        pl.semaphore_signal(barrier, inc=1, device_id=device, device_id_type=MESH)

    loads = {}
    for index, (name, source, target) in enumerate(
        (
            ("embed", embed_hbm, embed_weight),
            ("value", value_hbm, value_weight),
            ("spread", spread_hbm, spread),
            ("pool", pool_hbm, pool_weight),
            ("cot", cot_hbm, cotangent),
            ("mat2", mat2_hbm, mat2),
            ("mat0", mat0_hbm, mat0),
            ("mat1", mat1_hbm, mat1),
            ("mat3", mat3_hbm, mat3),
            ("mat4", mat4_hbm, mat4),
            ("mat5", mat5_hbm, mat5),
            ("down", down_hbm, down_weight),
            ("qkv", qkv_hbm, qkv_weight),
            ("proj", proj_hbm, proj_weight),
            ("up", up_hbm, up_weight),
        )
    ):
        loads[name] = pltpu.make_async_copy(source, target, load_sem.at[index])
        loads[name].start()

    def remote(source, target, index, device):
        copy = pltpu.make_async_remote_copy(
            src_ref=source,
            dst_ref=target,
            send_sem=send.at[index],
            recv_sem=recv.at[index],
            device_id=device,
            device_id_type=MESH,
        )
        copy.start()
        return copy

    def sort_pixels(slot, _):
        block = pixels[slot].astype(f32).reshape(4 * SPOTS, PIXELS).astype(bf16)
        block = dot(pixel_order[...], block).astype(bf16).astype(f32)
        for owner in range(4):
            outgoing[owner, slot] = block[owner * SPOTS : (owner + 1) * SPOTS].astype(bf16)
        return 0

    lax.fori_loop(0, PER, sort_pixels, 0)
    pl.semaphore_wait(barrier, 5 + len(others))
    far_copies = []
    for k, (first, count) in enumerate(((0, FAR), (FAR, PER - FAR))):
        slots_there = pl.ds(first, count)
        for i in (1, 2):
            far_copies.append(
                remote(
                    outgoing.at[peers[i], slots_there],
                    arrived.at[i, slots_there],
                    7 + 2 * k + i,
                    (peers[i], lon),
                )
            )
        if k == 0:
            copy_mate = remote(outgoing.at[peers[0]], arrived.at[0], 0, (peers[0], lon))

    bias[...] = embed_bias[...].astype(f32)
    queries = dot(latents[...], query_weight[...]).astype(bf16).astype(f32)
    blocks = [queries[l : l + 1] * heads[...] for l in range(LEVELS)]
    blocks = jnp.concatenate(blocks, axis=0).astype(bf16)
    head_of = lax.rem(lax.broadcasted_iota(jnp.int32, (LEVELS * HEADS, 1), 0), HEADS)
    temp = jnp.zeros((LEVELS * HEADS, 1), f32)
    for h in range(HEADS):
        temp = jnp.where(head_of == h, pool_temp[h] * (1.0 / math.sqrt(HEAD_WIDTH)), temp)
    folded = dot(blocks, key_weight[...], ((1,), (1,))) * temp
    high = folded.astype(bf16)
    low = (folded - high.astype(f32)).astype(bf16)
    keys = jnp.concatenate([high, high, low, low], axis=0)

    def token_of(block, slot):
        level = ids[slot]
        return dot(block, embed_weight[level]) + bias[pl.ds(level, 1), :]

    def embed_near(i, _):
        near = token_of(outgoing[enc, i], enc * PER + i)
        far = token_of(arrived[0, i], mate * PER + i)
        tokens[i] = jnp.concatenate([near, far], axis=0).astype(bf16)
        return 0

    def embed_far(first):
        def embed(i, _):
            near = token_of(arrived[1, first + i], peers[1] * PER + first + i)
            far = token_of(arrived[2, first + i], peers[2] * PER + first + i)
            tokens[i] = jnp.concatenate([near, far], axis=0).astype(bf16)
            return 0

        return embed

    def project(first, count):
        block = jnp.concatenate([tokens[first + i] for i in range(count)], axis=0)
        projected = dot(block, value_weight[...])
        scored = dot(block, keys, ((1,), (1,)))
        scored = scored[:, :128] + scored[:, 128:]
        for i in range(2 * count):
            values[first * 2 + i] = projected[i * SPOTS : (i + 1) * SPOTS]
            scores[first * 2 + i] = scored[i * SPOTS : (i + 1) * SPOTS]

    def project_two(i, _):
        project(2 * i, 2)
        return 0

    def mix(stage, first, count, lo, hi):
        probs = jnp.concatenate([scores[first + i, lo:hi] for i in range(count)], axis=0)
        split = split_parts(probs)
        size = hi - lo
        for l in range(LEVELS):
            wider = dot(split, spread[:, l * WIDTH : (l + 1) * WIDTH])
            part = sums[stage, l, lo:hi]
            for i in range(count):
                part = part + wider[i * size : (i + 1) * size] * values[first + i, lo:hi]
            sums[stage, l, lo:hi] = part

    def mix_all(stage, pairs, lo, hi):
        def mix_four(i, _):
            mix(stage, 4 * i, 4, lo, hi)
            return 0

        lax.fori_loop(0, pairs // 2, mix_four, 0)
        if pairs % 2:
            mix(stage, 2 * pairs - 2, 2, lo, hi)

    def pool_stage(stage, pairs, embed):
        lax.fori_loop(0, pairs, embed, 0)
        if stage == 0:
            loads["value"].wait()
        lax.fori_loop(0, pairs // 2, project_two, 0)
        if pairs % 2:
            project(pairs - 1, 1)
        peak = scores[0]
        for s in range(1, 2 * pairs):
            peak = jnp.maximum(peak, scores[s])
        weight = jnp.zeros_like(peak)
        for s in range(2 * pairs):
            exponent = jnp.exp(scores[s] - peak)
            scores[s] = exponent
            weight = weight + exponent
        sums[stage] = jnp.zeros((LEVELS, SPOTS, WIDTH), f32)
        return peak, weight

    loads["embed"].wait()
    copy_mate.wait_recv()
    stats = [pool_stage(0, PER, embed_near)]
    loads["spread"].wait()
    mix_all(0, PER, 0, SPOTS)
    far_copies[0].wait_recv()
    far_copies[1].wait_recv()
    stats.append(pool_stage(1, FAR, embed_far(0)))
    mix_all(1, FAR, 0, SPOTS)
    far_copies[2].wait_recv()
    far_copies[3].wait_recv()
    loads["cot"].wait()
    loads["mat2"].wait()
    own_cot = cotangent[...].astype(f32).reshape(TOKENS, WIDTH).astype(bf16)
    cot_left[...] = dot(mat2[...], own_cot).astype(bf16)
    copy_cot = remote(cot_left, cot_east, 3, west_id)
    stats.append(pool_stage(2, PER - FAR, embed_far(FAR)))

    peak = stats[0][0]
    for other, _ in stats[1:]:
        peak = jnp.maximum(peak, other)
    decays = [jnp.exp(top - peak) for top, _ in stats]
    inverse = 1.0 / sum(weight * decay for decay, (_, weight) in zip(decays, stats))
    decays = [decay * inverse for decay in decays]
    loads["pool"].wait()

    def finish_pool(lo, hi):
        shares = split_parts(jnp.concatenate([decay[lo:hi] for decay in decays], axis=0))
        size = hi - lo
        pooled = []
        for l in range(LEVELS):
            share = dot(shares, spread[:, l * WIDTH : (l + 1) * WIDTH])
            level = share[:size] * sums[0, l, lo:hi]
            for k in range(1, STAGES):
                level = level + share[k * size : (k + 1) * size] * sums[k, l, lo:hi]
            pooled.append(level)
        projected = dot(jnp.concatenate(pooled, axis=0).astype(bf16), pool_weight[...])
        rows = [
            projected[l * size : (l + 1) * size] + latents[l : l + 1].astype(f32)
            for l in range(LEVELS)
        ]
        return jnp.concatenate(rows, axis=0).astype(bf16)

    mix_all(2, PER - FAR, 0, LEAD)
    lead = finish_pool(0, LEAD)
    loads["mat0"].wait()
    left[...] = dot(mat0[...], lead).astype(bf16)
    copy_left = remote(left, east, 4, west_id)
    mix_all(2, PER - FAR, LEAD, SPOTS)
    stream = jnp.concatenate([lead, finish_pool(LEAD, SPOTS)], axis=0)
    loads["mat1"].wait()
    kept = dot(mat1[...], stream)
    copy_cot.wait_recv()
    loads["mat3"].wait()
    loads["mat4"].wait()
    cot = (dot(mat3[...], own_cot) + dot(mat4[...], cot_east[...])).astype(bf16)
    cot_shifted[...] = cot
    loads["down"].wait()
    for j in range(4):
        back_grad[j] = dot(cot, down_weight[j * 512 : (j + 1) * 512], ((1,), (1,)))
    copy_left.wait_recv()
    own = (kept + dot(mat4[...], east[...])).astype(bf16)
    wide[HALF : HALF + TOKENS] = own
    copy_up = remote(
        wide.at[pl.ds(HALF, HALF)],
        wide.at[pl.ds(HALF + TOKENS, HALF)],
        5,
        (lax.rem(enc + 3, 4), lon),
    )
    copy_down = remote(
        wide.at[pl.ds(TOKENS, HALF)], wide.at[pl.ds(0, HALF)], 6, (lax.rem(enc + 1, 4), lon)
    )

    loads["qkv"].wait()
    norm = normed(own.astype(f32), first_gain[...])
    own_q = dot(norm, qkv_weight[:, :WIDTH])
    own_k = dot(norm, qkv_weight[:, WIDTH : 2 * WIDTH])
    own_v = dot(norm, qkv_weight[:, 2 * WIDTH :])
    row = lax.broadcasted_iota(jnp.int32, (HALO, HALF), 0)
    col = lax.broadcasted_iota(jnp.int32, (HALO, HALF), 1)
    same = lax.rem(row, 2) == lax.rem(col, 2)
    first_key = jnp.where(enc == 0, HALO, 0)
    last_key = jnp.where(enc == 3, HALO, HALF)
    ones = jnp.ones((HALF, 128), f32)
    for win in range(2):
        inside = (col >= first_key) if win == 0 else (col < last_key)
        masks[win * 2] = jnp.where(inside, 0.0, -1e30)
        masks[win * 2 + 1] = jnp.where(inside & same, 0.0, -1e30)
    copy_up.wait_recv()
    copy_down.wait_recv()
    halo = jnp.concatenate([wide[:HALF], wide[HALF + TOKENS :]], axis=0).astype(f32)
    norm = normed(halo, first_gain[...])
    halo_k = dot(norm, qkv_weight[:, WIDTH : 2 * WIDTH])
    halo_v = dot(norm, qkv_weight[:, 2 * WIDTH :])
    for win in range(2):
        for two in range(2):
            at = win * HALF + two * HALO
            rows = slice(at, at + HALO)
            for g in range(4):
                lanes = slice(g * 128, (g + 1) * 128)
                index = (win * 2 + two) * 4 + g
                qs[index] = own_q[rows, lanes]
                key = (halo_k[rows, lanes], own_k[rows, lanes])
                value = (halo_v[rows, lanes], own_v[rows, lanes])
                if win == 1:
                    key, value = key[::-1], value[::-1]
                ks[index] = jnp.concatenate(key, axis=0).astype(bf16)
                value = jnp.concatenate(value, axis=0)
                vs[index] = jnp.concatenate([value, ones], axis=1).astype(bf16)

    lane = lax.broadcasted_iota(jnp.int32, (HALO, 128), 1) // HEAD_WIDTH

    def attend(index, _):
        group = lax.rem(index, 4)
        query = qs[index]
        mask = masks[index // 4]
        stacked = [jnp.where(lane == h, query, 0.0) for h in range(4)]
        raw = dot(jnp.concatenate(stacked, axis=0).astype(bf16), ks[index], ((1,), (1,)))
        exponents = []
        for h in range(4):
            masked = raw[h * HALO : (h + 1) * HALO] + mask
            top = jnp.max(masked, axis=-1, keepdims=True)
            factor = window_temp[group * 4 + h] * (1.0 / math.sqrt(HEAD_WIDTH))
            exponents.append(jnp.exp((masked - top) * factor).astype(bf16).astype(f32))
        exponent = jnp.concatenate(exponents, axis=0).astype(bf16)
        mixed = dot(exponent, vs[index])
        above = mixed[:HALO, :128]
        under = mixed[:HALO, 128:]
        for h in range(1, 4):
            rows = slice(h * HALO, (h + 1) * HALO)
            above = jnp.where(lane == h, mixed[rows, :128], above)
            under = jnp.where(lane == h, mixed[rows, 128:], under)
        attended[index] = above / under
        return 0

    lax.fori_loop(0, 16, attend, 0, unroll=2)

    rows = [
        jnp.concatenate([attended[block * 4 + g] for g in range(4)], axis=1) for block in range(4)
    ]
    loads["proj"].wait()
    mixed = dot(jnp.concatenate(rows, axis=0).astype(bf16), proj_weight[...])
    middle = (own.astype(f32) + mixed).astype(bf16).astype(f32)
    norm = normed(middle, second_gain[...])
    norm2[...] = norm
    norm2_t[...] = norm.T
    total[...] = middle

    got = (got1, got2)
    sizes = [PART_ROWS // 4, PART_ROWS // 64]
    offsets = [0, len(combos[0])]
    dims = [[[lax.rem(p + core + dim, 3) for dim in phase] for phase in PHASES] for p in range(PARTS)]
    mine = [[[place_along(dim) for dim in phase] for phase in dims[p]] for p in range(PARTS)]

    def chunk_of(places):
        chunk = 0
        for place in places:
            chunk = chunk * 4 + place
        return chunk

    starts = []
    for p in range(PARTS):
        at = [0]
        for phase in range(len(PHASES)):
            at.append(at[-1] + chunk_of(mine[p][phase]) * sizes[phase])
        starts.append(at)
    pair_id = (mate, lon)
    pair_copies = []
    stores = []
    copies = {}

    def give_pair(index, source, target):
        copy = pltpu.make_async_remote_copy(
            src_ref=source,
            dst_ref=target,
            send_sem=pair_send.at[index],
            recv_sem=pair_recv.at[index],
            device_id=pair_id,
            device_id_type=MESH,
        )
        copy.start()
        pair_copies.append(copy)
        return copy

    def ring_copy(way, p, phase, k, source, target):
        at = offsets[phase] + k
        return pltpu.make_async_remote_copy(
            src_ref=source,
            dst_ref=target,
            send_sem=ring_send.at[way, p, at],
            recv_sem=ring_recv.at[way, p, at],
            device_id=moved(list(zip(dims[p][phase], combos[phase][k]))),
            device_id_type=MESH,
        )

    def scatter(p, phase):
        size = sizes[phase]
        for k, by in enumerate(combos[phase]):
            target = chunk_of([lax.rem(at + step, 4) for at, step in zip(mine[p][phase], by)])
            first = pl.multiple_of(starts[p][phase] + target * size, 16)
            source = work.at[p, pl.ds(first, size)]
            copy = ring_copy(0, p, phase, k, source, got[phase].at[p, k])
            copy.start()
            copies[0, p, phase, k] = copy

    def add_up(p, phase):
        for k in range(len(combos[phase])):
            copies[0, p, phase, k].wait_recv()
        size = sizes[phase]
        first = pl.multiple_of(starts[p][phase + 1], 16)
        held = work[p, pl.ds(first, size), :].astype(f32)
        for k in range(len(combos[phase])):
            held = held + got[phase][p, k].astype(f32)
        if phase == 0:
            work[p, pl.ds(first, size), :] = held.astype(bf16)
            scatter(p, 1)
        else:
            result[core, p, pl.ds(first, size), :] = held.astype(bf16)
            gather(p, 1)

    def gather(p, phase):
        first = pl.multiple_of(starts[p][phase + 1], 16)
        piece = result.at[core, p, pl.ds(first, sizes[phase])]
        for k in range(len(combos[phase])):
            copy = ring_copy(1, p, phase, k, piece, piece)
            copy.start()
            copies[1, p, phase, k] = copy

    def gathered(p, phase):
        for k, by in enumerate(combos[phase]):
            source = chunk_of([lax.rem(at + 4 - step, 4) for at, step in zip(mine[p][phase], by)])
            first = pl.multiple_of(starts[p][phase] + source * sizes[phase], 16)
            piece = result.at[core, p, pl.ds(first, sizes[phase])]
            ring_copy(1, p, phase, k, piece, piece).wait_recv()
            if phase == 0:
                give_pair(PARTS + 4 * p + 1 + k, piece, piece)
        if phase == 1:
            gather(p, 0)
            first = pl.multiple_of(starts[p][1], 16)
            piece = result.at[core, p, pl.ds(first, sizes[0])]
            give_pair(PARTS + 4 * p, piece, piece)
        else:
            store(core, p)

    def store(half, p):
        copy = pltpu.make_async_copy(result.at[half, p], whole.at[half, p], store_sem.at[len(stores)])
        copy.start()
        stores.append(copy)

    def paired(p):
        for k in range(4):
            piece = result.at[1 - core, p, pl.ds(0, sizes[0])]
            pltpu.make_async_remote_copy(
                src_ref=piece,
                dst_ref=piece,
                send_sem=pair_send.at[PARTS + 4 * p + k],
                recv_sem=pair_recv.at[PARTS + 4 * p + k],
                device_id=pair_id,
                device_id_type=MESH,
            ).wait_recv()
        store(1 - core, p)

    def mlp(j):
        columns = slice(j * 512, (j + 1) * 512)
        x = dot(norm2[...], up_weight[:, columns])
        cubic = 0.044715 * (x * x)
        scale = math.sqrt(2.0 / math.pi)
        bend = jnp.tanh(scale * (x * (1.0 + cubic)))
        hidden = (0.5 * x * (1.0 + bend)).astype(bf16)
        slope = 0.5 * (1.0 + bend) + 0.5 * x * (1.0 - bend * bend) * (scale * (1.0 + 3.0 * cubic))
        slope = (slope * back_grad[j]).astype(bf16)
        down_grad = dot(hidden, cot_shifted[...], ((0,), (0,))).astype(bf16)
        up_grad = dot(norm2_t[...], slope).astype(bf16)
        for i in range(2):
            lanes = slice(i * PART_COLS, (i + 1) * PART_COLS)
            grads[0, j, i * 512 : (i + 1) * 512] = up_grad[:, lanes]
            grads[1, j, i * 512 : (i + 1) * 512] = down_grad[:, lanes]
        total[...] += dot(hidden, down_weight[columns])

    def reduce_pair(p):
        pair_copies[p].wait_recv()
        work[p] = (grads[core, p].astype(f32) + pair[p].astype(f32)).astype(bf16)
        scatter(p, 0)

    loads["up"].wait()
    for j in range(PARTS):
        mlp(j)
        give_pair(j, grads.at[1 - core, j], pair.at[j])
        if j > 0:
            reduce_pair(j - 1)
    done = total[...].astype(bf16)
    output[...] = done
    loads["mat5"].wait()
    leave[...] = dot(mat5[...], done).astype(bf16)
    reduce_pair(PARTS - 1)
    copy_back = remote(leave, back, 7, east_id)
    add_up(0, 0)
    add_up(1, 0)
    add_up(2, 0)
    add_up(0, 1)
    add_up(3, 0)
    add_up(1, 1)
    add_up(2, 1)
    gathered(0, 1)
    add_up(3, 1)
    gathered(1, 1)
    gathered(2, 1)
    gathered(3, 1)
    for p in range(PARTS):
        gathered(p, 0)
        if p > 0:
            paired(p - 1)
    paired(PARTS - 1)
    copy_back.wait_recv()
    for copy in (copy_mate, copy_cot, copy_left, copy_up, copy_down, copy_back, *far_copies):
        copy.wait_send()
    for copy in pair_copies:
        copy.wait_send()
    for copy in copies.values():
        copy.wait_send()
    for copy in stores:
        copy.wait()


def main_call(
    pixels,
    ids,
    embed_weight,
    embed_bias,
    latents,
    query_weight,
    key_weight,
    value_weight,
    pool_weight,
    pool_temp,
    first_gain,
    qkv_weight,
    window_temp,
    proj_weight,
    second_gain,
    up_weight,
    down_weight,
    cot,
):
    vmem = pl.BlockSpec(memory_space=pltpu.VMEM)
    smem = pl.BlockSpec(memory_space=pltpu.SMEM)
    anywhere = pl.BlockSpec(memory_space=pl.ANY)
    matrices = [jnp.asarray(matrix, bf16) for matrix in order_matrices()]
    spread = jnp.asarray(spread_matrix(), bf16)
    loaded = (
        embed_weight,
        value_weight,
        pool_weight,
        spread,
        qkv_weight,
        proj_weight,
        up_weight,
        down_weight,
        cot,
        *matrices,
    )
    piece = pltpu.VMEM((HALF, WIDTH), bf16)
    part = pltpu.VMEM((PARTS, PART_ROWS, PART_COLS), bf16)
    return pl.pallas_call(
        main_kernel,
        out_shape=(
            jax.ShapeDtypeStruct((TOKENS, WIDTH), bf16),
            jax.ShapeDtypeStruct((HALF, WIDTH), bf16),
            jax.ShapeDtypeStruct((2, PARTS, PART_ROWS, PART_COLS), bf16),
        ),
        in_specs=[smem] * 3 + [vmem] * 9 + [anywhere] * len(loaded),
        out_specs=(vmem, vmem, anywhere),
        scratch_shapes=[pltpu.VMEM((2, PARTS, PART_ROWS, PART_COLS), bf16)]
        + [pltpu.VMEM(value.shape, bf16) for value in loaded]
        + [
            pltpu.VMEM((SLOTS, WIDTH), f32),
            pltpu.VMEM((4, PER, SPOTS, PIXELS), bf16),
            pltpu.VMEM((3, PER, SPOTS, PIXELS), bf16),
            pltpu.VMEM((PER, 2 * SPOTS, WIDTH), bf16),
            pltpu.VMEM((2 * PER, SPOTS, 128), f32),
            pltpu.VMEM((2 * PER, SPOTS, WIDTH), f32),
            pltpu.VMEM((STAGES, LEVELS, SPOTS, WIDTH), f32),
            piece,
            piece,
            piece,
            piece,
            pltpu.VMEM((2 * TOKENS, WIDTH), bf16),
            pltpu.VMEM((TOKENS, WIDTH), bf16),
            pltpu.VMEM((4, TOKENS, 512), f32),
            pltpu.VMEM((16, HALO, 128), f32),
            pltpu.VMEM((16, HALF, 128), bf16),
            pltpu.VMEM((16, HALF, 256), bf16),
            pltpu.VMEM((4, HALO, HALF), f32),
            pltpu.VMEM((16, HALO, 128), f32),
            pltpu.VMEM((TOKENS, WIDTH), bf16),
            pltpu.VMEM((WIDTH, TOKENS), bf16),
            pltpu.VMEM((TOKENS, WIDTH), f32),
            piece,
            pltpu.VMEM((2, PARTS, PART_ROWS, PART_COLS), bf16),
            part,
            part,
            pltpu.VMEM((PARTS, 3, PART_ROWS // 4, PART_COLS), bf16),
            pltpu.VMEM((PARTS, 15, PART_ROWS // 64, PART_COLS), bf16),
            pltpu.SemaphoreType.DMA((len(loaded),)),
            pltpu.SemaphoreType.DMA((2 * PARTS,)),
            pltpu.SemaphoreType.DMA((12,)),
            pltpu.SemaphoreType.DMA((12,)),
            pltpu.SemaphoreType.DMA((2, PARTS, 18)),
            pltpu.SemaphoreType.DMA((2, PARTS, 18)),
            pltpu.SemaphoreType.DMA((5 * PARTS,)),
            pltpu.SemaphoreType.DMA((5 * PARTS,)),
        ],
        compiler_params=pltpu.CompilerParams(
            collective_id=1, has_side_effects=True, vmem_limit_bytes=60 * 1024 * 1024
        ),
        name="main",
    )(
        ids,
        pool_temp,
        window_temp,
        pixels,
        jnp.asarray(pixel_matrix(), bf16),
        latents,
        query_weight,
        key_weight,
        jnp.asarray(head_rows(), f32),
        first_gain[None, :],
        second_gain[None, :],
        embed_bias,
        *loaded,
    )


def finish_kernel(sums, shifted, back, keep, take, output, up_grad, down_grad):
    scaling = 1.0 / math.sqrt(NTOK)

    @pl.when(pl.program_id(0) == 0)
    def _():
        whole = dot(keep[...], shifted[...]) + dot(take[...], back[...])
        output[...] = whole.reshape(SPOTS, LEVELS, WIDTH).astype(bf16)

    for i in range(2):
        lanes = slice(i * PART_COLS, (i + 1) * PART_COLS)
        rows = slice(i * 512, (i + 1) * 512)
        up_grad[:, lanes] = sums[0, 0, rows].astype(f32) * scaling
        down_grad[:, lanes] = sums[1, 0, rows].astype(f32) * scaling


def finish(sums, shifted, back):
    keep, take = final_matrices()
    fixed = lambda *shape: pl.BlockSpec(shape, lambda p: (0, 0))
    return pl.pallas_call(
        finish_kernel,
        grid=(PARTS,),
        out_shape=(
            jax.ShapeDtypeStruct((SPOTS, LEVELS, WIDTH), bf16),
            jax.ShapeDtypeStruct((WIDTH, FF), f32),
            jax.ShapeDtypeStruct((FF, WIDTH), f32),
        ),
        in_specs=[
            pl.BlockSpec((2, 1, PART_ROWS, PART_COLS), lambda p: (0, p, 0, 0)),
            fixed(TOKENS, WIDTH),
            fixed(HALF, WIDTH),
            fixed(TOKENS, TOKENS),
            fixed(TOKENS, HALF),
        ],
        out_specs=(
            pl.BlockSpec((SPOTS, LEVELS, WIDTH), lambda p: (0, 0, 0)),
            pl.BlockSpec((WIDTH, 512), lambda p: (0, p)),
            pl.BlockSpec((512, WIDTH), lambda p: (p, 0)),
        ),
        compiler_params=pltpu.CompilerParams(vmem_limit_bytes=60 * 1024 * 1024),
        name="finish",
    )(
        sums,
        shifted,
        back,
        jnp.asarray(keep, bf16),
        jnp.asarray(take, bf16),
    )


def per_device(
    pixel_field,
    level_ids,
    embed_weight,
    embed_bias,
    latents,
    query_weight,
    key_weight,
    value_weight,
    pool_weight,
    pool_temp,
    first_gain,
    qkv_weight,
    window_temp,
    proj_weight,
    second_gain,
    up_weight,
    down_weight,
    cotangent,
):
    cot = jnp.transpose(cotangent, (1, 2, 0, 3)).reshape(SPOTS, LEVELS, WIDTH)
    shifted, back, sums = main_call(
        jnp.transpose(pixel_field, (0, 3, 1, 2)),
        level_ids,
        embed_weight,
        embed_bias,
        latents,
        query_weight,
        key_weight,
        value_weight,
        pool_weight,
        pool_temp,
        first_gain,
        qkv_weight,
        window_temp,
        proj_weight,
        second_gain,
        up_weight,
        down_weight,
        cot,
    )
    output, up_grad, down_grad = finish(sums, shifted, back)
    output = output.reshape(ROWS, COLS, LEVELS, WIDTH)
    return (jnp.transpose(output, (2, 0, 1, 3)), up_grad, down_grad)


def solution(mesh):
    placed = (P("enc", None, None, "lon"),) + (P(),) * 16 + (P(None, "enc", "lon", None),)
    return jax.shard_map(
        per_device,
        mesh=mesh,
        in_specs=placed,
        out_specs=(P(None, "enc", "lon", None), P(), P()),
        check_vma=False,
    )
```

```python
import itertools
import math

import jax
import jax.numpy as jnp
import numpy as np
from jax import lax
from jax.experimental import pallas as pl
from jax.experimental.pallas import tpu as pltpu
from jax.sharding import PartitionSpec as P

SLOTS = 52
HEADS = 16
HEAD_WIDTH = 32
WIDTH = 512
FF = 2048
LEVELS = 4
ROWS = 6
COLS = 12
SPOTS = ROWS * COLS
TOKENS = LEVELS * SPOTS
HALF = TOKENS // 2
PIXELS = 100
PER = SLOTS // 4
FAR = 7
EPSILON = 1e-05
NTOK = 36864
PARTS = 4
PART_ROWS = 1024
PART_COLS = 256
HALO = HALF // 2
LEAD = 40
STAGES = 3
PHASES = ((0,), (1, 2))
MESH = pl.DeviceIdType.MESH

f32 = jnp.float32
bf16 = jnp.bfloat16


def dot(a, b, contract=((1,), (0,))):
    return lax.dot_general(a, b, (contract, ((), ())), preferred_element_type=f32)


def normed(values, gain):
    mean = jnp.mean(values, axis=-1, keepdims=True)
    centred = values - mean
    variance = jnp.mean(centred * centred, axis=-1, keepdims=True)
    return (centred * lax.rsqrt(variance + EPSILON) * gain).astype(bf16)


def pooled_at(r, c, l):
    spot = c * ROWS + r
    if spot < LEAD:
        return l * LEAD + spot
    return LEVELS * LEAD + l * (SPOTS - LEAD) + spot - LEAD


def piece_at(r, c, l):
    return (r * (COLS // 2) + c) * LEVELS + l


def natural_at(r, c, l):
    return (r * COLS + c) * LEVELS + l


def shifted_at(r, c, l):
    pair, place = ((1, 0), (0, 0), (0, 1), (1, 1))[l]
    return (r // 3) * HALF + pair * HALO + ((r % 3) * COLS + c) * 2 + place


def matrix_of(rows, cols, entries):
    matrix = np.zeros((rows, cols), np.float32)
    for r in range(ROWS):
        for c in range(COLS // 2):
            for l in range(LEVELS):
                matrix[entries(r, c, l)] = 1.0
    return matrix


def order_matrices():
    half = COLS // 2
    return (
        matrix_of(HALF, LEVELS * LEAD, lambda r, c, l: (piece_at(r, c, l), pooled_at(r, c, l))),
        matrix_of(TOKENS, TOKENS, lambda r, c, l: (shifted_at(r, c, l), pooled_at(r, half + c, l))),
        matrix_of(HALF, TOKENS, lambda r, c, l: (piece_at(r, c, l), natural_at(r, c, l))),
        matrix_of(TOKENS, TOKENS, lambda r, c, l: (shifted_at(r, c, l), natural_at(r, half + c, l))),
        matrix_of(TOKENS, HALF, lambda r, c, l: (shifted_at(r, half + c, l), piece_at(r, c, l))),
        matrix_of(HALF, TOKENS, lambda r, c, l: (piece_at(r, c, l), shifted_at(r, half + c, l))),
    )


def final_matrices():
    half = COLS // 2
    return (
        matrix_of(TOKENS, TOKENS, lambda r, c, l: (natural_at(r, half + c, l), shifted_at(r, c, l))),
        matrix_of(TOKENS, HALF, lambda r, c, l: (natural_at(r, c, l), piece_at(r, c, l))),
    )


def pixel_matrix():
    matrix = np.zeros((4 * SPOTS, 4 * SPOTS), np.float32)
    for owner in range(4):
        for c in range(COLS):
            for r in range(ROWS):
                matrix[owner * SPOTS + c * ROWS + r, c * 4 * ROWS + owner * ROWS + r] = 1.0
    return matrix


def head_rows():
    mask = np.zeros((HEADS, WIDTH), np.float32)
    for h in range(HEADS):
        mask[h, h * HEAD_WIDTH : (h + 1) * HEAD_WIDTH] = 1.0
    return mask


def spread_matrix():
    one = np.zeros((LEVELS * HEADS, LEVELS * WIDTH), np.float32)
    for l in range(LEVELS):
        for h in range(HEADS):
            at = l * WIDTH + h * HEAD_WIDTH
            one[l * HEADS + h, at : at + HEAD_WIDTH] = 1.0
    return np.concatenate([one, one], axis=0)


def mesh_id(x, y, z, core):
    return (lax.rem(y, 2) * 2 + core, x * 8 + z * 2 + y // 2)


def split_parts(values):
    first = lax.broadcasted_iota(jnp.int32, values.shape, 1) < 64
    high = values.astype(bf16).astype(f32)
    return jnp.where(first, high, values - high).astype(bf16)


def main_kernel(
    ids,
    pool_temp,
    window_temp,
    pixels,
    pixel_order,
    latents,
    heads,
    first_gain,
    second_gain,
    embed_bias,
    query_hbm,
    key_hbm,
    embed_hbm,
    value_hbm,
    pool_hbm,
    spread_hbm,
    qkv_hbm,
    proj_hbm,
    up_hbm,
    down_hbm,
    cot_hbm,
    mat0_hbm,
    mat1_hbm,
    mat2_hbm,
    mat3_hbm,
    mat4_hbm,
    mat5_hbm,
    output,
    back,
    whole,
    result,
    query_weight,
    key_weight,
    embed_weight,
    value_weight,
    pool_weight,
    spread,
    qkv_weight,
    proj_weight,
    up_weight,
    down_weight,
    cotangent,
    mat0,
    mat1,
    mat2,
    mat3,
    mat4,
    mat5,
    bias,
    outgoing,
    arrived,
    tokens,
    scores,
    values,
    sums,
    own_cot,
    cot_left,
    cot_east,
    left,
    east,
    wide,
    cot_shifted,
    back_grad,
    qs,
    ks,
    vs,
    masks,
    attended,
    norm2,
    norm2_t,
    total,
    leave,
    grads,
    pair,
    work,
    got1,
    got2,
    load_sem,
    store_sem,
    send,
    recv,
    ring_send,
    ring_recv,
    pair_send,
    pair_recv,
):
    enc = lax.axis_index("enc")
    lon = lax.axis_index("lon")
    mate = enc + 1 - 2 * lax.rem(enc, 2)
    peers = (mate, lax.rem(enc + 2, 4), lax.rem(mate + 2, 4))
    west_id = (enc, lax.rem(lon + 31, 32))
    east_id = (enc, lax.rem(lon + 1, 32))
    core = lax.rem(enc, 2)
    x_at = lon // 8
    y_at = lax.rem(lon, 2) * 2 + enc // 2
    z_at = lax.rem(lon // 2, 4)

    places = [[lax.rem(at + by, 4) for by in range(4)] for at in (x_at, y_at, z_at)]
    x_part = [place * 8 for place in places[0]]
    y_part = [place // 2 for place in places[1]]
    z_part = [place * 2 for place in places[2]]
    enc_part = [lax.rem(place, 2) * 2 + core for place in places[1]]

    def device_at(step):
        return enc_part[step[1]], x_part[step[0]] + y_part[step[1]] + z_part[step[2]]

    def by_core(first, second):
        return first + core * (second - first)

    def step_of(part, way, phase, by):
        step = [0, 0, 0]
        for dim, count in zip(phase, by):
            step[(part + way + dim) % 3] = count
        return tuple(step)

    def chunk_for(part, way, phase, by):
        chunk = 0
        for dim, count in zip(phase, by):
            chunk = chunk * 4 + places[(part + way + dim) % 3][count % 4]
        return chunk

    def chunk_at(part, phase, by):
        return by_core(*[chunk_for(part, way, phase, by) for way in range(2)])

    combos = [
        [by for by in itertools.product(range(4), repeat=len(phase)) if any(by)]
        for phase in PHASES
    ]
    others = sorted(
        {
            step_of(turn, 0, phase, by)
            for turn in range(3)
            for phase, bys in zip(PHASES, combos)
            for by in bys
        }
    )
    devices = {step: device_at(step) for step in others}

    def device_for(part, phase, by):
        near, far = [devices[step_of(part, way, phase, by)] for way in range(2)]
        return by_core(near[0], far[0]), by_core(near[1], far[1])

    barrier = pltpu.get_barrier_semaphore()
    for peer in peers:
        pl.semaphore_signal(barrier, inc=1, device_id=(peer, lon), device_id_type=MESH)
    for other in (west_id, east_id):
        pl.semaphore_signal(barrier, inc=1, device_id=other, device_id_type=MESH)
    for step in others:
        pl.semaphore_signal(barrier, inc=1, device_id=devices[step], device_id_type=MESH)

    loads = {}
    for index, (name, source, target) in enumerate(
        (
            ("query", query_hbm, query_weight),
            ("key", key_hbm, key_weight),
            ("cot", cot_hbm, cotangent),
            ("mat2", mat2_hbm, mat2),
            ("embed", embed_hbm, embed_weight),
            ("value", value_hbm, value_weight),
            ("spread", spread_hbm, spread),
            ("pool", pool_hbm, pool_weight),
            ("mat0", mat0_hbm, mat0),
            ("mat1", mat1_hbm, mat1),
            ("mat3", mat3_hbm, mat3),
            ("mat4", mat4_hbm, mat4),
            ("mat5", mat5_hbm, mat5),
            ("down", down_hbm, down_weight),
            ("qkv", qkv_hbm, qkv_weight),
            ("proj", proj_hbm, proj_weight),
            ("up", up_hbm, up_weight),
        )
    ):
        loads[name] = pltpu.make_async_copy(source, target, load_sem.at[index])
        loads[name].start()

    def remote(source, target, index, device):
        copy = pltpu.make_async_remote_copy(
            src_ref=source,
            dst_ref=target,
            send_sem=send.at[index],
            recv_sem=recv.at[index],
            device_id=device,
            device_id_type=MESH,
        )
        copy.start()
        return copy

    def sort_pixels(slot, _):
        block = pixels[slot].astype(f32).reshape(4 * SPOTS, PIXELS).astype(bf16)
        block = dot(pixel_order[...], block).astype(bf16).astype(f32)
        for owner in range(4):
            outgoing[owner, slot] = block[owner * SPOTS : (owner + 1) * SPOTS].astype(bf16)
        return 0

    far_copies = []

    def send_far(k, first, count):
        slots_there = pl.ds(first, count)
        for i in (1, 2):
            far_copies.append(
                remote(
                    outgoing.at[peers[i], slots_there],
                    arrived.at[i, slots_there],
                    7 + 2 * k + i,
                    (peers[i], lon),
                )
            )

    lax.fori_loop(0, FAR, sort_pixels, 0, unroll=True)
    pl.semaphore_wait(barrier, 5 + len(others))
    send_far(0, 0, FAR)
    lax.fori_loop(FAR, PER, sort_pixels, 0, unroll=True)
    copy_mate = remote(outgoing.at[peers[0]], arrived.at[0], 0, (peers[0], lon))
    send_far(1, FAR, PER - FAR)

    bias[...] = embed_bias[...].astype(f32)
    loads["query"].wait()
    loads["key"].wait()
    queries = dot(latents[...], query_weight[...]).astype(bf16).astype(f32)
    blocks = [queries[l : l + 1] * heads[...] for l in range(LEVELS)]
    blocks = jnp.concatenate(blocks, axis=0).astype(bf16)
    head_of = lax.rem(lax.broadcasted_iota(jnp.int32, (LEVELS * HEADS, 1), 0), HEADS)
    temp = jnp.zeros((LEVELS * HEADS, 1), f32)
    for h in range(HEADS):
        temp = jnp.where(head_of == h, pool_temp[h] * (1.0 / math.sqrt(HEAD_WIDTH)), temp)
    folded = dot(blocks, key_weight[...], ((1,), (1,))) * temp
    high = folded.astype(bf16)
    low = (folded - high.astype(f32)).astype(bf16)
    keys = jnp.concatenate([high, high, low, low], axis=0)

    def token_of(block, slot):
        level = ids[slot]
        return dot(block, embed_weight[level]) + bias[pl.ds(level, 1), :]

    def embed_near(i, _):
        near = token_of(outgoing[enc, i], enc * PER + i)
        far = token_of(arrived[0, i], mate * PER + i)
        tokens[i] = jnp.concatenate([near, far], axis=0).astype(bf16)
        return 0

    def embed_far(first):
        def embed(i, _):
            near = token_of(arrived[1, first + i], peers[1] * PER + first + i)
            far = token_of(arrived[2, first + i], peers[2] * PER + first + i)
            tokens[i] = jnp.concatenate([near, far], axis=0).astype(bf16)
            return 0

        return embed

    def project(first, count):
        block = jnp.concatenate([tokens[first + i] for i in range(count)], axis=0)
        projected = dot(block, value_weight[...])
        scored = dot(block, keys, ((1,), (1,)))
        scored = scored[:, :128] + scored[:, 128:]
        for i in range(2 * count):
            values[first * 2 + i] = projected[i * SPOTS : (i + 1) * SPOTS]
            scores[first * 2 + i] = scored[i * SPOTS : (i + 1) * SPOTS]

    def project_two(i, _):
        project(2 * i, 2)
        return 0

    def mix(stage, first, count, lo, hi):
        probs = jnp.concatenate([scores[first + i, lo:hi] for i in range(count)], axis=0)
        split = split_parts(probs)
        size = hi - lo
        for l in range(LEVELS):
            wider = dot(split, spread[:, l * WIDTH : (l + 1) * WIDTH])
            part = sums[stage, l, lo:hi]
            for i in range(count):
                part = part + wider[i * size : (i + 1) * size] * values[first + i, lo:hi]
            sums[stage, l, lo:hi] = part

    def mix_all(stage, pairs, lo, hi):
        def mix_four(i, _):
            mix(stage, 4 * i, 4, lo, hi)
            return 0

        lax.fori_loop(0, pairs // 2, mix_four, 0, unroll=True)
        if pairs % 2:
            mix(stage, 2 * pairs - 2, 2, lo, hi)

    def pool_stage(stage, pairs, embed):
        lax.fori_loop(0, pairs, embed, 0, unroll=True)
        if stage == 0:
            loads["value"].wait()
        lax.fori_loop(0, pairs // 2, project_two, 0, unroll=True)
        if pairs % 2:
            project(pairs - 1, 1)
        peak = scores[0]
        for s in range(1, 2 * pairs):
            peak = jnp.maximum(peak, scores[s])
        weight = jnp.zeros_like(peak)
        for s in range(2 * pairs):
            exponent = jnp.exp(scores[s] - peak)
            scores[s] = exponent
            weight = weight + exponent
        sums[stage] = jnp.zeros((LEVELS, SPOTS, WIDTH), f32)
        return peak, weight

    loads["cot"].wait()
    loads["mat2"].wait()
    own_cot[...] = cotangent[...].astype(f32).reshape(TOKENS, WIDTH).astype(bf16)
    cot_left[...] = dot(mat2[...], own_cot[...]).astype(bf16)
    loads["embed"].wait()
    copy_mate.wait_recv()
    stats = [pool_stage(0, PER, embed_near)]
    loads["spread"].wait()
    mix_all(0, PER, 0, SPOTS)
    far_copies[0].wait_recv()
    far_copies[1].wait_recv()
    stats.append(pool_stage(1, FAR, embed_far(0)))
    mix_all(1, FAR, 0, SPOTS)
    far_copies[2].wait_recv()
    far_copies[3].wait_recv()
    copy_cot = remote(cot_left, cot_east, 3, west_id)
    stats.append(pool_stage(2, PER - FAR, embed_far(FAR)))

    peak = stats[0][0]
    for other, _ in stats[1:]:
        peak = jnp.maximum(peak, other)
    decays = [jnp.exp(top - peak) for top, _ in stats]
    inverse = 1.0 / sum(weight * decay for decay, (_, weight) in zip(decays, stats))
    decays = [decay * inverse for decay in decays]
    loads["pool"].wait()

    def finish_pool(lo, hi):
        shares = split_parts(jnp.concatenate([decay[lo:hi] for decay in decays], axis=0))
        size = hi - lo
        pooled = []
        for l in range(LEVELS):
            share = dot(shares, spread[:, l * WIDTH : (l + 1) * WIDTH])
            level = share[:size] * sums[0, l, lo:hi]
            for k in range(1, STAGES):
                level = level + share[k * size : (k + 1) * size] * sums[k, l, lo:hi]
            pooled.append(level)
        projected = dot(jnp.concatenate(pooled, axis=0).astype(bf16), pool_weight[...])
        rows = [
            projected[l * size : (l + 1) * size] + latents[l : l + 1].astype(f32)
            for l in range(LEVELS)
        ]
        return jnp.concatenate(rows, axis=0).astype(bf16)

    mix_all(2, PER - FAR, 0, LEAD)
    lead = finish_pool(0, LEAD)
    loads["mat0"].wait()
    left[...] = dot(mat0[...], lead).astype(bf16)
    copy_left = remote(left, east, 4, west_id)
    mix_all(2, PER - FAR, LEAD, SPOTS)
    stream = jnp.concatenate([lead, finish_pool(LEAD, SPOTS)], axis=0)
    loads["mat1"].wait()
    kept = dot(mat1[...], stream)
    copy_cot.wait_recv()
    loads["mat3"].wait()
    loads["mat4"].wait()
    cot = (dot(mat3[...], own_cot[...]) + dot(mat4[...], cot_east[...])).astype(bf16)
    cot_shifted[...] = cot
    loads["down"].wait()
    for j in range(4):
        back_grad[j] = dot(cot, down_weight[j * 512 : (j + 1) * 512], ((1,), (1,)))
    copy_left.wait_recv()
    own = (kept + dot(mat4[...], east[...])).astype(bf16)
    wide[HALF : HALF + TOKENS] = own
    copy_up = remote(
        wide.at[pl.ds(HALF, HALF)],
        wide.at[pl.ds(HALF + TOKENS, HALF)],
        5,
        (lax.rem(enc + 3, 4), lon),
    )
    copy_down = remote(
        wide.at[pl.ds(TOKENS, HALF)], wide.at[pl.ds(0, HALF)], 6, (lax.rem(enc + 1, 4), lon)
    )

    loads["qkv"].wait()
    norm = normed(own.astype(f32), first_gain[...])
    own_q = dot(norm, qkv_weight[:, :WIDTH])
    own_k = dot(norm, qkv_weight[:, WIDTH : 2 * WIDTH])
    own_v = dot(norm, qkv_weight[:, 2 * WIDTH :])
    row = lax.broadcasted_iota(jnp.int32, (HALO, HALF), 0)
    col = lax.broadcasted_iota(jnp.int32, (HALO, HALF), 1)
    same = lax.rem(row, 2) == lax.rem(col, 2)
    first_key = jnp.where(enc == 0, HALO, 0)
    last_key = jnp.where(enc == 3, HALO, HALF)
    ones = jnp.ones((HALF, 128), f32)
    for win in range(2):
        inside = (col >= first_key) if win == 0 else (col < last_key)
        masks[win * 2] = jnp.where(inside, 0.0, -1e30)
        masks[win * 2 + 1] = jnp.where(inside & same, 0.0, -1e30)
    copy_up.wait_recv()
    copy_down.wait_recv()
    halo = jnp.concatenate([wide[:HALF], wide[HALF + TOKENS :]], axis=0).astype(f32)
    norm = normed(halo, first_gain[...])
    halo_k = dot(norm, qkv_weight[:, WIDTH : 2 * WIDTH])
    halo_v = dot(norm, qkv_weight[:, 2 * WIDTH :])
    for win in range(2):
        for two in range(2):
            at = win * HALF + two * HALO
            rows = slice(at, at + HALO)
            for g in range(4):
                lanes = slice(g * 128, (g + 1) * 128)
                index = (win * 2 + two) * 4 + g
                qs[index] = own_q[rows, lanes]
                key = (halo_k[rows, lanes], own_k[rows, lanes])
                value = (halo_v[rows, lanes], own_v[rows, lanes])
                if win == 1:
                    key, value = key[::-1], value[::-1]
                ks[index] = jnp.concatenate(key, axis=0).astype(bf16)
                value = jnp.concatenate(value, axis=0)
                vs[index] = jnp.concatenate([value, ones], axis=1).astype(bf16)

    lane = lax.broadcasted_iota(jnp.int32, (HALO, 128), 1) // HEAD_WIDTH

    def attend(index, _):
        group = lax.rem(index, 4)
        query = qs[index]
        mask = masks[index // 4]
        stacked = [jnp.where(lane == h, query, 0.0) for h in range(4)]
        raw = dot(jnp.concatenate(stacked, axis=0).astype(bf16), ks[index], ((1,), (1,)))
        exponents = []
        for h in range(4):
            masked = raw[h * HALO : (h + 1) * HALO] + mask
            top = jnp.max(masked, axis=-1, keepdims=True)
            factor = window_temp[group * 4 + h] * (1.0 / math.sqrt(HEAD_WIDTH))
            exponents.append(jnp.exp((masked - top) * factor).astype(bf16).astype(f32))
        exponent = jnp.concatenate(exponents, axis=0).astype(bf16)
        mixed = dot(exponent, vs[index])
        above = mixed[:HALO, :128]
        under = mixed[:HALO, 128:]
        for h in range(1, 4):
            rows = slice(h * HALO, (h + 1) * HALO)
            above = jnp.where(lane == h, mixed[rows, :128], above)
            under = jnp.where(lane == h, mixed[rows, 128:], under)
        attended[index] = above / under
        return 0

    lax.fori_loop(0, 16, attend, 0, unroll=True)

    rows = [
        jnp.concatenate([attended[block * 4 + g] for g in range(4)], axis=1) for block in range(4)
    ]
    loads["proj"].wait()
    mixed = dot(jnp.concatenate(rows, axis=0).astype(bf16), proj_weight[...])
    middle = (own.astype(f32) + mixed).astype(bf16).astype(f32)
    norm = normed(middle, second_gain[...])
    norm2[...] = norm
    norm2_t[...] = norm.T
    total[...] = middle

    got = (got1, got2)
    sizes = [PART_ROWS // 4, PART_ROWS // 64]
    offsets = [0, len(combos[0])]
    starts = []
    for p in range(PARTS):
        at = [0]
        for phase in range(len(PHASES)):
            at.append(at[-1] + chunk_at(p, PHASES[phase], (0, 0)) * sizes[phase])
        starts.append(at)
    pair_id = (mate, lon)
    pair_copies = []
    stores = []
    copies = {}

    def give_pair(index, source, target):
        copy = pltpu.make_async_remote_copy(
            src_ref=source,
            dst_ref=target,
            send_sem=pair_send.at[index],
            recv_sem=pair_recv.at[index],
            device_id=pair_id,
            device_id_type=MESH,
        )
        copy.start()
        pair_copies.append(copy)
        return copy

    def ring_copy(way, p, phase, k, source, target):
        at = offsets[phase] + k
        return pltpu.make_async_remote_copy(
            src_ref=source,
            dst_ref=target,
            send_sem=ring_send.at[way, p, at],
            recv_sem=ring_recv.at[way, p, at],
            device_id=device_for(p, PHASES[phase], combos[phase][k]),
            device_id_type=MESH,
        )

    def scatter(p, phase):
        size = sizes[phase]
        for k, by in enumerate(combos[phase]):
            target = chunk_at(p, PHASES[phase], by)
            first = pl.multiple_of(starts[p][phase] + target * size, 16)
            source = work.at[p, pl.ds(first, size)]
            copy = ring_copy(0, p, phase, k, source, got[phase].at[p, k])
            copy.start()
            copies[0, p, phase, k] = copy

    def add_up(p, phase):
        for k in range(len(combos[phase])):
            copies[0, p, phase, k].wait_recv()
        size = sizes[phase]
        first = pl.multiple_of(starts[p][phase + 1], 16)
        held = work[p, pl.ds(first, size), :].astype(f32)
        for k in range(len(combos[phase])):
            held = held + got[phase][p, k].astype(f32)
        if phase == 0:
            work[p, pl.ds(first, size), :] = held.astype(bf16)
            scatter(p, 1)
        else:
            result[core, p, pl.ds(first, size), :] = held.astype(bf16)
            gather(p, 1)

    def gather(p, phase):
        first = pl.multiple_of(starts[p][phase + 1], 16)
        piece = result.at[core, p, pl.ds(first, sizes[phase])]
        for k in range(len(combos[phase])):
            copy = ring_copy(1, p, phase, k, piece, piece)
            copy.start()
            copies[1, p, phase, k] = copy

    def gathered(p, phase):
        for k, by in enumerate(combos[phase]):
            source = chunk_at(p, PHASES[phase], [4 - step for step in by])
            first = pl.multiple_of(starts[p][phase] + source * sizes[phase], 16)
            piece = result.at[core, p, pl.ds(first, sizes[phase])]
            ring_copy(1, p, phase, k, piece, piece).wait_recv()
            if phase == 0:
                give_pair(PARTS + 4 * p + 1 + k, piece, piece)
        if phase == 1:
            gather(p, 0)
            first = pl.multiple_of(starts[p][1], 16)
            piece = result.at[core, p, pl.ds(first, sizes[0])]
            give_pair(PARTS + 4 * p, piece, piece)
        else:
            store(core, p)

    def store(half, p):
        copy = pltpu.make_async_copy(result.at[half, p], whole.at[half, p], store_sem.at[len(stores)])
        copy.start()
        stores.append(copy)

    def paired(p):
        for k in range(4):
            piece = result.at[1 - core, p, pl.ds(0, sizes[0])]
            pltpu.make_async_remote_copy(
                src_ref=piece,
                dst_ref=piece,
                send_sem=pair_send.at[PARTS + 4 * p + k],
                recv_sem=pair_recv.at[PARTS + 4 * p + k],
                device_id=pair_id,
                device_id_type=MESH,
            ).wait_recv()
        store(1 - core, p)

    def mlp(j):
        columns = slice(j * 512, (j + 1) * 512)
        x = dot(norm2[...], up_weight[:, columns])
        cubic = 0.044715 * (x * x)
        scale = math.sqrt(2.0 / math.pi)
        bend = jnp.tanh(scale * (x * (1.0 + cubic)))
        hidden = (0.5 * x * (1.0 + bend)).astype(bf16)
        slope = 0.5 * (1.0 + bend) + 0.5 * x * (1.0 - bend * bend) * (scale * (1.0 + 3.0 * cubic))
        slope = (slope * back_grad[j]).astype(bf16)
        down_grad = dot(hidden, cot_shifted[...], ((0,), (0,))).astype(bf16)
        up_grad = dot(norm2_t[...], slope).astype(bf16)
        for i in range(2):
            lanes = slice(i * PART_COLS, (i + 1) * PART_COLS)
            grads[0, j, i * 512 : (i + 1) * 512] = up_grad[:, lanes]
            grads[1, j, i * 512 : (i + 1) * 512] = down_grad[:, lanes]
        total[...] += dot(hidden, down_weight[columns])

    def reduce_pair(p):
        pair_copies[p].wait_recv()
        work[p] = (grads[core, p].astype(f32) + pair[p].astype(f32)).astype(bf16)
        scatter(p, 0)

    loads["up"].wait()
    for j in range(PARTS):
        mlp(j)
        give_pair(j, grads.at[1 - core, j], pair.at[j])
        if j > 0:
            reduce_pair(j - 1)
    done = total[...].astype(bf16)
    output[...] = done
    loads["mat5"].wait()
    leave[...] = dot(mat5[...], done).astype(bf16)
    reduce_pair(PARTS - 1)
    copy_back = remote(leave, back, 7, east_id)
    add_up(0, 0)
    add_up(1, 0)
    add_up(2, 0)
    add_up(0, 1)
    add_up(3, 0)
    add_up(1, 1)
    add_up(2, 1)
    gathered(0, 1)
    add_up(3, 1)
    gathered(1, 1)
    gathered(2, 1)
    gathered(3, 1)
    for p in range(PARTS):
        gathered(p, 0)
        if p > 0:
            paired(p - 1)
    paired(PARTS - 1)
    copy_back.wait_recv()
    for copy in (copy_mate, copy_cot, copy_left, copy_up, copy_down, copy_back, *far_copies):
        copy.wait_send()
    for copy in pair_copies:
        copy.wait_send()
    for copy in copies.values():
        copy.wait_send()
    for copy in stores:
        copy.wait()


def main_call(
    pixels,
    ids,
    embed_weight,
    embed_bias,
    latents,
    query_weight,
    key_weight,
    value_weight,
    pool_weight,
    pool_temp,
    first_gain,
    qkv_weight,
    window_temp,
    proj_weight,
    second_gain,
    up_weight,
    down_weight,
    cot,
):
    vmem = pl.BlockSpec(memory_space=pltpu.VMEM)
    smem = pl.BlockSpec(memory_space=pltpu.SMEM)
    anywhere = pl.BlockSpec(memory_space=pl.ANY)
    matrices = [jnp.asarray(matrix, bf16) for matrix in order_matrices()]
    spread = jnp.asarray(spread_matrix(), bf16)
    loaded = (
        query_weight,
        key_weight,
        embed_weight,
        value_weight,
        pool_weight,
        spread,
        qkv_weight,
        proj_weight,
        up_weight,
        down_weight,
        cot,
        *matrices,
    )
    piece = pltpu.VMEM((HALF, WIDTH), bf16)
    part = pltpu.VMEM((PARTS, PART_ROWS, PART_COLS), bf16)
    return pl.pallas_call(
        main_kernel,
        out_shape=(
            jax.ShapeDtypeStruct((TOKENS, WIDTH), bf16),
            jax.ShapeDtypeStruct((HALF, WIDTH), bf16),
            jax.ShapeDtypeStruct((2, PARTS, PART_ROWS, PART_COLS), bf16),
        ),
        in_specs=[smem] * 3 + [vmem] * 7 + [anywhere] * len(loaded),
        out_specs=(vmem, vmem, anywhere),
        scratch_shapes=[pltpu.VMEM((2, PARTS, PART_ROWS, PART_COLS), bf16)]
        + [pltpu.VMEM(value.shape, bf16) for value in loaded]
        + [
            pltpu.VMEM((SLOTS, WIDTH), f32),
            pltpu.VMEM((4, PER, SPOTS, PIXELS), bf16),
            pltpu.VMEM((3, PER, SPOTS, PIXELS), bf16),
            pltpu.VMEM((PER, 2 * SPOTS, WIDTH), bf16),
            pltpu.VMEM((2 * PER, SPOTS, 128), f32),
            pltpu.VMEM((2 * PER, SPOTS, WIDTH), f32),
            pltpu.VMEM((STAGES, LEVELS, SPOTS, WIDTH), f32),
            pltpu.VMEM((TOKENS, WIDTH), bf16),
            piece,
            piece,
            piece,
            piece,
            pltpu.VMEM((2 * TOKENS, WIDTH), bf16),
            pltpu.VMEM((TOKENS, WIDTH), bf16),
            pltpu.VMEM((4, TOKENS, 512), f32),
            pltpu.VMEM((16, HALO, 128), f32),
            pltpu.VMEM((16, HALF, 128), bf16),
            pltpu.VMEM((16, HALF, 256), bf16),
            pltpu.VMEM((4, HALO, HALF), f32),
            pltpu.VMEM((16, HALO, 128), f32),
            pltpu.VMEM((TOKENS, WIDTH), bf16),
            pltpu.VMEM((WIDTH, TOKENS), bf16),
            pltpu.VMEM((TOKENS, WIDTH), f32),
            piece,
            pltpu.VMEM((2, PARTS, PART_ROWS, PART_COLS), bf16),
            part,
            part,
            pltpu.VMEM((PARTS, 3, PART_ROWS // 4, PART_COLS), bf16),
            pltpu.VMEM((PARTS, 15, PART_ROWS // 64, PART_COLS), bf16),
            pltpu.SemaphoreType.DMA((len(loaded),)),
            pltpu.SemaphoreType.DMA((2 * PARTS,)),
            pltpu.SemaphoreType.DMA((12,)),
            pltpu.SemaphoreType.DMA((12,)),
            pltpu.SemaphoreType.DMA((2, PARTS, 18)),
            pltpu.SemaphoreType.DMA((2, PARTS, 18)),
            pltpu.SemaphoreType.DMA((5 * PARTS,)),
            pltpu.SemaphoreType.DMA((5 * PARTS,)),
        ],
        compiler_params=pltpu.CompilerParams(
            collective_id=1, has_side_effects=True, vmem_limit_bytes=60 * 1024 * 1024
        ),
        name="main",
    )(
        ids,
        pool_temp,
        window_temp,
        pixels,
        jnp.asarray(pixel_matrix(), bf16),
        latents,
        jnp.asarray(head_rows(), f32),
        first_gain[None, :],
        second_gain[None, :],
        embed_bias,
        *loaded,
    )


def finish_kernel(sums, shifted, back, keep, take, output, up_grad, down_grad):
    scaling = 1.0 / math.sqrt(NTOK)

    @pl.when(pl.program_id(0) == 0)
    def _():
        whole = dot(keep[...], shifted[...]) + dot(take[...], back[...])
        output[...] = whole.reshape(SPOTS, LEVELS, WIDTH).astype(bf16)

    up_grad[...] = sums[0, 0].astype(f32) * scaling
    down_grad[...] = sums[1, 0].astype(f32) * scaling


def finish(sums, shifted, back):
    keep, take = final_matrices()
    fixed = lambda *shape: pl.BlockSpec(shape, lambda p: (0, 0))
    return pl.pallas_call(
        finish_kernel,
        grid=(2 * PARTS,),
        out_shape=(
            jax.ShapeDtypeStruct((SPOTS, LEVELS, WIDTH), bf16),
            jax.ShapeDtypeStruct((WIDTH, FF), f32),
            jax.ShapeDtypeStruct((FF, WIDTH), f32),
        ),
        in_specs=[
            pl.BlockSpec((2, 1, PART_ROWS // 2, PART_COLS), lambda p: (0, p // 2, p % 2, 0)),
            fixed(TOKENS, WIDTH),
            fixed(HALF, WIDTH),
            fixed(TOKENS, TOKENS),
            fixed(TOKENS, HALF),
        ],
        out_specs=(
            pl.BlockSpec((SPOTS, LEVELS, WIDTH), lambda p: (0, 0, 0)),
            pl.BlockSpec((WIDTH, PART_COLS), lambda p: (0, p)),
            pl.BlockSpec((512, PART_COLS), lambda p: (p // 2, p % 2)),
        ),
        compiler_params=pltpu.CompilerParams(vmem_limit_bytes=60 * 1024 * 1024),
        name="finish",
    )(
        sums,
        shifted,
        back,
        jnp.asarray(keep, bf16),
        jnp.asarray(take, bf16),
    )


def per_device(
    pixel_field,
    level_ids,
    embed_weight,
    embed_bias,
    latents,
    query_weight,
    key_weight,
    value_weight,
    pool_weight,
    pool_temp,
    first_gain,
    qkv_weight,
    window_temp,
    proj_weight,
    second_gain,
    up_weight,
    down_weight,
    cotangent,
):
    cot = jnp.transpose(cotangent, (1, 2, 0, 3)).reshape(SPOTS, LEVELS, WIDTH)
    shifted, back, sums = main_call(
        jnp.transpose(pixel_field, (0, 3, 1, 2)),
        level_ids,
        embed_weight,
        embed_bias,
        latents,
        query_weight,
        key_weight,
        value_weight,
        pool_weight,
        pool_temp,
        first_gain,
        qkv_weight,
        window_temp,
        proj_weight,
        second_gain,
        up_weight,
        down_weight,
        cot,
    )
    output, up_grad, down_grad = finish(sums, shifted, back)
    output = output.reshape(ROWS, COLS, LEVELS, WIDTH)
    return (jnp.transpose(output, (2, 0, 1, 3)), up_grad, down_grad)


def solution(mesh):
    placed = (P("enc", None, None, "lon"),) + (P(),) * 16 + (P(None, "enc", "lon", None),)
    return jax.shard_map(
        per_device,
        mesh=mesh,
        in_specs=placed,
        out_specs=(P(None, "enc", "lon", None), P(), P()),
        check_vma=False,
    )
```

```python
import itertools
import math

import jax
import jax.numpy as jnp
import numpy as np
from jax import lax
from jax.experimental import pallas as pl
from jax.experimental.pallas import tpu as pltpu
from jax.sharding import PartitionSpec as P

SLOTS = 52
HEADS = 16
HEAD_WIDTH = 32
WIDTH = 512
FF = 2048
LEVELS = 4
ROWS = 6
COLS = 12
SPOTS = ROWS * COLS
TOKENS = LEVELS * SPOTS
HALF = TOKENS // 2
PIXELS = 100
PER = SLOTS // 4
FAR = 7
EPSILON = 1e-05
NTOK = 36864
PARTS = 4
PART_ROWS = 1024
PART_COLS = 256
HALO = HALF // 2
LEAD = 40
STAGES = 3
PHASES = ((0,), (1, 2))
MESH = pl.DeviceIdType.MESH

f32 = jnp.float32
bf16 = jnp.bfloat16


def dot(a, b, contract=((1,), (0,))):
    return lax.dot_general(a, b, (contract, ((), ())), preferred_element_type=f32)


def normed(values, gain):
    mean = jnp.mean(values, axis=-1, keepdims=True)
    centred = values - mean
    variance = jnp.mean(centred * centred, axis=-1, keepdims=True)
    return (centred * lax.rsqrt(variance + EPSILON) * gain).astype(bf16)


def pooled_at(r, c, l):
    spot = c * ROWS + r
    if spot < LEAD:
        return l * LEAD + spot
    return LEVELS * LEAD + l * (SPOTS - LEAD) + spot - LEAD


def piece_at(r, c, l):
    return (r * (COLS // 2) + c) * LEVELS + l


def natural_at(r, c, l):
    return (r * COLS + c) * LEVELS + l


def shifted_at(r, c, l):
    pair, place = ((1, 0), (0, 0), (0, 1), (1, 1))[l]
    return (r // 3) * HALF + pair * HALO + ((r % 3) * COLS + c) * 2 + place


def matrix_of(rows, cols, entries):
    matrix = np.zeros((rows, cols), np.float32)
    for r in range(ROWS):
        for c in range(COLS // 2):
            for l in range(LEVELS):
                matrix[entries(r, c, l)] = 1.0
    return matrix


def order_matrices():
    half = COLS // 2
    return (
        matrix_of(HALF, LEVELS * LEAD, lambda r, c, l: (piece_at(r, c, l), pooled_at(r, c, l))),
        matrix_of(TOKENS, TOKENS, lambda r, c, l: (shifted_at(r, c, l), pooled_at(r, half + c, l))),
        matrix_of(HALF, TOKENS, lambda r, c, l: (piece_at(r, c, l), natural_at(r, c, l))),
        matrix_of(TOKENS, TOKENS, lambda r, c, l: (shifted_at(r, c, l), natural_at(r, half + c, l))),
        matrix_of(TOKENS, HALF, lambda r, c, l: (shifted_at(r, half + c, l), piece_at(r, c, l))),
        matrix_of(HALF, TOKENS, lambda r, c, l: (piece_at(r, c, l), shifted_at(r, half + c, l))),
    )


def final_matrices():
    half = COLS // 2
    return (
        matrix_of(TOKENS, TOKENS, lambda r, c, l: (natural_at(r, half + c, l), shifted_at(r, c, l))),
        matrix_of(TOKENS, HALF, lambda r, c, l: (natural_at(r, c, l), piece_at(r, c, l))),
    )


def pixel_matrix():
    matrix = np.zeros((4 * SPOTS, 4 * SPOTS), np.float32)
    for owner in range(4):
        for c in range(COLS):
            for r in range(ROWS):
                matrix[owner * SPOTS + c * ROWS + r, c * 4 * ROWS + owner * ROWS + r] = 1.0
    return matrix


def head_rows():
    mask = np.zeros((HEADS, WIDTH), np.float32)
    for h in range(HEADS):
        mask[h, h * HEAD_WIDTH : (h + 1) * HEAD_WIDTH] = 1.0
    return mask


def spread_matrix():
    one = np.zeros((LEVELS * HEADS, LEVELS * WIDTH), np.float32)
    for l in range(LEVELS):
        for h in range(HEADS):
            at = l * WIDTH + h * HEAD_WIDTH
            one[l * HEADS + h, at : at + HEAD_WIDTH] = 1.0
    return np.concatenate([one, one], axis=0)


def mesh_id(x, y, z, core):
    return (lax.rem(y, 2) * 2 + core, x * 8 + z * 2 + y // 2)


def split_parts(values):
    first = lax.broadcasted_iota(jnp.int32, values.shape, 1) < 64
    high = values.astype(bf16).astype(f32)
    return jnp.where(first, high, values - high).astype(bf16)


def main_kernel(
    ids,
    pool_temp,
    window_temp,
    pixels,
    pixel_order,
    latents,
    heads,
    first_gain,
    second_gain,
    embed_bias,
    query_hbm,
    key_hbm,
    embed_hbm,
    value_hbm,
    pool_hbm,
    spread_hbm,
    qkv_hbm,
    proj_hbm,
    up_hbm,
    down_hbm,
    cot_hbm,
    mat0_hbm,
    mat1_hbm,
    mat2_hbm,
    mat3_hbm,
    mat4_hbm,
    mat5_hbm,
    output,
    back,
    whole,
    result,
    query_weight,
    key_weight,
    embed_weight,
    value_weight,
    pool_weight,
    spread,
    qkv_weight,
    proj_weight,
    up_weight,
    down_weight,
    cotangent,
    mat0,
    mat1,
    mat2,
    mat3,
    mat4,
    mat5,
    bias,
    outgoing,
    arrived,
    tokens,
    scores,
    values,
    sums,
    own_cot,
    cot_left,
    cot_east,
    left,
    east,
    wide,
    cot_shifted,
    back_grad,
    qs,
    ks,
    vs,
    masks,
    attended,
    norm2,
    norm2_t,
    total,
    leave,
    grads,
    pair,
    work,
    got1,
    got2,
    load_sem,
    store_sem,
    send,
    recv,
    ring_send,
    ring_recv,
    pair_send,
    pair_recv,
):
    enc = lax.axis_index("enc")
    lon = lax.axis_index("lon")
    mate = enc + 1 - 2 * lax.rem(enc, 2)
    peers = (mate, lax.rem(enc + 2, 4), lax.rem(mate + 2, 4))
    west_id = (enc, lax.rem(lon + 31, 32))
    east_id = (enc, lax.rem(lon + 1, 32))
    core = lax.rem(enc, 2)
    x_at = lon // 8
    y_at = lax.rem(lon, 2) * 2 + enc // 2
    z_at = lax.rem(lon // 2, 4)

    places = [[lax.rem(at + by, 4) for by in range(4)] for at in (x_at, y_at, z_at)]
    x_part = [place * 8 for place in places[0]]
    y_part = [place // 2 for place in places[1]]
    z_part = [place * 2 for place in places[2]]
    enc_part = [lax.rem(place, 2) * 2 + core for place in places[1]]

    def device_at(step):
        return enc_part[step[1]], x_part[step[0]] + y_part[step[1]] + z_part[step[2]]

    def by_core(first, second):
        return first + core * (second - first)

    def step_of(part, way, phase, by):
        step = [0, 0, 0]
        for dim, count in zip(phase, by):
            step[(part + way + dim) % 3] = count
        return tuple(step)

    def chunk_for(part, way, phase, by):
        chunk = 0
        for dim, count in zip(phase, by):
            chunk = chunk * 4 + places[(part + way + dim) % 3][count % 4]
        return chunk

    def chunk_at(part, phase, by):
        return by_core(*[chunk_for(part, way, phase, by) for way in range(2)])

    combos = [
        [by for by in itertools.product(range(4), repeat=len(phase)) if any(by)]
        for phase in PHASES
    ]
    others = sorted(
        {
            step_of(turn, 0, phase, by)
            for turn in range(3)
            for phase, bys in zip(PHASES, combos)
            for by in bys
        }
    )
    devices = {step: device_at(step) for step in others}

    def device_for(part, phase, by):
        near, far = [devices[step_of(part, way, phase, by)] for way in range(2)]
        return by_core(near[0], far[0]), by_core(near[1], far[1])

    barrier = pltpu.get_barrier_semaphore()
    for peer in peers:
        pl.semaphore_signal(barrier, inc=1, device_id=(peer, lon), device_id_type=MESH)
    for other in (west_id, east_id):
        pl.semaphore_signal(barrier, inc=1, device_id=other, device_id_type=MESH)
    for step in others:
        pl.semaphore_signal(barrier, inc=1, device_id=devices[step], device_id_type=MESH)

    loads = {}
    for index, (name, source, target) in enumerate(
        (
            ("query", query_hbm, query_weight),
            ("key", key_hbm, key_weight),
            ("cot", cot_hbm, cotangent),
            ("mat2", mat2_hbm, mat2),
            ("embed", embed_hbm, embed_weight),
            ("value", value_hbm, value_weight),
            ("spread", spread_hbm, spread),
            ("pool", pool_hbm, pool_weight),
            ("mat0", mat0_hbm, mat0),
            ("mat1", mat1_hbm, mat1),
            ("mat3", mat3_hbm, mat3),
            ("mat4", mat4_hbm, mat4),
            ("mat5", mat5_hbm, mat5),
            ("down", down_hbm, down_weight),
            ("qkv", qkv_hbm, qkv_weight),
            ("proj", proj_hbm, proj_weight),
            ("up", up_hbm, up_weight),
        )
    ):
        loads[name] = pltpu.make_async_copy(source, target, load_sem.at[index])
        loads[name].start()

    def remote(source, target, index, device):
        copy = pltpu.make_async_remote_copy(
            src_ref=source,
            dst_ref=target,
            send_sem=send.at[index],
            recv_sem=recv.at[index],
            device_id=device,
            device_id_type=MESH,
        )
        copy.start()
        return copy

    def sort_pixels(slot, _):
        block = pixels[slot].astype(f32).reshape(4 * SPOTS, PIXELS).astype(bf16)
        block = dot(pixel_order[...], block).astype(bf16).astype(f32)
        for owner in range(4):
            outgoing[owner, slot] = block[owner * SPOTS : (owner + 1) * SPOTS].astype(bf16)
        return 0

    far_copies = []

    def send_far(k, first, count):
        slots_there = pl.ds(first, count)
        for i in (1, 2):
            far_copies.append(
                remote(
                    outgoing.at[peers[i], slots_there],
                    arrived.at[i, slots_there],
                    7 + 2 * k + i,
                    (peers[i], lon),
                )
            )

    lax.fori_loop(0, FAR, sort_pixels, 0, unroll=True)
    pl.semaphore_wait(barrier, 5 + len(others))
    send_far(0, 0, FAR)
    lax.fori_loop(FAR, PER, sort_pixels, 0, unroll=True)
    copy_mate = remote(outgoing.at[peers[0]], arrived.at[0], 0, (peers[0], lon))
    send_far(1, FAR, PER - FAR)

    bias[...] = embed_bias[...].astype(f32)
    loads["query"].wait()
    loads["key"].wait()
    queries = dot(latents[...], query_weight[...]).astype(bf16).astype(f32)
    blocks = [queries[l : l + 1] * heads[...] for l in range(LEVELS)]
    blocks = jnp.concatenate(blocks, axis=0).astype(bf16)
    head_of = lax.rem(lax.broadcasted_iota(jnp.int32, (LEVELS * HEADS, 1), 0), HEADS)
    temp = jnp.zeros((LEVELS * HEADS, 1), f32)
    for h in range(HEADS):
        temp = jnp.where(head_of == h, pool_temp[h] * (1.0 / math.sqrt(HEAD_WIDTH)), temp)
    folded = dot(blocks, key_weight[...], ((1,), (1,))) * temp
    high = folded.astype(bf16)
    low = (folded - high.astype(f32)).astype(bf16)
    keys = jnp.concatenate([high, high, low, low], axis=0)

    def token_of(block, slot):
        level = ids[slot]
        return dot(block, embed_weight[level]) + bias[pl.ds(level, 1), :]

    def embed_near(i, _):
        near = token_of(outgoing[enc, i], enc * PER + i)
        far = token_of(arrived[0, i], mate * PER + i)
        tokens[i] = jnp.concatenate([near, far], axis=0).astype(bf16)
        return 0

    def embed_far(first):
        def embed(i, _):
            near = token_of(arrived[1, first + i], peers[1] * PER + first + i)
            far = token_of(arrived[2, first + i], peers[2] * PER + first + i)
            tokens[i] = jnp.concatenate([near, far], axis=0).astype(bf16)
            return 0

        return embed

    def project(first, count):
        block = jnp.concatenate([tokens[first + i] for i in range(count)], axis=0)
        projected = dot(block, value_weight[...])
        scored = dot(block, keys, ((1,), (1,)))
        scored = scored[:, :128] + scored[:, 128:]
        for i in range(2 * count):
            values[first * 2 + i] = projected[i * SPOTS : (i + 1) * SPOTS]
            scores[first * 2 + i] = scored[i * SPOTS : (i + 1) * SPOTS]

    def project_two(i, _):
        project(2 * i, 2)
        return 0

    def mix(stage, first, count, lo, hi):
        probs = jnp.concatenate([scores[first + i, lo:hi] for i in range(count)], axis=0)
        split = split_parts(probs)
        size = hi - lo
        for l in range(LEVELS):
            wider = dot(split, spread[:, l * WIDTH : (l + 1) * WIDTH])
            part = sums[stage, l, lo:hi]
            for i in range(count):
                part = part + wider[i * size : (i + 1) * size] * values[first + i, lo:hi]
            sums[stage, l, lo:hi] = part

    def mix_all(stage, pairs, lo, hi):
        def mix_four(i, _):
            mix(stage, 4 * i, 4, lo, hi)
            return 0

        lax.fori_loop(0, pairs // 2, mix_four, 0, unroll=True)
        if pairs % 2:
            mix(stage, 2 * pairs - 2, 2, lo, hi)

    def pool_stage(stage, pairs, embed):
        lax.fori_loop(0, pairs, embed, 0, unroll=True)
        if stage == 0:
            loads["value"].wait()
        lax.fori_loop(0, pairs // 2, project_two, 0, unroll=True)
        if pairs % 2:
            project(pairs - 1, 1)
        peak = scores[0]
        for s in range(1, 2 * pairs):
            peak = jnp.maximum(peak, scores[s])
        weight = jnp.zeros_like(peak)
        for s in range(2 * pairs):
            exponent = jnp.exp(scores[s] - peak)
            scores[s] = exponent
            weight = weight + exponent
        sums[stage] = jnp.zeros((LEVELS, SPOTS, WIDTH), f32)
        return peak, weight

    loads["cot"].wait()
    loads["mat2"].wait()
    own_cot[...] = cotangent[...].astype(f32).reshape(TOKENS, WIDTH).astype(bf16)
    cot_left[...] = dot(mat2[...], own_cot[...]).astype(bf16)
    loads["embed"].wait()
    copy_mate.wait_recv()
    stats = [pool_stage(0, PER, embed_near)]
    loads["spread"].wait()
    mix_all(0, PER, 0, SPOTS)
    far_copies[0].wait_recv()
    far_copies[1].wait_recv()
    stats.append(pool_stage(1, FAR, embed_far(0)))
    mix_all(1, FAR, 0, SPOTS)
    far_copies[2].wait_recv()
    far_copies[3].wait_recv()
    copy_cot = remote(cot_left, cot_east, 3, west_id)
    stats.append(pool_stage(2, PER - FAR, embed_far(FAR)))

    peak = stats[0][0]
    for other, _ in stats[1:]:
        peak = jnp.maximum(peak, other)
    decays = [jnp.exp(top - peak) for top, _ in stats]
    inverse = 1.0 / sum(weight * decay for decay, (_, weight) in zip(decays, stats))
    decays = [decay * inverse for decay in decays]
    loads["pool"].wait()

    def finish_pool(lo, hi):
        shares = split_parts(jnp.concatenate([decay[lo:hi] for decay in decays], axis=0))
        size = hi - lo
        pooled = []
        for l in range(LEVELS):
            share = dot(shares, spread[:, l * WIDTH : (l + 1) * WIDTH])
            level = share[:size] * sums[0, l, lo:hi]
            for k in range(1, STAGES):
                level = level + share[k * size : (k + 1) * size] * sums[k, l, lo:hi]
            pooled.append(level)
        projected = dot(jnp.concatenate(pooled, axis=0).astype(bf16), pool_weight[...])
        rows = [
            projected[l * size : (l + 1) * size] + latents[l : l + 1].astype(f32)
            for l in range(LEVELS)
        ]
        return jnp.concatenate(rows, axis=0).astype(bf16)

    mix_all(2, PER - FAR, 0, LEAD)
    lead = finish_pool(0, LEAD)
    loads["mat0"].wait()
    left[...] = dot(mat0[...], lead).astype(bf16)
    copy_left = remote(left, east, 4, west_id)
    mix_all(2, PER - FAR, LEAD, SPOTS)
    stream = jnp.concatenate([lead, finish_pool(LEAD, SPOTS)], axis=0)
    loads["mat1"].wait()
    kept = dot(mat1[...], stream)
    copy_cot.wait_recv()
    loads["mat3"].wait()
    loads["mat4"].wait()
    cot = (dot(mat3[...], own_cot[...]) + dot(mat4[...], cot_east[...])).astype(bf16)
    cot_shifted[...] = cot
    loads["down"].wait()
    for j in range(4):
        back_grad[j] = dot(cot, down_weight[j * 512 : (j + 1) * 512], ((1,), (1,)))
    copy_left.wait_recv()
    own = (kept + dot(mat4[...], east[...])).astype(bf16)
    wide[HALF : HALF + TOKENS] = own
    copy_up = remote(
        wide.at[pl.ds(HALF, HALF)],
        wide.at[pl.ds(HALF + TOKENS, HALF)],
        5,
        (lax.rem(enc + 3, 4), lon),
    )
    copy_down = remote(
        wide.at[pl.ds(TOKENS, HALF)], wide.at[pl.ds(0, HALF)], 6, (lax.rem(enc + 1, 4), lon)
    )

    loads["qkv"].wait()
    norm = normed(own.astype(f32), first_gain[...])
    own_q = dot(norm, qkv_weight[:, :WIDTH])
    own_k = dot(norm, qkv_weight[:, WIDTH : 2 * WIDTH])
    own_v = dot(norm, qkv_weight[:, 2 * WIDTH :])
    row = lax.broadcasted_iota(jnp.int32, (HALO, HALF), 0)
    col = lax.broadcasted_iota(jnp.int32, (HALO, HALF), 1)
    same = lax.rem(row, 2) == lax.rem(col, 2)
    first_key = jnp.where(enc == 0, HALO, 0)
    last_key = jnp.where(enc == 3, HALO, HALF)
    ones = jnp.ones((HALF, 128), f32)
    for win in range(2):
        inside = (col >= first_key) if win == 0 else (col < last_key)
        masks[win * 2] = jnp.where(inside, 0.0, -1e30)
        masks[win * 2 + 1] = jnp.where(inside & same, 0.0, -1e30)
    copy_up.wait_recv()
    copy_down.wait_recv()
    halo = jnp.concatenate([wide[:HALF], wide[HALF + TOKENS :]], axis=0).astype(f32)
    norm = normed(halo, first_gain[...])
    halo_k = dot(norm, qkv_weight[:, WIDTH : 2 * WIDTH])
    halo_v = dot(norm, qkv_weight[:, 2 * WIDTH :])
    for win in range(2):
        for two in range(2):
            at = win * HALF + two * HALO
            rows = slice(at, at + HALO)
            for g in range(4):
                lanes = slice(g * 128, (g + 1) * 128)
                index = (win * 2 + two) * 4 + g
                qs[index] = own_q[rows, lanes]
                key = (halo_k[rows, lanes], own_k[rows, lanes])
                value = (halo_v[rows, lanes], own_v[rows, lanes])
                if win == 1:
                    key, value = key[::-1], value[::-1]
                ks[index] = jnp.concatenate(key, axis=0).astype(bf16)
                value = jnp.concatenate(value, axis=0)
                vs[index] = jnp.concatenate([value, ones], axis=1).astype(bf16)

    lane = lax.broadcasted_iota(jnp.int32, (HALO, 128), 1) // HEAD_WIDTH

    def attend(index, _):
        group = lax.rem(index, 4)
        query = qs[index]
        mask = masks[index // 4]
        stacked = [jnp.where(lane == h, query, 0.0) for h in range(4)]
        raw = dot(jnp.concatenate(stacked, axis=0).astype(bf16), ks[index], ((1,), (1,)))
        exponents = []
        for h in range(4):
            masked = raw[h * HALO : (h + 1) * HALO] + mask
            top = jnp.max(masked, axis=-1, keepdims=True)
            factor = window_temp[group * 4 + h] * (1.0 / math.sqrt(HEAD_WIDTH))
            exponents.append(jnp.exp((masked - top) * factor).astype(bf16).astype(f32))
        exponent = jnp.concatenate(exponents, axis=0).astype(bf16)
        mixed = dot(exponent, vs[index])
        above = mixed[:HALO, :128]
        under = mixed[:HALO, 128:]
        for h in range(1, 4):
            rows = slice(h * HALO, (h + 1) * HALO)
            above = jnp.where(lane == h, mixed[rows, :128], above)
            under = jnp.where(lane == h, mixed[rows, 128:], under)
        attended[index] = above / under
        return 0

    lax.fori_loop(0, 16, attend, 0, unroll=True)

    rows = [
        jnp.concatenate([attended[block * 4 + g] for g in range(4)], axis=1) for block in range(4)
    ]
    loads["proj"].wait()
    mixed = dot(jnp.concatenate(rows, axis=0).astype(bf16), proj_weight[...])
    middle = (own.astype(f32) + mixed).astype(bf16).astype(f32)
    norm = normed(middle, second_gain[...])
    norm2[...] = norm
    norm2_t[...] = norm.T
    total[...] = middle

    got = (got1, got2)
    sizes = [PART_ROWS // 4, PART_ROWS // 64]
    offsets = [0, len(combos[0])]
    starts = []
    for p in range(PARTS):
        at = [0]
        for phase in range(len(PHASES)):
            at.append(at[-1] + chunk_at(p, PHASES[phase], (0, 0)) * sizes[phase])
        starts.append(at)
    pair_id = (mate, lon)
    pair_copies = []
    stores = []
    copies = {}

    def give_pair(index, source, target):
        copy = pltpu.make_async_remote_copy(
            src_ref=source,
            dst_ref=target,
            send_sem=pair_send.at[index],
            recv_sem=pair_recv.at[index],
            device_id=pair_id,
            device_id_type=MESH,
        )
        copy.start()
        pair_copies.append(copy)
        return copy

    def ring_copy(way, p, phase, k, source, target):
        at = offsets[phase] + k
        return pltpu.make_async_remote_copy(
            src_ref=source,
            dst_ref=target,
            send_sem=ring_send.at[way, p, at],
            recv_sem=ring_recv.at[way, p, at],
            device_id=device_for(p, PHASES[phase], combos[phase][k]),
            device_id_type=MESH,
        )

    def scatter(p, phase):
        size = sizes[phase]
        for k, by in enumerate(combos[phase]):
            target = chunk_at(p, PHASES[phase], by)
            first = pl.multiple_of(starts[p][phase] + target * size, 16)
            source = work.at[p, pl.ds(first, size)]
            copy = ring_copy(0, p, phase, k, source, got[phase].at[p, k])
            copy.start()
            copies[0, p, phase, k] = copy

    def add_up(p, phase):
        for k in range(len(combos[phase])):
            copies[0, p, phase, k].wait_recv()
        size = sizes[phase]
        first = pl.multiple_of(starts[p][phase + 1], 16)
        held = work[p, pl.ds(first, size), :].astype(f32)
        for k in range(len(combos[phase])):
            held = held + got[phase][p, k].astype(f32)
        if phase == 0:
            work[p, pl.ds(first, size), :] = held.astype(bf16)
            scatter(p, 1)
        else:
            result[core, p, pl.ds(first, size), :] = held.astype(bf16)
            gather(p, 1)

    def gather(p, phase):
        first = pl.multiple_of(starts[p][phase + 1], 16)
        piece = result.at[core, p, pl.ds(first, sizes[phase])]
        for k in range(len(combos[phase])):
            copy = ring_copy(1, p, phase, k, piece, piece)
            copy.start()
            copies[1, p, phase, k] = copy

    def gathered(p, phase):
        for k, by in enumerate(combos[phase]):
            source = chunk_at(p, PHASES[phase], [4 - step for step in by])
            first = pl.multiple_of(starts[p][phase] + source * sizes[phase], 16)
            piece = result.at[core, p, pl.ds(first, sizes[phase])]
            ring_copy(1, p, phase, k, piece, piece).wait_recv()
            if phase == 0:
                give_pair(PARTS + 4 * p + 1 + k, piece, piece)
        if phase == 1:
            gather(p, 0)
            first = pl.multiple_of(starts[p][1], 16)
            piece = result.at[core, p, pl.ds(first, sizes[0])]
            give_pair(PARTS + 4 * p, piece, piece)
        else:
            store(core, p)

    def store(half, p):
        copy = pltpu.make_async_copy(result.at[half, p], whole.at[half, p], store_sem.at[len(stores)])
        copy.start()
        stores.append(copy)

    def paired(p):
        for k in range(4):
            piece = result.at[1 - core, p, pl.ds(0, sizes[0])]
            pltpu.make_async_remote_copy(
                src_ref=piece,
                dst_ref=piece,
                send_sem=pair_send.at[PARTS + 4 * p + k],
                recv_sem=pair_recv.at[PARTS + 4 * p + k],
                device_id=pair_id,
                device_id_type=MESH,
            ).wait_recv()
        store(1 - core, p)

    def mlp(j):
        columns = slice(j * 512, (j + 1) * 512)
        x = dot(norm2[...], up_weight[:, columns])
        cubic = 0.044715 * (x * x)
        scale = math.sqrt(2.0 / math.pi)
        bend = jnp.tanh(scale * (x * (1.0 + cubic)))
        hidden = (0.5 * x * (1.0 + bend)).astype(bf16)
        slope = 0.5 * (1.0 + bend) + 0.5 * x * (1.0 - bend * bend) * (scale * (1.0 + 3.0 * cubic))
        slope = (slope * back_grad[j]).astype(bf16)
        down_grad = dot(hidden, cot_shifted[...], ((0,), (0,))).astype(bf16)
        up_grad = dot(norm2_t[...], slope).astype(bf16)
        for i in range(2):
            lanes = slice(i * PART_COLS, (i + 1) * PART_COLS)
            grads[0, j, i * 512 : (i + 1) * 512] = up_grad[:, lanes]
            grads[1, j, i * 512 : (i + 1) * 512] = down_grad[:, lanes]
        total[...] += dot(hidden, down_weight[columns])

    def reduce_pair(p):
        pair_copies[p].wait_recv()
        work[p] = (grads[core, p].astype(f32) + pair[p].astype(f32)).astype(bf16)
        scatter(p, 0)

    loads["up"].wait()
    for j in range(PARTS):
        mlp(j)
        give_pair(j, grads.at[1 - core, j], pair.at[j])
        if j > 1:
            reduce_pair(j - 2)
    reduce_pair(PARTS - 2)
    done = total[...].astype(bf16)
    output[...] = done
    loads["mat5"].wait()
    leave[...] = dot(mat5[...], done).astype(bf16)
    reduce_pair(PARTS - 1)
    add_up(0, 0)
    add_up(1, 0)
    add_up(2, 0)
    add_up(0, 1)
    add_up(3, 0)
    copy_back = remote(leave, back, 7, east_id)
    add_up(1, 1)
    add_up(2, 1)
    gathered(0, 1)
    add_up(3, 1)
    gathered(1, 1)
    gathered(2, 1)
    gathered(3, 1)
    for p in range(PARTS):
        gathered(p, 0)
        if p > 0:
            paired(p - 1)
    paired(PARTS - 1)
    copy_back.wait_recv()
    for copy in (copy_mate, copy_cot, copy_left, copy_up, copy_down, copy_back, *far_copies):
        copy.wait_send()
    for copy in pair_copies:
        copy.wait_send()
    for copy in copies.values():
        copy.wait_send()
    for copy in stores:
        copy.wait()


def main_call(
    pixels,
    ids,
    embed_weight,
    embed_bias,
    latents,
    query_weight,
    key_weight,
    value_weight,
    pool_weight,
    pool_temp,
    first_gain,
    qkv_weight,
    window_temp,
    proj_weight,
    second_gain,
    up_weight,
    down_weight,
    cot,
):
    vmem = pl.BlockSpec(memory_space=pltpu.VMEM)
    smem = pl.BlockSpec(memory_space=pltpu.SMEM)
    anywhere = pl.BlockSpec(memory_space=pl.ANY)
    matrices = [jnp.asarray(matrix, bf16) for matrix in order_matrices()]
    spread = jnp.asarray(spread_matrix(), bf16)
    loaded = (
        query_weight,
        key_weight,
        embed_weight,
        value_weight,
        pool_weight,
        spread,
        qkv_weight,
        proj_weight,
        up_weight,
        down_weight,
        cot,
        *matrices,
    )
    piece = pltpu.VMEM((HALF, WIDTH), bf16)
    part = pltpu.VMEM((PARTS, PART_ROWS, PART_COLS), bf16)
    return pl.pallas_call(
        main_kernel,
        out_shape=(
            jax.ShapeDtypeStruct((TOKENS, WIDTH), bf16),
            jax.ShapeDtypeStruct((HALF, WIDTH), bf16),
            jax.ShapeDtypeStruct((2, PARTS, PART_ROWS, PART_COLS), bf16),
        ),
        in_specs=[smem] * 3 + [vmem] * 7 + [anywhere] * len(loaded),
        out_specs=(vmem, vmem, anywhere),
        scratch_shapes=[pltpu.VMEM((2, PARTS, PART_ROWS, PART_COLS), bf16)]
        + [pltpu.VMEM(value.shape, bf16) for value in loaded]
        + [
            pltpu.VMEM((SLOTS, WIDTH), f32),
            pltpu.VMEM((4, PER, SPOTS, PIXELS), bf16),
            pltpu.VMEM((3, PER, SPOTS, PIXELS), bf16),
            pltpu.VMEM((PER, 2 * SPOTS, WIDTH), bf16),
            pltpu.VMEM((2 * PER, SPOTS, 128), f32),
            pltpu.VMEM((2 * PER, SPOTS, WIDTH), f32),
            pltpu.VMEM((STAGES, LEVELS, SPOTS, WIDTH), f32),
            pltpu.VMEM((TOKENS, WIDTH), bf16),
            piece,
            piece,
            piece,
            piece,
            pltpu.VMEM((2 * TOKENS, WIDTH), bf16),
            pltpu.VMEM((TOKENS, WIDTH), bf16),
            pltpu.VMEM((4, TOKENS, 512), f32),
            pltpu.VMEM((16, HALO, 128), f32),
            pltpu.VMEM((16, HALF, 128), bf16),
            pltpu.VMEM((16, HALF, 256), bf16),
            pltpu.VMEM((4, HALO, HALF), f32),
            pltpu.VMEM((16, HALO, 128), f32),
            pltpu.VMEM((TOKENS, WIDTH), bf16),
            pltpu.VMEM((WIDTH, TOKENS), bf16),
            pltpu.VMEM((TOKENS, WIDTH), f32),
            piece,
            pltpu.VMEM((2, PARTS, PART_ROWS, PART_COLS), bf16),
            part,
            part,
            pltpu.VMEM((PARTS, 3, PART_ROWS // 4, PART_COLS), bf16),
            pltpu.VMEM((PARTS, 15, PART_ROWS // 64, PART_COLS), bf16),
            pltpu.SemaphoreType.DMA((len(loaded),)),
            pltpu.SemaphoreType.DMA((2 * PARTS,)),
            pltpu.SemaphoreType.DMA((12,)),
            pltpu.SemaphoreType.DMA((12,)),
            pltpu.SemaphoreType.DMA((2, PARTS, 18)),
            pltpu.SemaphoreType.DMA((2, PARTS, 18)),
            pltpu.SemaphoreType.DMA((5 * PARTS,)),
            pltpu.SemaphoreType.DMA((5 * PARTS,)),
        ],
        compiler_params=pltpu.CompilerParams(
            collective_id=1, has_side_effects=True, vmem_limit_bytes=60 * 1024 * 1024
        ),
        name="main",
    )(
        ids,
        pool_temp,
        window_temp,
        pixels,
        jnp.asarray(pixel_matrix(), bf16),
        latents,
        jnp.asarray(head_rows(), f32),
        first_gain[None, :],
        second_gain[None, :],
        embed_bias,
        *loaded,
    )


def finish_kernel(
    sums, shifted, back, keep, take, output, up_hbm, down_hbm, loaded, up_grad, down_grad, load_sem, store_sem
):
    scaling = 1.0 / math.sqrt(NTOK)
    loads = []
    for p in range(PARTS):
        loads.append(pltpu.make_async_copy(sums.at[:, p], loaded.at[p], load_sem.at[p]))
        loads[-1].start()
    stores = []

    def store(source, target):
        stores.append(pltpu.make_async_copy(source, target, store_sem.at[len(stores)]))
        stores[-1].start()

    for p in range(PARTS):
        loads[p].wait()
        wide = slice(p * 512, (p + 1) * 512)
        for i in range(2):
            rows = slice(i * 512, (i + 1) * 512)
            lanes = slice(i * PART_COLS, (i + 1) * PART_COLS)
            up_lanes = slice(p * 512 + i * PART_COLS, p * 512 + (i + 1) * PART_COLS)
            down_grad[wide, lanes] = loaded[p, 1, rows].astype(f32) * scaling
            up_grad[:, up_lanes] = loaded[p, 0, rows].astype(f32) * scaling
        store(down_grad.at[pl.ds(p * 512, 512)], down_hbm.at[pl.ds(p * 512, 512)])
        store(up_grad.at[:, pl.ds(p * 512, 512)], up_hbm.at[:, pl.ds(p * 512, 512)])
    whole = dot(keep[...], shifted[...]) + dot(take[...], back[...])
    output[...] = whole.reshape(SPOTS, LEVELS, WIDTH).astype(bf16)
    for copy in stores:
        copy.wait()


def finish(sums, shifted, back):
    keep, take = final_matrices()
    vmem = pl.BlockSpec(memory_space=pltpu.VMEM)
    anywhere = pl.BlockSpec(memory_space=pl.ANY)
    return pl.pallas_call(
        finish_kernel,
        out_shape=(
            jax.ShapeDtypeStruct((SPOTS, LEVELS, WIDTH), bf16),
            jax.ShapeDtypeStruct((WIDTH, FF), f32),
            jax.ShapeDtypeStruct((FF, WIDTH), f32),
        ),
        in_specs=[anywhere] + [vmem] * 4,
        out_specs=(vmem, anywhere, anywhere),
        scratch_shapes=[
            pltpu.VMEM((PARTS, 2, PART_ROWS, PART_COLS), bf16),
            pltpu.VMEM((WIDTH, FF), f32),
            pltpu.VMEM((FF, WIDTH), f32),
            pltpu.SemaphoreType.DMA((PARTS,)),
            pltpu.SemaphoreType.DMA((2 * PARTS,)),
        ],
        compiler_params=pltpu.CompilerParams(vmem_limit_bytes=60 * 1024 * 1024),
        name="finish",
    )(
        sums,
        shifted,
        back,
        jnp.asarray(keep, bf16),
        jnp.asarray(take, bf16),
    )


def per_device(
    pixel_field,
    level_ids,
    embed_weight,
    embed_bias,
    latents,
    query_weight,
    key_weight,
    value_weight,
    pool_weight,
    pool_temp,
    first_gain,
    qkv_weight,
    window_temp,
    proj_weight,
    second_gain,
    up_weight,
    down_weight,
    cotangent,
):
    cot = jnp.transpose(cotangent, (1, 2, 0, 3)).reshape(SPOTS, LEVELS, WIDTH)
    shifted, back, sums = main_call(
        jnp.transpose(pixel_field, (0, 3, 1, 2)),
        level_ids,
        embed_weight,
        embed_bias,
        latents,
        query_weight,
        key_weight,
        value_weight,
        pool_weight,
        pool_temp,
        first_gain,
        qkv_weight,
        window_temp,
        proj_weight,
        second_gain,
        up_weight,
        down_weight,
        cot,
    )
    output, up_grad, down_grad = finish(sums, shifted, back)
    output = output.reshape(ROWS, COLS, LEVELS, WIDTH)
    return (jnp.transpose(output, (2, 0, 1, 3)), up_grad, down_grad)


def solution(mesh):
    placed = (P("enc", None, None, "lon"),) + (P(),) * 16 + (P(None, "enc", "lon", None),)
    return jax.shard_map(
        per_device,
        mesh=mesh,
        in_specs=placed,
        out_specs=(P(None, "enc", "lon", None), P(), P()),
        check_vma=False,
    )
```

```python
import itertools
import math

import jax
import jax.numpy as jnp
import numpy as np
from jax import lax
from jax.experimental import pallas as pl
from jax.experimental.pallas import tpu as pltpu
from jax.sharding import PartitionSpec as P

SLOTS = 52
HEADS = 16
HEAD_WIDTH = 32
WIDTH = 512
FF = 2048
LEVELS = 4
ROWS = 6
COLS = 12
SPOTS = ROWS * COLS
TOKENS = LEVELS * SPOTS
HALF = TOKENS // 2
PIXELS = 100
PER = SLOTS // 4
FAR = 7
EPSILON = 1e-05
NTOK = 36864
PARTS = 4
PART_ROWS = 1024
PART_COLS = 256
HALO = HALF // 2
LEAD = 40
STAGES = 3
PHASES = ((0,), (1, 2))
MESH = pl.DeviceIdType.MESH

f32 = jnp.float32
bf16 = jnp.bfloat16


def dot(a, b, contract=((1,), (0,))):
    return lax.dot_general(a, b, (contract, ((), ())), preferred_element_type=f32)


def normed(values, gain):
    mean = jnp.mean(values, axis=-1, keepdims=True)
    centred = values - mean
    variance = jnp.mean(centred * centred, axis=-1, keepdims=True)
    return (centred * lax.rsqrt(variance + EPSILON) * gain).astype(bf16)


def pooled_at(r, c, l):
    spot = c * ROWS + r
    if spot < LEAD:
        return l * LEAD + spot
    return LEVELS * LEAD + l * (SPOTS - LEAD) + spot - LEAD


def piece_at(r, c, l):
    return (r * (COLS // 2) + c) * LEVELS + l


def natural_at(r, c, l):
    return (r * COLS + c) * LEVELS + l


def shifted_at(r, c, l):
    pair, place = ((1, 0), (0, 0), (0, 1), (1, 1))[l]
    return (r // 3) * HALF + pair * HALO + ((r % 3) * COLS + c) * 2 + place


def matrix_of(rows, cols, entries):
    matrix = np.zeros((rows, cols), np.float32)
    for r in range(ROWS):
        for c in range(COLS // 2):
            for l in range(LEVELS):
                matrix[entries(r, c, l)] = 1.0
    return matrix


def order_matrices():
    half = COLS // 2
    return (
        matrix_of(HALF, LEVELS * LEAD, lambda r, c, l: (piece_at(r, c, l), pooled_at(r, c, l))),
        matrix_of(TOKENS, TOKENS, lambda r, c, l: (shifted_at(r, c, l), pooled_at(r, half + c, l))),
        matrix_of(HALF, TOKENS, lambda r, c, l: (piece_at(r, c, l), natural_at(r, c, l))),
        matrix_of(TOKENS, TOKENS, lambda r, c, l: (shifted_at(r, c, l), natural_at(r, half + c, l))),
        matrix_of(TOKENS, HALF, lambda r, c, l: (shifted_at(r, half + c, l), piece_at(r, c, l))),
        matrix_of(HALF, TOKENS, lambda r, c, l: (piece_at(r, c, l), shifted_at(r, half + c, l))),
    )


def final_matrices():
    half = COLS // 2
    return (
        matrix_of(TOKENS, TOKENS, lambda r, c, l: (natural_at(r, half + c, l), shifted_at(r, c, l))),
        matrix_of(TOKENS, HALF, lambda r, c, l: (natural_at(r, c, l), piece_at(r, c, l))),
    )


def pixel_matrix():
    matrix = np.zeros((4 * SPOTS, 4 * SPOTS), np.float32)
    for owner in range(4):
        for c in range(COLS):
            for r in range(ROWS):
                matrix[owner * SPOTS + c * ROWS + r, c * 4 * ROWS + owner * ROWS + r] = 1.0
    return matrix


def head_rows():
    mask = np.zeros((HEADS, WIDTH), np.float32)
    for h in range(HEADS):
        mask[h, h * HEAD_WIDTH : (h + 1) * HEAD_WIDTH] = 1.0
    return mask


def spread_matrix():
    one = np.zeros((LEVELS * HEADS, LEVELS * WIDTH), np.float32)
    for l in range(LEVELS):
        for h in range(HEADS):
            at = l * WIDTH + h * HEAD_WIDTH
            one[l * HEADS + h, at : at + HEAD_WIDTH] = 1.0
    return np.concatenate([one, one], axis=0)


def mesh_id(x, y, z, core):
    return (lax.rem(y, 2) * 2 + core, x * 8 + z * 2 + y // 2)


def split_parts(values):
    first = lax.broadcasted_iota(jnp.int32, values.shape, 1) < 64
    high = values.astype(bf16).astype(f32)
    return jnp.where(first, high, values - high).astype(bf16)


def main_kernel(
    ids,
    pool_temp,
    window_temp,
    pixels,
    pixel_order,
    latents,
    heads,
    first_gain,
    second_gain,
    embed_bias,
    query_hbm,
    key_hbm,
    embed_hbm,
    value_hbm,
    pool_hbm,
    spread_hbm,
    qkv_hbm,
    proj_hbm,
    up_hbm,
    down_hbm,
    cot_hbm,
    mat0_hbm,
    mat1_hbm,
    mat2_hbm,
    mat3_hbm,
    mat4_hbm,
    mat5_hbm,
    output,
    back,
    whole,
    result,
    query_weight,
    key_weight,
    embed_weight,
    value_weight,
    pool_weight,
    spread,
    qkv_weight,
    proj_weight,
    up_weight,
    down_weight,
    cotangent,
    mat0,
    mat1,
    mat2,
    mat3,
    mat4,
    mat5,
    bias,
    outgoing,
    arrived,
    tokens,
    scores,
    values,
    sums,
    own_cot,
    cot_left,
    cot_east,
    left,
    east,
    wide,
    cot_shifted,
    back_grad,
    qs,
    ks,
    vs,
    masks,
    attended,
    norm2,
    norm2_t,
    total,
    leave,
    grads,
    pair,
    work,
    got1,
    got2,
    load_sem,
    store_sem,
    send,
    recv,
    ring_send,
    ring_recv,
    pair_send,
    pair_recv,
):
    enc = lax.axis_index("enc")
    lon = lax.axis_index("lon")
    mate = enc + 1 - 2 * lax.rem(enc, 2)
    peers = (mate, lax.rem(enc + 2, 4), lax.rem(mate + 2, 4))
    west_id = (enc, lax.rem(lon + 31, 32))
    east_id = (enc, lax.rem(lon + 1, 32))
    core = lax.rem(enc, 2)
    x_at = lon // 8
    y_at = lax.rem(lon, 2) * 2 + enc // 2
    z_at = lax.rem(lon // 2, 4)

    places = [[lax.rem(at + by, 4) for by in range(4)] for at in (x_at, y_at, z_at)]
    x_part = [place * 8 for place in places[0]]
    y_part = [place // 2 for place in places[1]]
    z_part = [place * 2 for place in places[2]]
    enc_part = [lax.rem(place, 2) * 2 + core for place in places[1]]

    def device_at(step):
        return enc_part[step[1]], x_part[step[0]] + y_part[step[1]] + z_part[step[2]]

    def by_core(first, second):
        return first + core * (second - first)

    def step_of(part, way, phase, by):
        step = [0, 0, 0]
        for dim, count in zip(phase, by):
            step[(part + way + dim) % 3] = count
        return tuple(step)

    def chunk_for(part, way, phase, by):
        chunk = 0
        for dim, count in zip(phase, by):
            chunk = chunk * 4 + places[(part + way + dim) % 3][count % 4]
        return chunk

    def chunk_at(part, phase, by):
        return by_core(*[chunk_for(part, way, phase, by) for way in range(2)])

    combos = [
        [by for by in itertools.product(range(4), repeat=len(phase)) if any(by)]
        for phase in PHASES
    ]
    others = sorted(
        {
            step_of(turn, 0, phase, by)
            for turn in range(3)
            for phase, bys in zip(PHASES, combos)
            for by in bys
        }
    )
    devices = {step: device_at(step) for step in others}

    def device_for(part, phase, by):
        near, far = [devices[step_of(part, way, phase, by)] for way in range(2)]
        return by_core(near[0], far[0]), by_core(near[1], far[1])

    barrier = pltpu.get_barrier_semaphore()
    for peer in peers:
        pl.semaphore_signal(barrier, inc=1, device_id=(peer, lon), device_id_type=MESH)
    for other in (west_id, east_id):
        pl.semaphore_signal(barrier, inc=1, device_id=other, device_id_type=MESH)
    for step in others:
        pl.semaphore_signal(barrier, inc=1, device_id=devices[step], device_id_type=MESH)

    loads = {}
    for index, (name, source, target) in enumerate(
        (
            ("query", query_hbm, query_weight),
            ("key", key_hbm, key_weight),
            ("cot", cot_hbm, cotangent),
            ("mat2", mat2_hbm, mat2),
            ("embed", embed_hbm, embed_weight),
            ("value", value_hbm, value_weight),
            ("spread", spread_hbm, spread),
            ("pool", pool_hbm, pool_weight),
            ("mat0", mat0_hbm, mat0),
            ("mat1", mat1_hbm, mat1),
            ("mat3", mat3_hbm, mat3),
            ("mat4", mat4_hbm, mat4),
            ("mat5", mat5_hbm, mat5),
            ("down", down_hbm, down_weight),
            ("qkv", qkv_hbm, qkv_weight),
            ("proj", proj_hbm, proj_weight),
            ("up", up_hbm, up_weight),
        )
    ):
        loads[name] = pltpu.make_async_copy(source, target, load_sem.at[index])
        loads[name].start()

    def remote(source, target, index, device):
        copy = pltpu.make_async_remote_copy(
            src_ref=source,
            dst_ref=target,
            send_sem=send.at[index],
            recv_sem=recv.at[index],
            device_id=device,
            device_id_type=MESH,
        )
        copy.start()
        return copy

    def sort_pixels(slot, _):
        block = pixels[slot].astype(f32).reshape(4 * SPOTS, PIXELS).astype(bf16)
        block = dot(pixel_order[...], block).astype(bf16).astype(f32)
        for owner in range(4):
            outgoing[owner, slot] = block[owner * SPOTS : (owner + 1) * SPOTS].astype(bf16)
        return 0

    far_copies = []

    def send_far(k, first, count):
        slots_there = pl.ds(first, count)
        for i in (1, 2):
            far_copies.append(
                remote(
                    outgoing.at[peers[i], slots_there],
                    arrived.at[i, slots_there],
                    7 + 2 * k + i,
                    (peers[i], lon),
                )
            )

    lax.fori_loop(0, FAR, sort_pixels, 0, unroll=True)
    pl.semaphore_wait(barrier, 5 + len(others))
    send_far(0, 0, FAR)
    lax.fori_loop(FAR, PER, sort_pixels, 0, unroll=True)
    copy_mate = remote(outgoing.at[peers[0]], arrived.at[0], 0, (peers[0], lon))
    send_far(1, FAR, PER - FAR)

    bias[...] = embed_bias[...].astype(f32)
    loads["query"].wait()
    loads["key"].wait()
    queries = dot(latents[...], query_weight[...]).astype(bf16).astype(f32)
    blocks = [queries[l : l + 1] * heads[...] for l in range(LEVELS)]
    blocks = jnp.concatenate(blocks, axis=0).astype(bf16)
    head_of = lax.rem(lax.broadcasted_iota(jnp.int32, (LEVELS * HEADS, 1), 0), HEADS)
    temp = jnp.zeros((LEVELS * HEADS, 1), f32)
    for h in range(HEADS):
        temp = jnp.where(head_of == h, pool_temp[h] * (1.0 / math.sqrt(HEAD_WIDTH)), temp)
    folded = dot(blocks, key_weight[...], ((1,), (1,))) * temp
    high = folded.astype(bf16)
    low = (folded - high.astype(f32)).astype(bf16)
    keys = jnp.concatenate([high, high, low, low], axis=0)

    def token_of(block, slot):
        level = ids[slot]
        return dot(block, embed_weight[level]) + bias[pl.ds(level, 1), :]

    def embed_near(i, _):
        near = token_of(outgoing[enc, i], enc * PER + i)
        far = token_of(arrived[0, i], mate * PER + i)
        tokens[i] = jnp.concatenate([near, far], axis=0).astype(bf16)
        return 0

    def embed_far(first):
        def embed(i, _):
            near = token_of(arrived[1, first + i], peers[1] * PER + first + i)
            far = token_of(arrived[2, first + i], peers[2] * PER + first + i)
            tokens[i] = jnp.concatenate([near, far], axis=0).astype(bf16)
            return 0

        return embed

    def project(first, count):
        block = jnp.concatenate([tokens[first + i] for i in range(count)], axis=0)
        projected = dot(block, value_weight[...])
        scored = dot(block, keys, ((1,), (1,)))
        scored = scored[:, :128] + scored[:, 128:]
        for i in range(2 * count):
            values[first * 2 + i] = projected[i * SPOTS : (i + 1) * SPOTS]
            scores[first * 2 + i] = scored[i * SPOTS : (i + 1) * SPOTS]

    def project_two(i, _):
        project(2 * i, 2)
        return 0

    def mix(stage, first, count, lo, hi):
        probs = jnp.concatenate([scores[first + i, lo:hi] for i in range(count)], axis=0)
        split = split_parts(probs)
        size = hi - lo
        for l in range(LEVELS):
            wider = dot(split, spread[:, l * WIDTH : (l + 1) * WIDTH])
            part = sums[stage, l, lo:hi]
            for i in range(count):
                part = part + wider[i * size : (i + 1) * size] * values[first + i, lo:hi]
            sums[stage, l, lo:hi] = part

    def mix_all(stage, pairs, lo, hi):
        def mix_four(i, _):
            mix(stage, 4 * i, 4, lo, hi)
            return 0

        lax.fori_loop(0, pairs // 2, mix_four, 0, unroll=True)
        if pairs % 2:
            mix(stage, 2 * pairs - 2, 2, lo, hi)

    def pool_stage(stage, pairs, embed):
        lax.fori_loop(0, pairs, embed, 0, unroll=True)
        if stage == 0:
            loads["value"].wait()
        lax.fori_loop(0, pairs // 2, project_two, 0, unroll=True)
        if pairs % 2:
            project(pairs - 1, 1)
        peak = scores[0]
        for s in range(1, 2 * pairs):
            peak = jnp.maximum(peak, scores[s])
        weight = jnp.zeros_like(peak)
        for s in range(2 * pairs):
            exponent = jnp.exp(scores[s] - peak)
            scores[s] = exponent
            weight = weight + exponent
        sums[stage] = jnp.zeros((LEVELS, SPOTS, WIDTH), f32)
        return peak, weight

    loads["cot"].wait()
    loads["mat2"].wait()
    own_cot[...] = cotangent[...].astype(f32).reshape(TOKENS, WIDTH).astype(bf16)
    cot_left[...] = dot(mat2[...], own_cot[...]).astype(bf16)
    loads["embed"].wait()
    copy_mate.wait_recv()
    stats = [pool_stage(0, PER, embed_near)]
    loads["spread"].wait()
    mix_all(0, PER, 0, SPOTS)
    far_copies[0].wait_recv()
    far_copies[1].wait_recv()
    stats.append(pool_stage(1, FAR, embed_far(0)))
    mix_all(1, FAR, 0, SPOTS)
    far_copies[2].wait_recv()
    far_copies[3].wait_recv()
    copy_cot = remote(cot_left, cot_east, 3, west_id)
    stats.append(pool_stage(2, PER - FAR, embed_far(FAR)))

    peak = stats[0][0]
    for other, _ in stats[1:]:
        peak = jnp.maximum(peak, other)
    decays = [jnp.exp(top - peak) for top, _ in stats]
    inverse = 1.0 / sum(weight * decay for decay, (_, weight) in zip(decays, stats))
    decays = [decay * inverse for decay in decays]
    loads["pool"].wait()

    def finish_pool(lo, hi):
        shares = split_parts(jnp.concatenate([decay[lo:hi] for decay in decays], axis=0))
        size = hi - lo
        pooled = []
        for l in range(LEVELS):
            share = dot(shares, spread[:, l * WIDTH : (l + 1) * WIDTH])
            level = share[:size] * sums[0, l, lo:hi]
            for k in range(1, STAGES):
                level = level + share[k * size : (k + 1) * size] * sums[k, l, lo:hi]
            pooled.append(level)
        projected = dot(jnp.concatenate(pooled, axis=0).astype(bf16), pool_weight[...])
        rows = [
            projected[l * size : (l + 1) * size] + latents[l : l + 1].astype(f32)
            for l in range(LEVELS)
        ]
        return jnp.concatenate(rows, axis=0).astype(bf16)

    mix_all(2, PER - FAR, 0, LEAD)
    lead = finish_pool(0, LEAD)
    loads["mat0"].wait()
    left[...] = dot(mat0[...], lead).astype(bf16)
    copy_left = remote(left, east, 4, west_id)
    mix_all(2, PER - FAR, LEAD, SPOTS)
    stream = jnp.concatenate([lead, finish_pool(LEAD, SPOTS)], axis=0)
    loads["mat1"].wait()
    kept = dot(mat1[...], stream)
    copy_cot.wait_recv()
    loads["mat3"].wait()
    loads["mat4"].wait()
    cot = (dot(mat3[...], own_cot[...]) + dot(mat4[...], cot_east[...])).astype(bf16)
    cot_shifted[...] = cot
    loads["down"].wait()
    for j in range(4):
        back_grad[j] = dot(cot, down_weight[j * 512 : (j + 1) * 512], ((1,), (1,)))
    copy_left.wait_recv()
    own = (kept + dot(mat4[...], east[...])).astype(bf16)
    wide[HALF : HALF + TOKENS] = own
    copy_up = remote(
        wide.at[pl.ds(HALF, HALF)],
        wide.at[pl.ds(HALF + TOKENS, HALF)],
        5,
        (lax.rem(enc + 3, 4), lon),
    )
    copy_down = remote(
        wide.at[pl.ds(TOKENS, HALF)], wide.at[pl.ds(0, HALF)], 6, (lax.rem(enc + 1, 4), lon)
    )

    loads["qkv"].wait()
    norm = normed(own.astype(f32), first_gain[...])
    own_q = dot(norm, qkv_weight[:, :WIDTH])
    own_k = dot(norm, qkv_weight[:, WIDTH : 2 * WIDTH])
    own_v = dot(norm, qkv_weight[:, 2 * WIDTH :])
    row = lax.broadcasted_iota(jnp.int32, (HALO, HALF), 0)
    col = lax.broadcasted_iota(jnp.int32, (HALO, HALF), 1)
    same = lax.rem(row, 2) == lax.rem(col, 2)
    first_key = jnp.where(enc == 0, HALO, 0)
    last_key = jnp.where(enc == 3, HALO, HALF)
    ones = jnp.ones((HALF, 128), f32)
    for win in range(2):
        inside = (col >= first_key) if win == 0 else (col < last_key)
        masks[win * 2] = jnp.where(inside, 0.0, -1e30)
        masks[win * 2 + 1] = jnp.where(inside & same, 0.0, -1e30)
    copy_up.wait_recv()
    copy_down.wait_recv()
    halo = jnp.concatenate([wide[:HALF], wide[HALF + TOKENS :]], axis=0).astype(f32)
    norm = normed(halo, first_gain[...])
    halo_k = dot(norm, qkv_weight[:, WIDTH : 2 * WIDTH])
    halo_v = dot(norm, qkv_weight[:, 2 * WIDTH :])
    for win in range(2):
        for two in range(2):
            at = win * HALF + two * HALO
            rows = slice(at, at + HALO)
            for g in range(4):
                lanes = slice(g * 128, (g + 1) * 128)
                index = (win * 2 + two) * 4 + g
                qs[index] = own_q[rows, lanes]
                key = (halo_k[rows, lanes], own_k[rows, lanes])
                value = (halo_v[rows, lanes], own_v[rows, lanes])
                if win == 1:
                    key, value = key[::-1], value[::-1]
                ks[index] = jnp.concatenate(key, axis=0).astype(bf16)
                value = jnp.concatenate(value, axis=0)
                vs[index] = jnp.concatenate([value, ones], axis=1).astype(bf16)

    lane = lax.broadcasted_iota(jnp.int32, (HALO, 128), 1) // HEAD_WIDTH

    def attend(index, _):
        group = lax.rem(index, 4)
        query = qs[index]
        mask = masks[index // 4]
        stacked = [jnp.where(lane == h, query, 0.0) for h in range(4)]
        raw = dot(jnp.concatenate(stacked, axis=0).astype(bf16), ks[index], ((1,), (1,)))
        exponents = []
        for h in range(4):
            masked = raw[h * HALO : (h + 1) * HALO] + mask
            top = jnp.max(masked, axis=-1, keepdims=True)
            factor = window_temp[group * 4 + h] * (1.0 / math.sqrt(HEAD_WIDTH))
            exponents.append(jnp.exp((masked - top) * factor).astype(bf16).astype(f32))
        exponent = jnp.concatenate(exponents, axis=0).astype(bf16)
        mixed = dot(exponent, vs[index])
        above = mixed[:HALO, :128]
        under = mixed[:HALO, 128:]
        for h in range(1, 4):
            rows = slice(h * HALO, (h + 1) * HALO)
            above = jnp.where(lane == h, mixed[rows, :128], above)
            under = jnp.where(lane == h, mixed[rows, 128:], under)
        attended[index] = above / under
        return 0

    lax.fori_loop(0, 16, attend, 0, unroll=True)

    rows = [
        jnp.concatenate([attended[block * 4 + g] for g in range(4)], axis=1) for block in range(4)
    ]
    loads["proj"].wait()
    mixed = dot(jnp.concatenate(rows, axis=0).astype(bf16), proj_weight[...])
    middle = (own.astype(f32) + mixed).astype(bf16).astype(f32)
    norm = normed(middle, second_gain[...])
    norm2[...] = norm
    norm2_t[...] = norm.T
    total[...] = middle

    got = (got1, got2)
    sizes = [PART_ROWS // 4, PART_ROWS // 64]
    offsets = [0, len(combos[0])]
    starts = []
    for p in range(PARTS):
        at = [0]
        for phase in range(len(PHASES)):
            at.append(at[-1] + chunk_at(p, PHASES[phase], (0, 0)) * sizes[phase])
        starts.append(at)
    pair_id = (mate, lon)
    pair_copies = []
    stores = []
    copies = {}

    def give_pair(index, source, target):
        copy = pltpu.make_async_remote_copy(
            src_ref=source,
            dst_ref=target,
            send_sem=pair_send.at[index],
            recv_sem=pair_recv.at[index],
            device_id=pair_id,
            device_id_type=MESH,
        )
        copy.start()
        pair_copies.append(copy)
        return copy

    def ring_copy(way, p, phase, k, source, target):
        at = offsets[phase] + k
        return pltpu.make_async_remote_copy(
            src_ref=source,
            dst_ref=target,
            send_sem=ring_send.at[way, p, at],
            recv_sem=ring_recv.at[way, p, at],
            device_id=device_for(p, PHASES[phase], combos[phase][k]),
            device_id_type=MESH,
        )

    def scatter(p, phase):
        size = sizes[phase]
        for k, by in enumerate(combos[phase]):
            target = chunk_at(p, PHASES[phase], by)
            first = pl.multiple_of(starts[p][phase] + target * size, 16)
            source = work.at[p, pl.ds(first, size)]
            copy = ring_copy(0, p, phase, k, source, got[phase].at[p, k])
            copy.start()
            copies[0, p, phase, k] = copy

    def add_up(p, phase):
        for k in range(len(combos[phase])):
            copies[0, p, phase, k].wait_recv()
        size = sizes[phase]
        first = pl.multiple_of(starts[p][phase + 1], 16)
        held = work[p, pl.ds(first, size), :].astype(f32)
        for k in range(len(combos[phase])):
            held = held + got[phase][p, k].astype(f32)
        if phase == 0:
            work[p, pl.ds(first, size), :] = held.astype(bf16)
            scatter(p, 1)
        else:
            result[core, p, pl.ds(first, size), :] = held.astype(bf16)
            gather(p, 1)

    def gather(p, phase):
        first = pl.multiple_of(starts[p][phase + 1], 16)
        piece = result.at[core, p, pl.ds(first, sizes[phase])]
        for k in range(len(combos[phase])):
            copy = ring_copy(1, p, phase, k, piece, piece)
            copy.start()
            copies[1, p, phase, k] = copy

    def gathered(p, phase):
        for k, by in enumerate(combos[phase]):
            source = chunk_at(p, PHASES[phase], [4 - step for step in by])
            first = pl.multiple_of(starts[p][phase] + source * sizes[phase], 16)
            piece = result.at[core, p, pl.ds(first, sizes[phase])]
            ring_copy(1, p, phase, k, piece, piece).wait_recv()
            if phase == 0:
                give_pair(PARTS + 4 * p + 1 + k, piece, piece)
        if phase == 1:
            gather(p, 0)
            first = pl.multiple_of(starts[p][1], 16)
            piece = result.at[core, p, pl.ds(first, sizes[0])]
            give_pair(PARTS + 4 * p, piece, piece)
        else:
            store(core, p)

    def store(half, p):
        copy = pltpu.make_async_copy(result.at[half, p], whole.at[half, p], store_sem.at[len(stores)])
        copy.start()
        stores.append(copy)

    def paired(p):
        for k in range(4):
            piece = result.at[1 - core, p, pl.ds(0, sizes[0])]
            pltpu.make_async_remote_copy(
                src_ref=piece,
                dst_ref=piece,
                send_sem=pair_send.at[PARTS + 4 * p + k],
                recv_sem=pair_recv.at[PARTS + 4 * p + k],
                device_id=pair_id,
                device_id_type=MESH,
            ).wait_recv()
        store(1 - core, p)

    def mlp(j):
        columns = slice(j * 512, (j + 1) * 512)
        x = dot(norm2[...], up_weight[:, columns])
        cubic = 0.044715 * (x * x)
        scale = math.sqrt(2.0 / math.pi)
        bend = jnp.tanh(scale * (x * (1.0 + cubic)))
        hidden = (0.5 * x * (1.0 + bend)).astype(bf16)
        slope = 0.5 * (1.0 + bend) + 0.5 * x * (1.0 - bend * bend) * (scale * (1.0 + 3.0 * cubic))
        slope = (slope * back_grad[j]).astype(bf16)
        down_grad = dot(hidden, cot_shifted[...], ((0,), (0,))).astype(bf16)
        up_grad = dot(norm2_t[...], slope).astype(bf16)
        for i in range(2):
            lanes = slice(i * PART_COLS, (i + 1) * PART_COLS)
            grads[0, j, i * 512 : (i + 1) * 512] = up_grad[:, lanes]
            grads[1, j, i * 512 : (i + 1) * 512] = down_grad[:, lanes]
        total[...] += dot(hidden, down_weight[columns])

    def reduce_pair(p):
        pair_copies[p].wait_recv()
        work[p] = (grads[core, p].astype(f32) + pair[p].astype(f32)).astype(bf16)
        scatter(p, 0)

    loads["up"].wait()
    for j in range(PARTS):
        mlp(j)
        give_pair(j, grads.at[1 - core, j], pair.at[j])
        if j > 1:
            reduce_pair(j - 2)
    reduce_pair(PARTS - 2)
    done = total[...].astype(bf16)
    output[...] = done
    loads["mat5"].wait()
    leave[...] = dot(mat5[...], done).astype(bf16)
    reduce_pair(PARTS - 1)
    for p in range(PARTS):
        add_up(p, 0)
    copy_back = remote(leave, back, 7, east_id)
    for p in range(PARTS):
        add_up(p, 1)
    for p in range(PARTS):
        gathered(p, 1)
    for p in range(PARTS):
        gathered(p, 0)
    for p in range(PARTS):
        paired(p)
    copy_back.wait_recv()
    for copy in (copy_mate, copy_cot, copy_left, copy_up, copy_down, copy_back, *far_copies):
        copy.wait_send()
    for copy in pair_copies:
        copy.wait_send()
    for copy in copies.values():
        copy.wait_send()
    for copy in stores:
        copy.wait()


def main_call(
    pixels,
    ids,
    embed_weight,
    embed_bias,
    latents,
    query_weight,
    key_weight,
    value_weight,
    pool_weight,
    pool_temp,
    first_gain,
    qkv_weight,
    window_temp,
    proj_weight,
    second_gain,
    up_weight,
    down_weight,
    cot,
):
    vmem = pl.BlockSpec(memory_space=pltpu.VMEM)
    smem = pl.BlockSpec(memory_space=pltpu.SMEM)
    anywhere = pl.BlockSpec(memory_space=pl.ANY)
    matrices = [jnp.asarray(matrix, bf16) for matrix in order_matrices()]
    spread = jnp.asarray(spread_matrix(), bf16)
    loaded = (
        query_weight,
        key_weight,
        embed_weight,
        value_weight,
        pool_weight,
        spread,
        qkv_weight,
        proj_weight,
        up_weight,
        down_weight,
        cot,
        *matrices,
    )
    piece = pltpu.VMEM((HALF, WIDTH), bf16)
    part = pltpu.VMEM((PARTS, PART_ROWS, PART_COLS), bf16)
    return pl.pallas_call(
        main_kernel,
        out_shape=(
            jax.ShapeDtypeStruct((TOKENS, WIDTH), bf16),
            jax.ShapeDtypeStruct((HALF, WIDTH), bf16),
            jax.ShapeDtypeStruct((2, PARTS, PART_ROWS, PART_COLS), bf16),
        ),
        in_specs=[smem] * 3 + [vmem] * 7 + [anywhere] * len(loaded),
        out_specs=(vmem, vmem, anywhere),
        scratch_shapes=[pltpu.VMEM((2, PARTS, PART_ROWS, PART_COLS), bf16)]
        + [pltpu.VMEM(value.shape, bf16) for value in loaded]
        + [
            pltpu.VMEM((SLOTS, WIDTH), f32),
            pltpu.VMEM((4, PER, SPOTS, PIXELS), bf16),
            pltpu.VMEM((3, PER, SPOTS, PIXELS), bf16),
            pltpu.VMEM((PER, 2 * SPOTS, WIDTH), bf16),
            pltpu.VMEM((2 * PER, SPOTS, 128), f32),
            pltpu.VMEM((2 * PER, SPOTS, WIDTH), f32),
            pltpu.VMEM((STAGES, LEVELS, SPOTS, WIDTH), f32),
            pltpu.VMEM((TOKENS, WIDTH), bf16),
            piece,
            piece,
            piece,
            piece,
            pltpu.VMEM((2 * TOKENS, WIDTH), bf16),
            pltpu.VMEM((TOKENS, WIDTH), bf16),
            pltpu.VMEM((4, TOKENS, 512), f32),
            pltpu.VMEM((16, HALO, 128), f32),
            pltpu.VMEM((16, HALF, 128), bf16),
            pltpu.VMEM((16, HALF, 256), bf16),
            pltpu.VMEM((4, HALO, HALF), f32),
            pltpu.VMEM((16, HALO, 128), f32),
            pltpu.VMEM((TOKENS, WIDTH), bf16),
            pltpu.VMEM((WIDTH, TOKENS), bf16),
            pltpu.VMEM((TOKENS, WIDTH), f32),
            piece,
            pltpu.VMEM((2, PARTS, PART_ROWS, PART_COLS), bf16),
            part,
            part,
            pltpu.VMEM((PARTS, 3, PART_ROWS // 4, PART_COLS), bf16),
            pltpu.VMEM((PARTS, 15, PART_ROWS // 64, PART_COLS), bf16),
            pltpu.SemaphoreType.DMA((len(loaded),)),
            pltpu.SemaphoreType.DMA((2 * PARTS,)),
            pltpu.SemaphoreType.DMA((12,)),
            pltpu.SemaphoreType.DMA((12,)),
            pltpu.SemaphoreType.DMA((2, PARTS, 18)),
            pltpu.SemaphoreType.DMA((2, PARTS, 18)),
            pltpu.SemaphoreType.DMA((5 * PARTS,)),
            pltpu.SemaphoreType.DMA((5 * PARTS,)),
        ],
        compiler_params=pltpu.CompilerParams(
            collective_id=1, has_side_effects=True, vmem_limit_bytes=60 * 1024 * 1024
        ),
        name="main",
    )(
        ids,
        pool_temp,
        window_temp,
        pixels,
        jnp.asarray(pixel_matrix(), bf16),
        latents,
        jnp.asarray(head_rows(), f32),
        first_gain[None, :],
        second_gain[None, :],
        embed_bias,
        *loaded,
    )


def finish_kernel(
    sums,
    shifted_hbm,
    back_hbm,
    keep_hbm,
    take_hbm,
    output_hbm,
    up_hbm,
    down_hbm,
    loaded,
    up_grad,
    down_grad,
    shifted,
    back,
    keep,
    take,
    output,
    load_sem,
    store_sem,
):
    scaling = 1.0 / math.sqrt(NTOK)
    loads = []

    def load(source, target):
        loads.append(pltpu.make_async_copy(source, target, load_sem.at[len(loads)]))
        loads[-1].start()

    for p in range(PARTS):
        load(sums.at[:, p], loaded.at[p])
    load(shifted_hbm, shifted)
    load(back_hbm, back)
    load(keep_hbm, keep)
    load(take_hbm, take)
    stores = []

    def store(source, target):
        stores.append(pltpu.make_async_copy(source, target, store_sem.at[len(stores)]))
        stores[-1].start()

    for p in range(PARTS):
        loads[p].wait()
        wide = slice(p * 512, (p + 1) * 512)
        for i in range(2):
            rows = slice(i * 512, (i + 1) * 512)
            lanes = slice(i * PART_COLS, (i + 1) * PART_COLS)
            up_lanes = slice(p * 512 + i * PART_COLS, p * 512 + (i + 1) * PART_COLS)
            down_grad[wide, lanes] = loaded[p, 1, rows].astype(f32) * scaling
            up_grad[:, up_lanes] = loaded[p, 0, rows].astype(f32) * scaling
        store(down_grad.at[pl.ds(p * 512, 512)], down_hbm.at[pl.ds(p * 512, 512)])
        store(up_grad.at[:, pl.ds(p * 512, 512)], up_hbm.at[:, pl.ds(p * 512, 512)])
    for copy in loads[PARTS:]:
        copy.wait()
    whole = dot(keep[...], shifted[...]) + dot(take[...], back[...])
    output[...] = whole.reshape(SPOTS, LEVELS, WIDTH).astype(bf16)
    store(output, output_hbm)
    for copy in stores:
        copy.wait()


def finish(sums, shifted, back):
    keep, take = final_matrices()
    anywhere = pl.BlockSpec(memory_space=pl.ANY)
    return pl.pallas_call(
        finish_kernel,
        out_shape=(
            jax.ShapeDtypeStruct((SPOTS, LEVELS, WIDTH), bf16),
            jax.ShapeDtypeStruct((WIDTH, FF), f32),
            jax.ShapeDtypeStruct((FF, WIDTH), f32),
        ),
        in_specs=[anywhere] * 5,
        out_specs=(anywhere, anywhere, anywhere),
        scratch_shapes=[
            pltpu.VMEM((PARTS, 2, PART_ROWS, PART_COLS), bf16),
            pltpu.VMEM((WIDTH, FF), f32),
            pltpu.VMEM((FF, WIDTH), f32),
            pltpu.VMEM((TOKENS, WIDTH), bf16),
            pltpu.VMEM((HALF, WIDTH), bf16),
            pltpu.VMEM((TOKENS, TOKENS), bf16),
            pltpu.VMEM((TOKENS, HALF), bf16),
            pltpu.VMEM((SPOTS, LEVELS, WIDTH), bf16),
            pltpu.SemaphoreType.DMA((PARTS + 4,)),
            pltpu.SemaphoreType.DMA((2 * PARTS + 1,)),
        ],
        compiler_params=pltpu.CompilerParams(vmem_limit_bytes=60 * 1024 * 1024),
        name="finish",
    )(
        sums,
        shifted,
        back,
        jnp.asarray(keep, bf16),
        jnp.asarray(take, bf16),
    )


def per_device(
    pixel_field,
    level_ids,
    embed_weight,
    embed_bias,
    latents,
    query_weight,
    key_weight,
    value_weight,
    pool_weight,
    pool_temp,
    first_gain,
    qkv_weight,
    window_temp,
    proj_weight,
    second_gain,
    up_weight,
    down_weight,
    cotangent,
):
    cot = jnp.transpose(cotangent, (1, 2, 0, 3)).reshape(SPOTS, LEVELS, WIDTH)
    shifted, back, sums = main_call(
        jnp.transpose(pixel_field, (0, 3, 1, 2)),
        level_ids,
        embed_weight,
        embed_bias,
        latents,
        query_weight,
        key_weight,
        value_weight,
        pool_weight,
        pool_temp,
        first_gain,
        qkv_weight,
        window_temp,
        proj_weight,
        second_gain,
        up_weight,
        down_weight,
        cot,
    )
    output, up_grad, down_grad = finish(sums, shifted, back)
    output = output.reshape(ROWS, COLS, LEVELS, WIDTH)
    return (jnp.transpose(output, (2, 0, 1, 3)), up_grad, down_grad)


def solution(mesh):
    placed = (P("enc", None, None, "lon"),) + (P(),) * 16 + (P(None, "enc", "lon", None),)
    return jax.shard_map(
        per_device,
        mesh=mesh,
        in_specs=placed,
        out_specs=(P(None, "enc", "lon", None), P(), P()),
        check_vma=False,
    )
```

```python
import itertools
import math

import jax
import jax.numpy as jnp
import numpy as np
from jax import lax
from jax.experimental import pallas as pl
from jax.experimental.pallas import tpu as pltpu
from jax.sharding import PartitionSpec as P

SLOTS = 52
HEADS = 16
HEAD_WIDTH = 32
WIDTH = 512
FF = 2048
LEVELS = 4
ROWS = 6
COLS = 12
SPOTS = ROWS * COLS
TOKENS = LEVELS * SPOTS
HALF = TOKENS // 2
PIXELS = 100
PER = SLOTS // 4
FAR = 7
EPSILON = 1e-05
NTOK = 36864
PARTS = 4
PART_ROWS = 1024
PART_COLS = 256
HALO = HALF // 2
LEAD = 40
STAGES = 3
PHASES = ((0,), (1, 2))
MESH = pl.DeviceIdType.MESH

f32 = jnp.float32
bf16 = jnp.bfloat16


def dot(a, b, contract=((1,), (0,))):
    return lax.dot_general(a, b, (contract, ((), ())), preferred_element_type=f32)


def normed(values, gain):
    mean = jnp.mean(values, axis=-1, keepdims=True)
    centred = values - mean
    variance = jnp.mean(centred * centred, axis=-1, keepdims=True)
    return (centred * lax.rsqrt(variance + EPSILON) * gain).astype(bf16)


def pooled_at(r, c, l):
    spot = c * ROWS + r
    if spot < LEAD:
        return l * LEAD + spot
    return LEVELS * LEAD + l * (SPOTS - LEAD) + spot - LEAD


def piece_at(r, c, l):
    return (r * (COLS // 2) + c) * LEVELS + l


def natural_at(r, c, l):
    return (r * COLS + c) * LEVELS + l


def shifted_at(r, c, l):
    pair, place = ((1, 0), (0, 0), (0, 1), (1, 1))[l]
    return (r // 3) * HALF + pair * HALO + ((r % 3) * COLS + c) * 2 + place


def matrix_of(rows, cols, entries):
    matrix = np.zeros((rows, cols), np.float32)
    for r in range(ROWS):
        for c in range(COLS // 2):
            for l in range(LEVELS):
                matrix[entries(r, c, l)] = 1.0
    return matrix


def order_matrices():
    half = COLS // 2
    return (
        matrix_of(HALF, LEVELS * LEAD, lambda r, c, l: (piece_at(r, c, l), pooled_at(r, c, l))),
        matrix_of(TOKENS, TOKENS, lambda r, c, l: (shifted_at(r, c, l), pooled_at(r, half + c, l))),
        matrix_of(HALF, TOKENS, lambda r, c, l: (piece_at(r, c, l), natural_at(r, c, l))),
        matrix_of(TOKENS, TOKENS, lambda r, c, l: (shifted_at(r, c, l), natural_at(r, half + c, l))),
        matrix_of(TOKENS, HALF, lambda r, c, l: (shifted_at(r, half + c, l), piece_at(r, c, l))),
        matrix_of(HALF, TOKENS, lambda r, c, l: (piece_at(r, c, l), shifted_at(r, half + c, l))),
    )


def final_matrices():
    half = COLS // 2
    return (
        matrix_of(TOKENS, TOKENS, lambda r, c, l: (natural_at(r, half + c, l), shifted_at(r, c, l))),
        matrix_of(TOKENS, HALF, lambda r, c, l: (natural_at(r, c, l), piece_at(r, c, l))),
    )


def pixel_matrix():
    matrix = np.zeros((4 * SPOTS, 4 * SPOTS), np.float32)
    for owner in range(4):
        for c in range(COLS):
            for r in range(ROWS):
                matrix[owner * SPOTS + c * ROWS + r, c * 4 * ROWS + owner * ROWS + r] = 1.0
    return matrix


def head_rows():
    mask = np.zeros((HEADS, WIDTH), np.float32)
    for h in range(HEADS):
        mask[h, h * HEAD_WIDTH : (h + 1) * HEAD_WIDTH] = 1.0
    return mask


def spread_matrix():
    one = np.zeros((LEVELS * HEADS, LEVELS * WIDTH), np.float32)
    for l in range(LEVELS):
        for h in range(HEADS):
            at = l * WIDTH + h * HEAD_WIDTH
            one[l * HEADS + h, at : at + HEAD_WIDTH] = 1.0
    return np.concatenate([one, one], axis=0)


def mesh_id(x, y, z, core):
    return (lax.rem(y, 2) * 2 + core, x * 8 + z * 2 + y // 2)


def split_parts(values):
    first = lax.broadcasted_iota(jnp.int32, values.shape, 1) < 64
    high = values.astype(bf16).astype(f32)
    return jnp.where(first, high, values - high).astype(bf16)


def main_kernel(
    ids,
    pool_temp,
    window_temp,
    pixels,
    pixel_order,
    latents,
    heads,
    first_gain,
    second_gain,
    embed_bias,
    query_hbm,
    key_hbm,
    embed_hbm,
    value_hbm,
    pool_hbm,
    spread_hbm,
    qkv_hbm,
    proj_hbm,
    up_hbm,
    down_hbm,
    cot_hbm,
    mat0_hbm,
    mat1_hbm,
    mat2_hbm,
    mat3_hbm,
    mat4_hbm,
    mat5_hbm,
    output,
    back,
    whole,
    result,
    query_weight,
    key_weight,
    embed_weight,
    value_weight,
    pool_weight,
    spread,
    qkv_weight,
    proj_weight,
    up_weight,
    down_weight,
    cotangent,
    mat0,
    mat1,
    mat2,
    mat3,
    mat4,
    mat5,
    bias,
    outgoing,
    arrived,
    tokens,
    scores,
    values,
    sums,
    own_cot,
    cot_left,
    cot_east,
    left,
    east,
    wide,
    cot_shifted,
    back_grad,
    qs,
    ks,
    vs,
    masks,
    attended,
    norm2,
    norm2_t,
    total,
    hiddens,
    leave,
    grads,
    pair,
    work,
    got1,
    got2,
    load_sem,
    store_sem,
    send,
    recv,
    ring_send,
    ring_recv,
    pair_send,
    pair_recv,
):
    enc = lax.axis_index("enc")
    lon = lax.axis_index("lon")
    mate = enc + 1 - 2 * lax.rem(enc, 2)
    peers = (mate, lax.rem(enc + 2, 4), lax.rem(mate + 2, 4))
    west_id = (enc, lax.rem(lon + 31, 32))
    east_id = (enc, lax.rem(lon + 1, 32))
    core = lax.rem(enc, 2)
    x_at = lon // 8
    y_at = lax.rem(lon, 2) * 2 + enc // 2
    z_at = lax.rem(lon // 2, 4)

    places = [[lax.rem(at + by, 4) for by in range(4)] for at in (x_at, y_at, z_at)]
    x_part = [place * 8 for place in places[0]]
    y_part = [place // 2 for place in places[1]]
    z_part = [place * 2 for place in places[2]]
    enc_part = [lax.rem(place, 2) * 2 + core for place in places[1]]

    def device_at(step):
        return enc_part[step[1]], x_part[step[0]] + y_part[step[1]] + z_part[step[2]]

    def by_core(first, second):
        return first + core * (second - first)

    def step_of(part, way, phase, by):
        step = [0, 0, 0]
        for dim, count in zip(phase, by):
            step[(part + way + dim) % 3] = count
        return tuple(step)

    def chunk_for(part, way, phase, by):
        chunk = 0
        for dim, count in zip(phase, by):
            chunk = chunk * 4 + places[(part + way + dim) % 3][count % 4]
        return chunk

    def chunk_at(part, phase, by):
        return by_core(*[chunk_for(part, way, phase, by) for way in range(2)])

    combos = [
        sorted(
            [by for by in itertools.product(range(4), repeat=len(phase)) if any(by)],
            key=lambda by: -sum(min(count, 4 - count) for count in by),
        )
        for phase in PHASES
    ]
    others = sorted(
        {
            step_of(turn, 0, phase, by)
            for turn in range(3)
            for phase, bys in zip(PHASES, combos)
            for by in bys
        }
    )
    devices = {step: device_at(step) for step in others}

    def device_for(part, phase, by):
        near, far = [devices[step_of(part, way, phase, by)] for way in range(2)]
        return by_core(near[0], far[0]), by_core(near[1], far[1])

    barrier = pltpu.get_barrier_semaphore()
    for peer in peers:
        pl.semaphore_signal(barrier, inc=1, device_id=(peer, lon), device_id_type=MESH)
    for other in (west_id, east_id):
        pl.semaphore_signal(barrier, inc=1, device_id=other, device_id_type=MESH)
    for step in others:
        pl.semaphore_signal(barrier, inc=1, device_id=devices[step], device_id_type=MESH)

    loads = {}
    for index, (name, source, target) in enumerate(
        (
            ("query", query_hbm, query_weight),
            ("key", key_hbm, key_weight),
            ("cot", cot_hbm, cotangent),
            ("mat2", mat2_hbm, mat2),
            ("embed", embed_hbm, embed_weight),
            ("value", value_hbm, value_weight),
            ("spread", spread_hbm, spread),
            ("pool", pool_hbm, pool_weight),
            ("mat0", mat0_hbm, mat0),
            ("mat1", mat1_hbm, mat1),
            ("mat3", mat3_hbm, mat3),
            ("mat4", mat4_hbm, mat4),
            ("mat5", mat5_hbm, mat5),
            ("down", down_hbm, down_weight),
            ("qkv", qkv_hbm, qkv_weight),
            ("proj", proj_hbm, proj_weight),
            ("up", up_hbm, up_weight),
        )
    ):
        loads[name] = pltpu.make_async_copy(source, target, load_sem.at[index])
        loads[name].start()

    def remote(source, target, index, device):
        copy = pltpu.make_async_remote_copy(
            src_ref=source,
            dst_ref=target,
            send_sem=send.at[index],
            recv_sem=recv.at[index],
            device_id=device,
            device_id_type=MESH,
        )
        copy.start()
        return copy

    def sort_pixels(slot, _):
        block = pixels[slot].astype(f32).reshape(4 * SPOTS, PIXELS).astype(bf16)
        block = dot(pixel_order[...], block).astype(bf16).astype(f32)
        for owner in range(4):
            outgoing[owner, slot] = block[owner * SPOTS : (owner + 1) * SPOTS].astype(bf16)
        return 0

    far_copies = []

    def send_far(k, first, count):
        slots_there = pl.ds(first, count)
        for i in (1, 2):
            far_copies.append(
                remote(
                    outgoing.at[peers[i], slots_there],
                    arrived.at[i, slots_there],
                    7 + 2 * k + i,
                    (peers[i], lon),
                )
            )

    lax.fori_loop(0, FAR, sort_pixels, 0, unroll=True)
    pl.semaphore_wait(barrier, 5 + len(others))
    send_far(0, 0, FAR)
    lax.fori_loop(FAR, PER, sort_pixels, 0, unroll=True)
    copy_mate = remote(outgoing.at[peers[0]], arrived.at[0], 0, (peers[0], lon))
    send_far(1, FAR, PER - FAR)

    bias[...] = embed_bias[...].astype(f32)
    loads["query"].wait()
    loads["key"].wait()
    queries = dot(latents[...], query_weight[...]).astype(bf16).astype(f32)
    blocks = [queries[l : l + 1] * heads[...] for l in range(LEVELS)]
    blocks = jnp.concatenate(blocks, axis=0).astype(bf16)
    head_of = lax.rem(lax.broadcasted_iota(jnp.int32, (LEVELS * HEADS, 1), 0), HEADS)
    temp = jnp.zeros((LEVELS * HEADS, 1), f32)
    for h in range(HEADS):
        temp = jnp.where(head_of == h, pool_temp[h] * (1.0 / math.sqrt(HEAD_WIDTH)), temp)
    folded = dot(blocks, key_weight[...], ((1,), (1,))) * temp
    high = folded.astype(bf16)
    low = (folded - high.astype(f32)).astype(bf16)
    keys = jnp.concatenate([high, high, low, low], axis=0)

    def token_of(block, slot):
        level = ids[slot]
        return dot(block, embed_weight[level]) + bias[pl.ds(level, 1), :]

    def embed_near(i, _):
        near = token_of(outgoing[enc, i], enc * PER + i)
        far = token_of(arrived[0, i], mate * PER + i)
        tokens[i] = jnp.concatenate([near, far], axis=0).astype(bf16)
        return 0

    def embed_far(first):
        def embed(i, _):
            near = token_of(arrived[1, first + i], peers[1] * PER + first + i)
            far = token_of(arrived[2, first + i], peers[2] * PER + first + i)
            tokens[i] = jnp.concatenate([near, far], axis=0).astype(bf16)
            return 0

        return embed

    def project(first, count):
        block = jnp.concatenate([tokens[first + i] for i in range(count)], axis=0)
        projected = dot(block, value_weight[...])
        scored = dot(block, keys, ((1,), (1,)))
        scored = scored[:, :128] + scored[:, 128:]
        for i in range(2 * count):
            values[first * 2 + i] = projected[i * SPOTS : (i + 1) * SPOTS]
            scores[first * 2 + i] = scored[i * SPOTS : (i + 1) * SPOTS]

    def project_two(i, _):
        project(2 * i, 2)
        return 0

    def mix(stage, first, count, lo, hi):
        probs = jnp.concatenate([scores[first + i, lo:hi] for i in range(count)], axis=0)
        split = split_parts(probs)
        size = hi - lo
        for l in range(LEVELS):
            wider = dot(split, spread[:, l * WIDTH : (l + 1) * WIDTH])
            part = sums[stage, l, lo:hi]
            for i in range(count):
                part = part + wider[i * size : (i + 1) * size] * values[first + i, lo:hi]
            sums[stage, l, lo:hi] = part

    def mix_all(stage, pairs, lo, hi):
        def mix_four(i, _):
            mix(stage, 4 * i, 4, lo, hi)
            return 0

        lax.fori_loop(0, pairs // 2, mix_four, 0, unroll=True)
        if pairs % 2:
            mix(stage, 2 * pairs - 2, 2, lo, hi)

    def pool_stage(stage, pairs, embed):
        lax.fori_loop(0, pairs, embed, 0, unroll=True)
        if stage == 0:
            loads["value"].wait()
        lax.fori_loop(0, pairs // 2, project_two, 0, unroll=True)
        if pairs % 2:
            project(pairs - 1, 1)
        peak = scores[0]
        for s in range(1, 2 * pairs):
            peak = jnp.maximum(peak, scores[s])
        weight = jnp.zeros_like(peak)
        for s in range(2 * pairs):
            exponent = jnp.exp(scores[s] - peak)
            scores[s] = exponent
            weight = weight + exponent
        sums[stage] = jnp.zeros((LEVELS, SPOTS, WIDTH), f32)
        return peak, weight

    loads["cot"].wait()
    loads["mat2"].wait()
    own_cot[...] = cotangent[...].astype(f32).reshape(TOKENS, WIDTH).astype(bf16)
    cot_left[...] = dot(mat2[...], own_cot[...]).astype(bf16)
    loads["embed"].wait()
    copy_mate.wait_recv()
    stats = [pool_stage(0, PER, embed_near)]
    loads["spread"].wait()
    mix_all(0, PER, 0, SPOTS)
    far_copies[0].wait_recv()
    far_copies[1].wait_recv()
    stats.append(pool_stage(1, FAR, embed_far(0)))
    mix_all(1, FAR, 0, SPOTS)
    far_copies[2].wait_recv()
    far_copies[3].wait_recv()
    copy_cot = remote(cot_left, cot_east, 3, west_id)
    stats.append(pool_stage(2, PER - FAR, embed_far(FAR)))

    peak = stats[0][0]
    for other, _ in stats[1:]:
        peak = jnp.maximum(peak, other)
    decays = [jnp.exp(top - peak) for top, _ in stats]
    inverse = 1.0 / sum(weight * decay for decay, (_, weight) in zip(decays, stats))
    decays = [decay * inverse for decay in decays]
    loads["pool"].wait()

    def finish_pool(lo, hi):
        shares = split_parts(jnp.concatenate([decay[lo:hi] for decay in decays], axis=0))
        size = hi - lo
        pooled = []
        for l in range(LEVELS):
            share = dot(shares, spread[:, l * WIDTH : (l + 1) * WIDTH])
            level = share[:size] * sums[0, l, lo:hi]
            for k in range(1, STAGES):
                level = level + share[k * size : (k + 1) * size] * sums[k, l, lo:hi]
            pooled.append(level)
        projected = dot(jnp.concatenate(pooled, axis=0).astype(bf16), pool_weight[...])
        rows = [
            projected[l * size : (l + 1) * size] + latents[l : l + 1].astype(f32)
            for l in range(LEVELS)
        ]
        return jnp.concatenate(rows, axis=0).astype(bf16)

    mix_all(2, PER - FAR, 0, LEAD)
    lead = finish_pool(0, LEAD)
    loads["mat0"].wait()
    left[...] = dot(mat0[...], lead).astype(bf16)
    copy_left = remote(left, east, 4, west_id)
    mix_all(2, PER - FAR, LEAD, SPOTS)
    stream = jnp.concatenate([lead, finish_pool(LEAD, SPOTS)], axis=0)
    loads["mat1"].wait()
    kept = dot(mat1[...], stream)
    copy_cot.wait_recv()
    loads["mat3"].wait()
    loads["mat4"].wait()
    cot = (dot(mat3[...], own_cot[...]) + dot(mat4[...], cot_east[...])).astype(bf16)
    cot_shifted[...] = cot
    loads["down"].wait()
    for j in range(4):
        back_grad[j] = dot(cot, down_weight[j * 512 : (j + 1) * 512], ((1,), (1,)))
    copy_left.wait_recv()
    own = (kept + dot(mat4[...], east[...])).astype(bf16)
    wide[HALF : HALF + TOKENS] = own
    copy_up = remote(
        wide.at[pl.ds(HALF, HALF)],
        wide.at[pl.ds(HALF + TOKENS, HALF)],
        5,
        (lax.rem(enc + 3, 4), lon),
    )
    copy_down = remote(
        wide.at[pl.ds(TOKENS, HALF)], wide.at[pl.ds(0, HALF)], 6, (lax.rem(enc + 1, 4), lon)
    )

    loads["qkv"].wait()
    norm = normed(own.astype(f32), first_gain[...])
    own_q = dot(norm, qkv_weight[:, :WIDTH])
    own_k = dot(norm, qkv_weight[:, WIDTH : 2 * WIDTH])
    own_v = dot(norm, qkv_weight[:, 2 * WIDTH :])
    row = lax.broadcasted_iota(jnp.int32, (HALO, HALF), 0)
    col = lax.broadcasted_iota(jnp.int32, (HALO, HALF), 1)
    same = lax.rem(row, 2) == lax.rem(col, 2)
    first_key = jnp.where(enc == 0, HALO, 0)
    last_key = jnp.where(enc == 3, HALO, HALF)
    ones = jnp.ones((HALF, 128), f32)
    for win in range(2):
        inside = (col >= first_key) if win == 0 else (col < last_key)
        masks[win * 2] = jnp.where(inside, 0.0, -1e30)
        masks[win * 2 + 1] = jnp.where(inside & same, 0.0, -1e30)
    copy_up.wait_recv()
    copy_down.wait_recv()
    halo = jnp.concatenate([wide[:HALF], wide[HALF + TOKENS :]], axis=0).astype(f32)
    norm = normed(halo, first_gain[...])
    halo_k = dot(norm, qkv_weight[:, WIDTH : 2 * WIDTH])
    halo_v = dot(norm, qkv_weight[:, 2 * WIDTH :])
    for win in range(2):
        for two in range(2):
            at = win * HALF + two * HALO
            rows = slice(at, at + HALO)
            for g in range(4):
                lanes = slice(g * 128, (g + 1) * 128)
                index = (win * 2 + two) * 4 + g
                qs[index] = own_q[rows, lanes]
                key = (halo_k[rows, lanes], own_k[rows, lanes])
                value = (halo_v[rows, lanes], own_v[rows, lanes])
                if win == 1:
                    key, value = key[::-1], value[::-1]
                ks[index] = jnp.concatenate(key, axis=0).astype(bf16)
                value = jnp.concatenate(value, axis=0)
                vs[index] = jnp.concatenate([value, ones], axis=1).astype(bf16)

    lane = lax.broadcasted_iota(jnp.int32, (HALO, 128), 1) // HEAD_WIDTH

    def attend(index, _):
        group = lax.rem(index, 4)
        query = qs[index]
        mask = masks[index // 4]
        stacked = [jnp.where(lane == h, query, 0.0) for h in range(4)]
        raw = dot(jnp.concatenate(stacked, axis=0).astype(bf16), ks[index], ((1,), (1,)))
        exponents = []
        for h in range(4):
            masked = raw[h * HALO : (h + 1) * HALO] + mask
            top = jnp.max(masked, axis=-1, keepdims=True)
            factor = window_temp[group * 4 + h] * (1.0 / math.sqrt(HEAD_WIDTH))
            exponents.append(jnp.exp((masked - top) * factor).astype(bf16).astype(f32))
        exponent = jnp.concatenate(exponents, axis=0).astype(bf16)
        mixed = dot(exponent, vs[index])
        above = mixed[:HALO, :128]
        under = mixed[:HALO, 128:]
        for h in range(1, 4):
            rows = slice(h * HALO, (h + 1) * HALO)
            above = jnp.where(lane == h, mixed[rows, :128], above)
            under = jnp.where(lane == h, mixed[rows, 128:], under)
        attended[index] = above / under
        return 0

    lax.fori_loop(0, 16, attend, 0, unroll=True)

    rows = [
        jnp.concatenate([attended[block * 4 + g] for g in range(4)], axis=1) for block in range(4)
    ]
    loads["proj"].wait()
    mixed = dot(jnp.concatenate(rows, axis=0).astype(bf16), proj_weight[...])
    middle = (own.astype(f32) + mixed).astype(bf16).astype(f32)
    norm = normed(middle, second_gain[...])
    norm2[...] = norm
    norm2_t[...] = norm.T
    total[...] = middle

    got = (got1, got2)
    sizes = [PART_ROWS // 4, PART_ROWS // 64]
    offsets = [0, len(combos[0])]
    starts = []
    for p in range(PARTS):
        at = [0]
        for phase in range(len(PHASES)):
            at.append(at[-1] + chunk_at(p, PHASES[phase], (0, 0)) * sizes[phase])
        starts.append(at)
    pair_id = (mate, lon)
    pair_copies = []
    stores = []
    copies = {}

    def give_pair(index, source, target):
        copy = pltpu.make_async_remote_copy(
            src_ref=source,
            dst_ref=target,
            send_sem=pair_send.at[index],
            recv_sem=pair_recv.at[index],
            device_id=pair_id,
            device_id_type=MESH,
        )
        copy.start()
        pair_copies.append(copy)
        return copy

    def ring_copy(way, p, phase, k, source, target):
        at = offsets[phase] + k
        return pltpu.make_async_remote_copy(
            src_ref=source,
            dst_ref=target,
            send_sem=ring_send.at[way, p, at],
            recv_sem=ring_recv.at[way, p, at],
            device_id=device_for(p, PHASES[phase], combos[phase][k]),
            device_id_type=MESH,
        )

    def scatter(p, phase, make=None):
        size = sizes[phase]
        for k, by in enumerate(combos[phase]):
            target = chunk_at(p, PHASES[phase], by)
            first = pl.multiple_of(starts[p][phase] + target * size, 16)
            if make is not None:
                make(pl.ds(first, size))
            source = work.at[p, pl.ds(first, size)]
            copy = ring_copy(0, p, phase, k, source, got[phase].at[p, k])
            copy.start()
            copies[0, p, phase, k] = copy

    def add_up(p, phase):
        for k in range(len(combos[phase])):
            copies[0, p, phase, k].wait_recv()
        size = sizes[phase]
        first = pl.multiple_of(starts[p][phase + 1], 16)
        held = work[p, pl.ds(first, size), :].astype(f32)
        for k in range(len(combos[phase])):
            held = held + got[phase][p, k].astype(f32)
        if phase == 0:
            work[p, pl.ds(first, size), :] = held.astype(bf16)
            scatter(p, 1)
        else:
            result[core, p, pl.ds(first, size), :] = held.astype(bf16)
            gather(p, 1)

    def gather(p, phase):
        first = pl.multiple_of(starts[p][phase + 1], 16)
        piece = result.at[core, p, pl.ds(first, sizes[phase])]
        for k in range(len(combos[phase])):
            copy = ring_copy(1, p, phase, k, piece, piece)
            copy.start()
            copies[1, p, phase, k] = copy

    def gathered(p, phase):
        for k, by in enumerate(combos[phase]):
            source = chunk_at(p, PHASES[phase], [4 - step for step in by])
            first = pl.multiple_of(starts[p][phase] + source * sizes[phase], 16)
            piece = result.at[core, p, pl.ds(first, sizes[phase])]
            ring_copy(1, p, phase, k, piece, piece).wait_recv()
            if phase == 0:
                give_pair(PARTS + 4 * p + 1 + k, piece, piece)
        if phase == 1:
            gather(p, 0)
            first = pl.multiple_of(starts[p][1], 16)
            piece = result.at[core, p, pl.ds(first, sizes[0])]
            give_pair(PARTS + 4 * p, piece, piece)
        else:
            store(core, p)

    def store(half, p):
        copy = pltpu.make_async_copy(result.at[half, p], whole.at[half, p], store_sem.at[len(stores)])
        copy.start()
        stores.append(copy)

    def paired(p):
        for k in range(4):
            piece = result.at[1 - core, p, pl.ds(0, sizes[0])]
            pltpu.make_async_remote_copy(
                src_ref=piece,
                dst_ref=piece,
                send_sem=pair_send.at[PARTS + 4 * p + k],
                recv_sem=pair_recv.at[PARTS + 4 * p + k],
                device_id=pair_id,
                device_id_type=MESH,
            ).wait_recv()
        store(1 - core, p)

    def mlp(j):
        columns = slice(j * 512, (j + 1) * 512)
        x = dot(norm2[...], up_weight[:, columns])
        cubic = 0.044715 * (x * x)
        scale = math.sqrt(2.0 / math.pi)
        bend = jnp.tanh(scale * (x * (1.0 + cubic)))
        hidden = (0.5 * x * (1.0 + bend)).astype(bf16)
        hiddens[j] = hidden
        slope = 0.5 * (1.0 + bend) + 0.5 * x * (1.0 - bend * bend) * (scale * (1.0 + 3.0 * cubic))
        slope = (slope * back_grad[j]).astype(bf16)
        down_grad = dot(hidden, cot_shifted[...], ((0,), (0,))).astype(bf16)
        up_grad = dot(norm2_t[...], slope).astype(bf16)
        for i in range(2):
            lanes = slice(i * PART_COLS, (i + 1) * PART_COLS)
            grads[0, j, i * 512 : (i + 1) * 512] = up_grad[:, lanes]
            grads[1, j, i * 512 : (i + 1) * 512] = down_grad[:, lanes]

    def reduce_pair(p):
        pair_copies[p].wait_recv()

        def both(rows):
            work[p, rows, :] = (grads[core, p, rows, :].astype(f32) + pair[p, rows, :].astype(f32)).astype(bf16)

        scatter(p, 0, both)
        both(pl.ds(pl.multiple_of(starts[p][1], 16), sizes[0]))

    loads["up"].wait()
    for j in range(PARTS):
        mlp(j)
        give_pair(j, grads.at[1 - core, j], pair.at[j])
        if j > 1:
            reduce_pair(j - 2)
    reduce_pair(PARTS - 2)
    reduce_pair(PARTS - 1)
    done = total[...]
    for j in range(PARTS):
        done = done + dot(hiddens[j], down_weight[j * 512 : (j + 1) * 512])
    done = done.astype(bf16)
    output[...] = done
    loads["mat5"].wait()
    leave[...] = dot(mat5[...], done).astype(bf16)
    for p in range(PARTS):
        add_up(p, 0)
    copy_back = remote(leave, back, 7, east_id)
    for p in range(PARTS):
        add_up(p, 1)
    for p in range(PARTS):
        gathered(p, 1)
    for p in range(PARTS):
        gathered(p, 0)
    for p in range(PARTS):
        paired(p)
    copy_back.wait_recv()
    for copy in (copy_mate, copy_cot, copy_left, copy_up, copy_down, copy_back, *far_copies):
        copy.wait_send()
    for copy in pair_copies:
        copy.wait_send()
    for copy in copies.values():
        copy.wait_send()
    for copy in stores:
        copy.wait()


def main_call(
    pixels,
    ids,
    embed_weight,
    embed_bias,
    latents,
    query_weight,
    key_weight,
    value_weight,
    pool_weight,
    pool_temp,
    first_gain,
    qkv_weight,
    window_temp,
    proj_weight,
    second_gain,
    up_weight,
    down_weight,
    cot,
):
    vmem = pl.BlockSpec(memory_space=pltpu.VMEM)
    smem = pl.BlockSpec(memory_space=pltpu.SMEM)
    anywhere = pl.BlockSpec(memory_space=pl.ANY)
    matrices = [jnp.asarray(matrix, bf16) for matrix in order_matrices()]
    spread = jnp.asarray(spread_matrix(), bf16)
    loaded = (
        query_weight,
        key_weight,
        embed_weight,
        value_weight,
        pool_weight,
        spread,
        qkv_weight,
        proj_weight,
        up_weight,
        down_weight,
        cot,
        *matrices,
    )
    piece = pltpu.VMEM((HALF, WIDTH), bf16)
    part = pltpu.VMEM((PARTS, PART_ROWS, PART_COLS), bf16)
    return pl.pallas_call(
        main_kernel,
        out_shape=(
            jax.ShapeDtypeStruct((TOKENS, WIDTH), bf16),
            jax.ShapeDtypeStruct((HALF, WIDTH), bf16),
            jax.ShapeDtypeStruct((2, PARTS, PART_ROWS, PART_COLS), bf16),
        ),
        in_specs=[smem] * 3 + [vmem] * 7 + [anywhere] * len(loaded),
        out_specs=(vmem, vmem, anywhere),
        scratch_shapes=[pltpu.VMEM((2, PARTS, PART_ROWS, PART_COLS), bf16)]
        + [pltpu.VMEM(value.shape, bf16) for value in loaded]
        + [
            pltpu.VMEM((SLOTS, WIDTH), f32),
            pltpu.VMEM((4, PER, SPOTS, PIXELS), bf16),
            pltpu.VMEM((3, PER, SPOTS, PIXELS), bf16),
            pltpu.VMEM((PER, 2 * SPOTS, WIDTH), bf16),
            pltpu.VMEM((2 * PER, SPOTS, 128), f32),
            pltpu.VMEM((2 * PER, SPOTS, WIDTH), f32),
            pltpu.VMEM((STAGES, LEVELS, SPOTS, WIDTH), f32),
            pltpu.VMEM((TOKENS, WIDTH), bf16),
            piece,
            piece,
            piece,
            piece,
            pltpu.VMEM((2 * TOKENS, WIDTH), bf16),
            pltpu.VMEM((TOKENS, WIDTH), bf16),
            pltpu.VMEM((4, TOKENS, 512), f32),
            pltpu.VMEM((16, HALO, 128), f32),
            pltpu.VMEM((16, HALF, 128), bf16),
            pltpu.VMEM((16, HALF, 256), bf16),
            pltpu.VMEM((4, HALO, HALF), f32),
            pltpu.VMEM((16, HALO, 128), f32),
            pltpu.VMEM((TOKENS, WIDTH), bf16),
            pltpu.VMEM((WIDTH, TOKENS), bf16),
            pltpu.VMEM((TOKENS, WIDTH), f32),
            pltpu.VMEM((PARTS, TOKENS, 512), bf16),
            piece,
            pltpu.VMEM((2, PARTS, PART_ROWS, PART_COLS), bf16),
            part,
            part,
            pltpu.VMEM((PARTS, 3, PART_ROWS // 4, PART_COLS), bf16),
            pltpu.VMEM((PARTS, 15, PART_ROWS // 64, PART_COLS), bf16),
            pltpu.SemaphoreType.DMA((len(loaded),)),
            pltpu.SemaphoreType.DMA((2 * PARTS,)),
            pltpu.SemaphoreType.DMA((12,)),
            pltpu.SemaphoreType.DMA((12,)),
            pltpu.SemaphoreType.DMA((2, PARTS, 18)),
            pltpu.SemaphoreType.DMA((2, PARTS, 18)),
            pltpu.SemaphoreType.DMA((5 * PARTS,)),
            pltpu.SemaphoreType.DMA((5 * PARTS,)),
        ],
        compiler_params=pltpu.CompilerParams(
            collective_id=1, has_side_effects=True, vmem_limit_bytes=60 * 1024 * 1024
        ),
        name="main",
    )(
        ids,
        pool_temp,
        window_temp,
        pixels,
        jnp.asarray(pixel_matrix(), bf16),
        latents,
        jnp.asarray(head_rows(), f32),
        first_gain[None, :],
        second_gain[None, :],
        embed_bias,
        *loaded,
    )


def finish_kernel(
    sums,
    shifted_hbm,
    back_hbm,
    keep_hbm,
    take_hbm,
    output_hbm,
    up_hbm,
    down_hbm,
    loaded,
    up_grad,
    down_grad,
    shifted,
    back,
    keep,
    take,
    output,
    load_sem,
    store_sem,
):
    scaling = 1.0 / math.sqrt(NTOK)
    loads = []

    def load(source, target):
        loads.append(pltpu.make_async_copy(source, target, load_sem.at[len(loads)]))
        loads[-1].start()

    for p in range(PARTS):
        load(sums.at[:, p], loaded.at[p])
    load(shifted_hbm, shifted)
    load(back_hbm, back)
    load(keep_hbm, keep)
    load(take_hbm, take)
    stores = []

    def store(source, target):
        stores.append(pltpu.make_async_copy(source, target, store_sem.at[len(stores)]))
        stores[-1].start()

    for p in range(PARTS):
        loads[p].wait()
        wide = slice(p * 512, (p + 1) * 512)
        for i in range(2):
            rows = slice(i * 512, (i + 1) * 512)
            lanes = slice(i * PART_COLS, (i + 1) * PART_COLS)
            up_lanes = slice(p * 512 + i * PART_COLS, p * 512 + (i + 1) * PART_COLS)
            down_grad[wide, lanes] = loaded[p, 1, rows].astype(f32) * scaling
            up_grad[:, up_lanes] = loaded[p, 0, rows].astype(f32) * scaling
        store(down_grad.at[pl.ds(p * 512, 512)], down_hbm.at[pl.ds(p * 512, 512)])
        store(up_grad.at[:, pl.ds(p * 512, 512)], up_hbm.at[:, pl.ds(p * 512, 512)])
    for copy in loads[PARTS:]:
        copy.wait()
    whole = dot(keep[...], shifted[...]) + dot(take[...], back[...])
    output[...] = whole.reshape(SPOTS, LEVELS, WIDTH).astype(bf16)
    store(output, output_hbm)
    for copy in stores:
        copy.wait()


def finish(sums, shifted, back):
    keep, take = final_matrices()
    anywhere = pl.BlockSpec(memory_space=pl.ANY)
    return pl.pallas_call(
        finish_kernel,
        out_shape=(
            jax.ShapeDtypeStruct((SPOTS, LEVELS, WIDTH), bf16),
            jax.ShapeDtypeStruct((WIDTH, FF), f32),
            jax.ShapeDtypeStruct((FF, WIDTH), f32),
        ),
        in_specs=[anywhere] * 5,
        out_specs=(anywhere, anywhere, anywhere),
        scratch_shapes=[
            pltpu.VMEM((PARTS, 2, PART_ROWS, PART_COLS), bf16),
            pltpu.VMEM((WIDTH, FF), f32),
            pltpu.VMEM((FF, WIDTH), f32),
            pltpu.VMEM((TOKENS, WIDTH), bf16),
            pltpu.VMEM((HALF, WIDTH), bf16),
            pltpu.VMEM((TOKENS, TOKENS), bf16),
            pltpu.VMEM((TOKENS, HALF), bf16),
            pltpu.VMEM((SPOTS, LEVELS, WIDTH), bf16),
            pltpu.SemaphoreType.DMA((PARTS + 4,)),
            pltpu.SemaphoreType.DMA((2 * PARTS + 1,)),
        ],
        compiler_params=pltpu.CompilerParams(vmem_limit_bytes=60 * 1024 * 1024),
        name="finish",
    )(
        sums,
        shifted,
        back,
        jnp.asarray(keep, bf16),
        jnp.asarray(take, bf16),
    )


def per_device(
    pixel_field,
    level_ids,
    embed_weight,
    embed_bias,
    latents,
    query_weight,
    key_weight,
    value_weight,
    pool_weight,
    pool_temp,
    first_gain,
    qkv_weight,
    window_temp,
    proj_weight,
    second_gain,
    up_weight,
    down_weight,
    cotangent,
):
    cot = jnp.transpose(cotangent, (1, 2, 0, 3)).reshape(SPOTS, LEVELS, WIDTH)
    shifted, back, sums = main_call(
        jnp.transpose(pixel_field, (0, 3, 1, 2)),
        level_ids,
        embed_weight,
        embed_bias,
        latents,
        query_weight,
        key_weight,
        value_weight,
        pool_weight,
        pool_temp,
        first_gain,
        qkv_weight,
        window_temp,
        proj_weight,
        second_gain,
        up_weight,
        down_weight,
        cot,
    )
    output, up_grad, down_grad = finish(sums, shifted, back)
    output = output.reshape(ROWS, COLS, LEVELS, WIDTH)
    return (jnp.transpose(output, (2, 0, 1, 3)), up_grad, down_grad)


def solution(mesh):
    placed = (P("enc", None, None, "lon"),) + (P(),) * 16 + (P(None, "enc", "lon", None),)
    return jax.shard_map(
        per_device,
        mesh=mesh,
        in_specs=placed,
        out_specs=(P(None, "enc", "lon", None), P(), P()),
        check_vma=False,
    )
```

```python
import itertools
import math

import jax
import jax.numpy as jnp
import numpy as np
from jax import lax
from jax.experimental import pallas as pl
from jax.experimental.pallas import tpu as pltpu
from jax.sharding import PartitionSpec as P

SLOTS = 52
HEADS = 16
HEAD_WIDTH = 32
WIDTH = 512
FF = 2048
LEVELS = 4
ROWS = 6
COLS = 12
SPOTS = ROWS * COLS
TOKENS = LEVELS * SPOTS
HALF = TOKENS // 2
PIXELS = 100
PER = SLOTS // 4
FAR = 7
EPSILON = 1e-05
NTOK = 36864
PARTS = 4
PART_ROWS = 1024
PART_COLS = 256
HALO = HALF // 2
LEAD = 40
STAGES = 3
SCATTER = ((0,), (1,), (2,))
GATHER = ((0,), (1, 2))
MESH = pl.DeviceIdType.MESH

f32 = jnp.float32
bf16 = jnp.bfloat16


def dot(a, b, contract=((1,), (0,))):
    return lax.dot_general(a, b, (contract, ((), ())), preferred_element_type=f32)


def normed(values, gain):
    mean = jnp.mean(values, axis=-1, keepdims=True)
    centred = values - mean
    variance = jnp.mean(centred * centred, axis=-1, keepdims=True)
    return (centred * lax.rsqrt(variance + EPSILON) * gain).astype(bf16)


def pooled_at(r, c, l):
    spot = c * ROWS + r
    if spot < LEAD:
        return l * LEAD + spot
    return LEVELS * LEAD + l * (SPOTS - LEAD) + spot - LEAD


def piece_at(r, c, l):
    return (r * (COLS // 2) + c) * LEVELS + l


def natural_at(r, c, l):
    return (r * COLS + c) * LEVELS + l


def shifted_at(r, c, l):
    pair, place = ((1, 0), (0, 0), (0, 1), (1, 1))[l]
    return (r // 3) * HALF + pair * HALO + ((r % 3) * COLS + c) * 2 + place


def matrix_of(rows, cols, entries):
    matrix = np.zeros((rows, cols), np.float32)
    for r in range(ROWS):
        for c in range(COLS // 2):
            for l in range(LEVELS):
                matrix[entries(r, c, l)] = 1.0
    return matrix


def order_matrices():
    half = COLS // 2
    return (
        matrix_of(HALF, LEVELS * LEAD, lambda r, c, l: (piece_at(r, c, l), pooled_at(r, c, l))),
        matrix_of(TOKENS, TOKENS, lambda r, c, l: (shifted_at(r, c, l), pooled_at(r, half + c, l))),
        matrix_of(HALF, TOKENS, lambda r, c, l: (piece_at(r, c, l), natural_at(r, c, l))),
        matrix_of(TOKENS, TOKENS, lambda r, c, l: (shifted_at(r, c, l), natural_at(r, half + c, l))),
        matrix_of(TOKENS, HALF, lambda r, c, l: (shifted_at(r, half + c, l), piece_at(r, c, l))),
        matrix_of(HALF, TOKENS, lambda r, c, l: (piece_at(r, c, l), shifted_at(r, half + c, l))),
    )


def final_matrices():
    half = COLS // 2
    return (
        matrix_of(TOKENS, TOKENS, lambda r, c, l: (natural_at(r, half + c, l), shifted_at(r, c, l))),
        matrix_of(TOKENS, HALF, lambda r, c, l: (natural_at(r, c, l), piece_at(r, c, l))),
    )


def pixel_matrix():
    matrix = np.zeros((4 * SPOTS, 4 * SPOTS), np.float32)
    for owner in range(4):
        for c in range(COLS):
            for r in range(ROWS):
                matrix[owner * SPOTS + c * ROWS + r, c * 4 * ROWS + owner * ROWS + r] = 1.0
    return matrix


def head_rows():
    mask = np.zeros((HEADS, WIDTH), np.float32)
    for h in range(HEADS):
        mask[h, h * HEAD_WIDTH : (h + 1) * HEAD_WIDTH] = 1.0
    return mask


def spread_matrix():
    one = np.zeros((LEVELS * HEADS, LEVELS * WIDTH), np.float32)
    for l in range(LEVELS):
        for h in range(HEADS):
            at = l * WIDTH + h * HEAD_WIDTH
            one[l * HEADS + h, at : at + HEAD_WIDTH] = 1.0
    return np.concatenate([one, one], axis=0)


def mesh_id(x, y, z, core):
    return (lax.rem(y, 2) * 2 + core, x * 8 + z * 2 + y // 2)


def split_parts(values):
    first = lax.broadcasted_iota(jnp.int32, values.shape, 1) < 64
    high = values.astype(bf16).astype(f32)
    return jnp.where(first, high, values - high).astype(bf16)


def main_kernel(
    ids,
    pool_temp,
    window_temp,
    pixels,
    pixel_order,
    latents,
    heads,
    first_gain,
    second_gain,
    embed_bias,
    query_hbm,
    key_hbm,
    embed_hbm,
    value_hbm,
    pool_hbm,
    spread_hbm,
    qkv_hbm,
    proj_hbm,
    up_hbm,
    down_hbm,
    cot_hbm,
    mat0_hbm,
    mat1_hbm,
    mat2_hbm,
    mat3_hbm,
    mat4_hbm,
    mat5_hbm,
    output_hbm,
    back_hbm,
    whole,
    output,
    back,
    result,
    query_weight,
    key_weight,
    embed_weight,
    value_weight,
    pool_weight,
    spread,
    qkv_weight,
    proj_weight,
    up_weight,
    down_weight,
    cotangent,
    mat0,
    mat1,
    mat2,
    mat3,
    mat4,
    mat5,
    bias,
    outgoing,
    arrived,
    tokens,
    scores,
    values,
    sums,
    own_cot,
    cot_left,
    cot_east,
    left,
    east,
    wide,
    cot_shifted,
    back_grad,
    qs,
    ks,
    vs,
    masks,
    attended,
    norm2,
    norm2_t,
    total,
    hiddens,
    leave,
    grads,
    pair,
    work,
    got1,
    got2,
    got3,
    load_sem,
    store_sem,
    send,
    recv,
    ring_send,
    ring_recv,
    pair_send,
    pair_recv,
):
    enc = lax.axis_index("enc")
    lon = lax.axis_index("lon")
    mate = enc + 1 - 2 * lax.rem(enc, 2)
    peers = (mate, lax.rem(enc + 2, 4), lax.rem(mate + 2, 4))
    west_id = (enc, lax.rem(lon + 31, 32))
    east_id = (enc, lax.rem(lon + 1, 32))
    core = lax.rem(enc, 2)
    x_at = lon // 8
    y_at = lax.rem(lon, 2) * 2 + enc // 2
    z_at = lax.rem(lon // 2, 4)

    places = [[lax.rem(at + by, 4) for by in range(4)] for at in (x_at, y_at, z_at)]
    x_part = [place * 8 for place in places[0]]
    y_part = [place // 2 for place in places[1]]
    z_part = [place * 2 for place in places[2]]
    enc_part = [lax.rem(place, 2) * 2 + core for place in places[1]]

    def device_at(step):
        return enc_part[step[1]], x_part[step[0]] + y_part[step[1]] + z_part[step[2]]

    def by_core(first, second):
        return first + core * (second - first)

    def step_of(part, way, phase, by):
        step = [0, 0, 0]
        for dim, count in zip(phase, by):
            step[(part + way + dim) % 3] = count
        return tuple(step)

    def chunk_for(part, way, phase, by):
        chunk = 0
        for dim, count in zip(phase, by):
            chunk = chunk * 4 + places[(part + way + dim) % 3][count % 4]
        return chunk

    def chunk_at(part, phase, by):
        return by_core(*[chunk_for(part, way, phase, by) for way in range(2)])

    def combos_of(phases):
        return [
            sorted(
                [by for by in itertools.product(range(4), repeat=len(phase)) if any(by)],
                key=lambda by: -sum(min(count, 4 - count) for count in by),
            )
            for phase in phases
        ]

    ways = (SCATTER, GATHER)
    combos = [combos_of(phases) for phases in ways]
    others = sorted(
        {
            step_of(turn, 0, phase, by)
            for turn in range(3)
            for phase, bys in zip(GATHER, combos[1])
            for by in bys
        }
    )
    devices = {step: device_at(step) for step in others}

    def device_for(part, phase, by):
        near, far = [devices[step_of(part, way, phase, by)] for way in range(2)]
        return by_core(near[0], far[0]), by_core(near[1], far[1])

    barrier = pltpu.get_barrier_semaphore()
    for peer in peers:
        pl.semaphore_signal(barrier, inc=1, device_id=(peer, lon), device_id_type=MESH)
    for other in (west_id, east_id):
        pl.semaphore_signal(barrier, inc=1, device_id=other, device_id_type=MESH)
    for step in others:
        pl.semaphore_signal(barrier, inc=1, device_id=devices[step], device_id_type=MESH)

    loads = {}
    for index, (name, source, target) in enumerate(
        (
            ("query", query_hbm, query_weight),
            ("key", key_hbm, key_weight),
            ("cot", cot_hbm, cotangent),
            ("mat2", mat2_hbm, mat2),
            ("embed", embed_hbm, embed_weight),
            ("value", value_hbm, value_weight),
            ("spread", spread_hbm, spread),
            ("pool", pool_hbm, pool_weight),
            ("mat0", mat0_hbm, mat0),
            ("mat1", mat1_hbm, mat1),
            ("mat3", mat3_hbm, mat3),
            ("mat4", mat4_hbm, mat4),
            ("mat5", mat5_hbm, mat5),
            ("down", down_hbm, down_weight),
            ("qkv", qkv_hbm, qkv_weight),
            ("proj", proj_hbm, proj_weight),
            ("up", up_hbm, up_weight),
        )
    ):
        loads[name] = pltpu.make_async_copy(source, target, load_sem.at[index])
    needed_first = ("query", "key", "embed")
    for name in needed_first:
        loads[name].start()

    def remote(source, target, index, device):
        copy = pltpu.make_async_remote_copy(
            src_ref=source,
            dst_ref=target,
            send_sem=send.at[index],
            recv_sem=recv.at[index],
            device_id=device,
            device_id_type=MESH,
        )
        copy.start()
        return copy

    def sort_pixels(slot, _):
        block = pixels[slot].astype(f32).reshape(4 * SPOTS, PIXELS).astype(bf16)
        block = dot(pixel_order[...], block).astype(bf16).astype(f32)
        for owner in range(4):
            outgoing[owner, slot] = block[owner * SPOTS : (owner + 1) * SPOTS].astype(bf16)
        return 0

    far_copies = []

    def send_far(k, first, count):
        slots_there = pl.ds(first, count)
        for i in (1, 2):
            far_copies.append(
                remote(
                    outgoing.at[peers[i], slots_there],
                    arrived.at[i, slots_there],
                    7 + 2 * k + i,
                    (peers[i], lon),
                )
            )

    lax.fori_loop(0, FAR, sort_pixels, 0, unroll=True)
    pl.semaphore_wait(barrier, 5 + len(others))
    send_far(0, 0, FAR)
    for name in loads:
        if name not in needed_first:
            loads[name].start()
    lax.fori_loop(FAR, PER, sort_pixels, 0, unroll=True)
    copy_mate = remote(outgoing.at[peers[0]], arrived.at[0], 0, (peers[0], lon))
    send_far(1, FAR, PER - FAR)

    bias[...] = embed_bias[...].astype(f32)
    loads["query"].wait()
    loads["key"].wait()
    queries = dot(latents[...], query_weight[...]).astype(bf16).astype(f32)
    blocks = [queries[l : l + 1] * heads[...] for l in range(LEVELS)]
    blocks = jnp.concatenate(blocks, axis=0).astype(bf16)
    head_of = lax.rem(lax.broadcasted_iota(jnp.int32, (LEVELS * HEADS, 1), 0), HEADS)
    temp = jnp.zeros((LEVELS * HEADS, 1), f32)
    for h in range(HEADS):
        temp = jnp.where(head_of == h, pool_temp[h] * (1.0 / math.sqrt(HEAD_WIDTH)), temp)
    folded = dot(blocks, key_weight[...], ((1,), (1,))) * temp
    high = folded.astype(bf16)
    low = (folded - high.astype(f32)).astype(bf16)
    keys = jnp.concatenate([high, high, low, low], axis=0)

    def token_of(block, slot):
        level = ids[slot]
        return dot(block, embed_weight[level]) + bias[pl.ds(level, 1), :]

    def embed_near(i, _):
        near = token_of(outgoing[enc, i], enc * PER + i)
        far = token_of(arrived[0, i], mate * PER + i)
        tokens[i] = jnp.concatenate([near, far], axis=0).astype(bf16)
        return 0

    def embed_far(first):
        def embed(i, _):
            near = token_of(arrived[1, first + i], peers[1] * PER + first + i)
            far = token_of(arrived[2, first + i], peers[2] * PER + first + i)
            tokens[i] = jnp.concatenate([near, far], axis=0).astype(bf16)
            return 0

        return embed

    def project(first, count):
        block = jnp.concatenate([tokens[first + i] for i in range(count)], axis=0)
        projected = dot(block, value_weight[...])
        scored = dot(block, keys, ((1,), (1,)))
        scored = scored[:, :128] + scored[:, 128:]
        for i in range(2 * count):
            values[first * 2 + i] = projected[i * SPOTS : (i + 1) * SPOTS]
            scores[first * 2 + i] = scored[i * SPOTS : (i + 1) * SPOTS]

    def project_two(i, _):
        project(2 * i, 2)
        return 0

    def mix(stage, first, count, lo, hi):
        probs = jnp.concatenate([scores[first + i, lo:hi] for i in range(count)], axis=0)
        split = split_parts(probs)
        size = hi - lo
        for l in range(LEVELS):
            wider = dot(split, spread[:, l * WIDTH : (l + 1) * WIDTH])
            part = sums[stage, l, lo:hi]
            for i in range(count):
                part = part + wider[i * size : (i + 1) * size] * values[first + i, lo:hi]
            sums[stage, l, lo:hi] = part

    def mix_all(stage, pairs, lo, hi):
        def mix_four(i, _):
            mix(stage, 4 * i, 4, lo, hi)
            return 0

        lax.fori_loop(0, pairs // 2, mix_four, 0, unroll=True)
        if pairs % 2:
            mix(stage, 2 * pairs - 2, 2, lo, hi)

    def pool_stage(stage, pairs, embed):
        lax.fori_loop(0, pairs, embed, 0, unroll=True)
        if stage == 0:
            loads["value"].wait()
        lax.fori_loop(0, pairs // 2, project_two, 0, unroll=True)
        if pairs % 2:
            project(pairs - 1, 1)
        peak = scores[0]
        for s in range(1, 2 * pairs):
            peak = jnp.maximum(peak, scores[s])
        weight = jnp.zeros_like(peak)
        for s in range(2 * pairs):
            exponent = jnp.exp(scores[s] - peak)
            scores[s] = exponent
            weight = weight + exponent
        sums[stage] = jnp.zeros((LEVELS, SPOTS, WIDTH), f32)
        return peak, weight

    loads["cot"].wait()
    loads["mat2"].wait()
    own_cot[...] = cotangent[...].astype(f32).reshape(TOKENS, WIDTH).astype(bf16)
    cot_left[...] = dot(mat2[...], own_cot[...]).astype(bf16)
    loads["embed"].wait()
    copy_mate.wait_recv()
    stats = [pool_stage(0, PER, embed_near)]
    loads["spread"].wait()
    mix_all(0, PER, 0, SPOTS)
    far_copies[0].wait_recv()
    far_copies[1].wait_recv()
    stats.append(pool_stage(1, FAR, embed_far(0)))
    mix_all(1, FAR, 0, SPOTS)
    far_copies[2].wait_recv()
    far_copies[3].wait_recv()
    copy_cot = remote(cot_left, cot_east, 3, west_id)
    stats.append(pool_stage(2, PER - FAR, embed_far(FAR)))

    peak = stats[0][0]
    for other, _ in stats[1:]:
        peak = jnp.maximum(peak, other)
    decays = [jnp.exp(top - peak) for top, _ in stats]
    inverse = 1.0 / sum(weight * decay for decay, (_, weight) in zip(decays, stats))
    decays = [decay * inverse for decay in decays]
    loads["pool"].wait()

    def finish_pool(lo, hi):
        shares = split_parts(jnp.concatenate([decay[lo:hi] for decay in decays], axis=0))
        size = hi - lo
        pooled = []
        for l in range(LEVELS):
            share = dot(shares, spread[:, l * WIDTH : (l + 1) * WIDTH])
            level = share[:size] * sums[0, l, lo:hi]
            for k in range(1, STAGES):
                level = level + share[k * size : (k + 1) * size] * sums[k, l, lo:hi]
            pooled.append(level)
        projected = dot(jnp.concatenate(pooled, axis=0).astype(bf16), pool_weight[...])
        rows = [
            projected[l * size : (l + 1) * size] + latents[l : l + 1].astype(f32)
            for l in range(LEVELS)
        ]
        return jnp.concatenate(rows, axis=0).astype(bf16)

    mix_all(2, PER - FAR, 0, LEAD)
    lead = finish_pool(0, LEAD)
    loads["mat0"].wait()
    left[...] = dot(mat0[...], lead).astype(bf16)
    copy_left = remote(left, east, 4, west_id)
    mix_all(2, PER - FAR, LEAD, SPOTS)
    stream = jnp.concatenate([lead, finish_pool(LEAD, SPOTS)], axis=0)
    loads["mat1"].wait()
    kept = dot(mat1[...], stream)
    copy_cot.wait_recv()
    loads["mat3"].wait()
    loads["mat4"].wait()
    cot = (dot(mat3[...], own_cot[...]) + dot(mat4[...], cot_east[...])).astype(bf16)
    cot_shifted[...] = cot
    loads["down"].wait()
    for j in range(4):
        back_grad[j] = dot(cot, down_weight[j * 512 : (j + 1) * 512], ((1,), (1,)))
    copy_left.wait_recv()
    own = (kept + dot(mat4[...], east[...])).astype(bf16)
    wide[HALF : HALF + TOKENS] = own
    copy_up = remote(
        wide.at[pl.ds(HALF, HALF)],
        wide.at[pl.ds(HALF + TOKENS, HALF)],
        5,
        (lax.rem(enc + 3, 4), lon),
    )
    copy_down = remote(
        wide.at[pl.ds(TOKENS, HALF)], wide.at[pl.ds(0, HALF)], 6, (lax.rem(enc + 1, 4), lon)
    )

    loads["qkv"].wait()
    norm = normed(own.astype(f32), first_gain[...])
    own_q = dot(norm, qkv_weight[:, :WIDTH])
    own_k = dot(norm, qkv_weight[:, WIDTH : 2 * WIDTH])
    own_v = dot(norm, qkv_weight[:, 2 * WIDTH :])
    row = lax.broadcasted_iota(jnp.int32, (HALO, HALF), 0)
    col = lax.broadcasted_iota(jnp.int32, (HALO, HALF), 1)
    same = lax.rem(row, 2) == lax.rem(col, 2)
    first_key = jnp.where(enc == 0, HALO, 0)
    last_key = jnp.where(enc == 3, HALO, HALF)
    ones = jnp.ones((HALF, 128), f32)
    for win in range(2):
        inside = (col >= first_key) if win == 0 else (col < last_key)
        masks[win * 2] = jnp.where(inside, 0.0, -1e30)
        masks[win * 2 + 1] = jnp.where(inside & same, 0.0, -1e30)
    copy_up.wait_recv()
    copy_down.wait_recv()
    halo = jnp.concatenate([wide[:HALF], wide[HALF + TOKENS :]], axis=0).astype(f32)
    norm = normed(halo, first_gain[...])
    halo_k = dot(norm, qkv_weight[:, WIDTH : 2 * WIDTH])
    halo_v = dot(norm, qkv_weight[:, 2 * WIDTH :])
    for win in range(2):
        for two in range(2):
            at = win * HALF + two * HALO
            rows = slice(at, at + HALO)
            for g in range(4):
                lanes = slice(g * 128, (g + 1) * 128)
                index = (win * 2 + two) * 4 + g
                qs[index] = own_q[rows, lanes]
                key = (halo_k[rows, lanes], own_k[rows, lanes])
                value = (halo_v[rows, lanes], own_v[rows, lanes])
                if win == 1:
                    key, value = key[::-1], value[::-1]
                ks[index] = jnp.concatenate(key, axis=0).astype(bf16)
                value = jnp.concatenate(value, axis=0)
                vs[index] = jnp.concatenate([value, ones], axis=1).astype(bf16)

    lane = lax.broadcasted_iota(jnp.int32, (HALO, 128), 1) // HEAD_WIDTH

    def attend(index, _):
        group = lax.rem(index, 4)
        query = qs[index]
        mask = masks[index // 4]
        stacked = [jnp.where(lane == h, query, 0.0) for h in range(4)]
        raw = dot(jnp.concatenate(stacked, axis=0).astype(bf16), ks[index], ((1,), (1,)))
        exponents = []
        for h in range(4):
            masked = raw[h * HALO : (h + 1) * HALO] + mask
            top = jnp.max(masked, axis=-1, keepdims=True)
            factor = window_temp[group * 4 + h] * (1.0 / math.sqrt(HEAD_WIDTH))
            exponents.append(jnp.exp((masked - top) * factor).astype(bf16).astype(f32))
        exponent = jnp.concatenate(exponents, axis=0).astype(bf16)
        mixed = dot(exponent, vs[index])
        above = mixed[:HALO, :128]
        under = mixed[:HALO, 128:]
        for h in range(1, 4):
            rows = slice(h * HALO, (h + 1) * HALO)
            above = jnp.where(lane == h, mixed[rows, :128], above)
            under = jnp.where(lane == h, mixed[rows, 128:], under)
        attended[index] = above / under
        return 0

    lax.fori_loop(0, 16, attend, 0, unroll=True)

    rows = [
        jnp.concatenate([attended[block * 4 + g] for g in range(4)], axis=1) for block in range(4)
    ]
    loads["proj"].wait()
    mixed = dot(jnp.concatenate(rows, axis=0).astype(bf16), proj_weight[...])
    middle = (own.astype(f32) + mixed).astype(bf16).astype(f32)
    norm = normed(middle, second_gain[...])
    norm2[...] = norm
    norm2_t[...] = norm.T
    total[...] = middle

    got = (got1, got2, got3)
    sizes = ((PART_ROWS // 4, PART_ROWS // 16, PART_ROWS // 64), (PART_ROWS // 4, PART_ROWS // 64))
    offsets = ((0, 3, 6), (0, 3))

    starts = []
    for way, phases in enumerate(ways):
        starts.append([])
        for p in range(PARTS):
            at = [0]
            for phase, size in zip(phases, sizes[way]):
                at.append(at[-1] + chunk_at(p, phase, (0, 0)) * size)
            starts[way].append(at)
    pair_id = (mate, lon)
    pair_copies = []
    stores = []
    copies = {}

    def give_pair(index, source, target):
        copy = pltpu.make_async_remote_copy(
            src_ref=source,
            dst_ref=target,
            send_sem=pair_send.at[index],
            recv_sem=pair_recv.at[index],
            device_id=pair_id,
            device_id_type=MESH,
        )
        copy.start()
        pair_copies.append(copy)
        return copy

    def ring_copy(way, p, phase, k, source, target):
        at = offsets[way][phase] + k
        return pltpu.make_async_remote_copy(
            src_ref=source,
            dst_ref=target,
            send_sem=ring_send.at[way, p, at],
            recv_sem=ring_recv.at[way, p, at],
            device_id=device_for(p, ways[way][phase], combos[way][phase][k]),
            device_id_type=MESH,
        )

    def scatter(p, phase, make=None):
        size = sizes[0][phase]
        for k, by in enumerate(combos[0][phase]):
            target = chunk_at(p, SCATTER[phase], by)
            first = pl.multiple_of(starts[0][p][phase] + target * size, 16)
            if make is not None:
                make(pl.ds(first, size))
            source = work.at[p, pl.ds(first, size)]
            copy = ring_copy(0, p, phase, k, source, got[phase].at[p, k])
            copy.start()
            copies[0, p, phase, k] = copy

    def add_up(p, phase):
        for k in range(len(combos[0][phase])):
            copies[0, p, phase, k].wait_recv()
        size = sizes[0][phase]
        first = pl.multiple_of(starts[0][p][phase + 1], 16)
        held = work[p, pl.ds(first, size), :].astype(f32)
        for k in range(len(combos[0][phase])):
            held = held + got[phase][p, k].astype(f32)
        if phase < 2:
            work[p, pl.ds(first, size), :] = held.astype(bf16)
            scatter(p, phase + 1)
        else:
            result[core, p, pl.ds(first, size), :] = held.astype(bf16)
            gather(p, 1)

    def gather(p, phase):
        first = pl.multiple_of(starts[1][p][phase + 1], 16)
        piece = result.at[core, p, pl.ds(first, sizes[1][phase])]
        for k in range(len(combos[1][phase])):
            copy = ring_copy(1, p, phase, k, piece, piece)
            copy.start()
            copies[1, p, phase, k] = copy

    def gathered(p, phase):
        size = sizes[1][phase]
        for k, by in enumerate(combos[1][phase]):
            source = chunk_at(p, GATHER[phase], [4 - step for step in by])
            first = pl.multiple_of(starts[1][p][phase] + source * size, 16)
            piece = result.at[core, p, pl.ds(first, size)]
            ring_copy(1, p, phase, k, piece, piece).wait_recv()
            if phase == 0:
                give_pair(PARTS + 4 * p + 1 + k, piece, piece)
        if phase == 1:
            gather(p, 0)
            first = pl.multiple_of(starts[1][p][1], 16)
            piece = result.at[core, p, pl.ds(first, sizes[1][0])]
            give_pair(PARTS + 4 * p, piece, piece)
        else:
            store(result.at[core, p], whole.at[core, p])

    def store(source, target):
        copy = pltpu.make_async_copy(source, target, store_sem.at[len(stores)])
        copy.start()
        stores.append(copy)

    def paired(p):
        for k in range(4):
            piece = result.at[1 - core, p, pl.ds(0, sizes[1][0])]
            pltpu.make_async_remote_copy(
                src_ref=piece,
                dst_ref=piece,
                send_sem=pair_send.at[PARTS + 4 * p + k],
                recv_sem=pair_recv.at[PARTS + 4 * p + k],
                device_id=pair_id,
                device_id_type=MESH,
            ).wait_recv()
        store(result.at[1 - core, p], whole.at[1 - core, p])

    def mlp(j):
        columns = slice(j * 512, (j + 1) * 512)
        x = dot(norm2[...], up_weight[:, columns])
        cubic = 0.044715 * (x * x)
        scale = math.sqrt(2.0 / math.pi)
        bend = jnp.tanh(scale * (x * (1.0 + cubic)))
        hidden = (0.5 * x * (1.0 + bend)).astype(bf16)
        hiddens[j] = hidden
        slope = 0.5 * (1.0 + bend) + 0.5 * x * (1.0 - bend * bend) * (scale * (1.0 + 3.0 * cubic))
        slope = (slope * back_grad[j]).astype(bf16)
        down_grad = dot(hidden, cot_shifted[...], ((0,), (0,))).astype(bf16)
        up_grad = dot(norm2_t[...], slope).astype(bf16)
        for i in range(2):
            lanes = slice(i * PART_COLS, (i + 1) * PART_COLS)
            grads[0, j, i * 512 : (i + 1) * 512] = up_grad[:, lanes]
            grads[1, j, i * 512 : (i + 1) * 512] = down_grad[:, lanes]

    def reduce_pair(p):
        pair_copies[p].wait_recv()

        def both(rows):
            work[p, rows, :] = (grads[core, p, rows, :].astype(f32) + pair[p, rows, :].astype(f32)).astype(bf16)

        scatter(p, 0, both)
        both(pl.ds(pl.multiple_of(starts[0][p][1], 16), sizes[0][0]))

    loads["up"].wait()
    for j in range(PARTS):
        mlp(j)
        give_pair(j, grads.at[1 - core, j], pair.at[j])
        if j > 1:
            reduce_pair(j - 2)
    reduce_pair(PARTS - 2)
    reduce_pair(PARTS - 1)
    done = total[...]
    for j in range(PARTS):
        done = done + dot(hiddens[j], down_weight[j * 512 : (j + 1) * 512])
    done = done.astype(bf16)
    output[...] = done
    store(output, output_hbm)
    loads["mat5"].wait()
    leave[...] = dot(mat5[...], done).astype(bf16)
    for p in range(PARTS):
        add_up(p, 0)
    copy_back = remote(leave, back, 7, east_id)
    for phase in (1, 2):
        for p in range(PARTS):
            add_up(p, phase)
    for p in range(PARTS):
        gathered(p, 1)
    copy_back.wait_recv()
    store(back, back_hbm)
    for p in range(PARTS):
        gathered(p, 0)
    for p in range(PARTS):
        paired(p)
    for copy in (copy_mate, copy_cot, copy_left, copy_up, copy_down, copy_back, *far_copies):
        copy.wait_send()
    for copy in pair_copies:
        copy.wait_send()
    for copy in copies.values():
        copy.wait_send()
    for copy in stores:
        copy.wait()


def main_call(
    pixels,
    ids,
    embed_weight,
    embed_bias,
    latents,
    query_weight,
    key_weight,
    value_weight,
    pool_weight,
    pool_temp,
    first_gain,
    qkv_weight,
    window_temp,
    proj_weight,
    second_gain,
    up_weight,
    down_weight,
    cot,
):
    vmem = pl.BlockSpec(memory_space=pltpu.VMEM)
    smem = pl.BlockSpec(memory_space=pltpu.SMEM)
    anywhere = pl.BlockSpec(memory_space=pl.ANY)
    matrices = [jnp.asarray(matrix, bf16) for matrix in order_matrices()]
    spread = jnp.asarray(spread_matrix(), bf16)
    loaded = (
        query_weight,
        key_weight,
        embed_weight,
        value_weight,
        pool_weight,
        spread,
        qkv_weight,
        proj_weight,
        up_weight,
        down_weight,
        cot,
        *matrices,
    )
    piece = pltpu.VMEM((HALF, WIDTH), bf16)
    part = pltpu.VMEM((PARTS, PART_ROWS, PART_COLS), bf16)
    return pl.pallas_call(
        main_kernel,
        out_shape=(
            jax.ShapeDtypeStruct((TOKENS, WIDTH), bf16),
            jax.ShapeDtypeStruct((HALF, WIDTH), bf16),
            jax.ShapeDtypeStruct((2, PARTS, PART_ROWS, PART_COLS), bf16),
        ),
        in_specs=[smem] * 3 + [vmem] * 7 + [anywhere] * len(loaded),
        out_specs=(anywhere, anywhere, anywhere),
        scratch_shapes=[
            pltpu.VMEM((TOKENS, WIDTH), bf16),
            pltpu.VMEM((HALF, WIDTH), bf16),
            pltpu.VMEM((2, PARTS, PART_ROWS, PART_COLS), bf16),
        ]
        + [pltpu.VMEM(value.shape, bf16) for value in loaded]
        + [
            pltpu.VMEM((SLOTS, WIDTH), f32),
            pltpu.VMEM((4, PER, SPOTS, PIXELS), bf16),
            pltpu.VMEM((3, PER, SPOTS, PIXELS), bf16),
            pltpu.VMEM((PER, 2 * SPOTS, WIDTH), bf16),
            pltpu.VMEM((2 * PER, SPOTS, 128), f32),
            pltpu.VMEM((2 * PER, SPOTS, WIDTH), f32),
            pltpu.VMEM((STAGES, LEVELS, SPOTS, WIDTH), f32),
            pltpu.VMEM((TOKENS, WIDTH), bf16),
            piece,
            piece,
            piece,
            piece,
            pltpu.VMEM((2 * TOKENS, WIDTH), bf16),
            pltpu.VMEM((TOKENS, WIDTH), bf16),
            pltpu.VMEM((4, TOKENS, 512), f32),
            pltpu.VMEM((16, HALO, 128), f32),
            pltpu.VMEM((16, HALF, 128), bf16),
            pltpu.VMEM((16, HALF, 256), bf16),
            pltpu.VMEM((4, HALO, HALF), f32),
            pltpu.VMEM((16, HALO, 128), f32),
            pltpu.VMEM((TOKENS, WIDTH), bf16),
            pltpu.VMEM((WIDTH, TOKENS), bf16),
            pltpu.VMEM((TOKENS, WIDTH), f32),
            pltpu.VMEM((PARTS, TOKENS, 512), bf16),
            piece,
            pltpu.VMEM((2, PARTS, PART_ROWS, PART_COLS), bf16),
            part,
            part,
            pltpu.VMEM((PARTS, 3, PART_ROWS // 4, PART_COLS), bf16),
            pltpu.VMEM((PARTS, 3, PART_ROWS // 16, PART_COLS), bf16),
            pltpu.VMEM((PARTS, 3, PART_ROWS // 64, PART_COLS), bf16),
            pltpu.SemaphoreType.DMA((len(loaded),)),
            pltpu.SemaphoreType.DMA((2 * PARTS + 2,)),
            pltpu.SemaphoreType.DMA((12,)),
            pltpu.SemaphoreType.DMA((12,)),
            pltpu.SemaphoreType.DMA((2, PARTS, 18)),
            pltpu.SemaphoreType.DMA((2, PARTS, 18)),
            pltpu.SemaphoreType.DMA((5 * PARTS,)),
            pltpu.SemaphoreType.DMA((5 * PARTS,)),
        ],
        compiler_params=pltpu.CompilerParams(
            collective_id=1, has_side_effects=True, vmem_limit_bytes=60 * 1024 * 1024
        ),
        name="main",
    )(
        ids,
        pool_temp,
        window_temp,
        pixels,
        jnp.asarray(pixel_matrix(), bf16),
        latents,
        jnp.asarray(head_rows(), f32),
        first_gain[None, :],
        second_gain[None, :],
        embed_bias,
        *loaded,
    )


def finish_kernel(
    sums,
    shifted_hbm,
    back_hbm,
    keep_hbm,
    take_hbm,
    output_hbm,
    up_hbm,
    down_hbm,
    loaded,
    up_grad,
    down_grad,
    shifted,
    back,
    keep,
    take,
    output,
    load_sem,
    store_sem,
):
    scaling = 1.0 / math.sqrt(NTOK)
    loads = []

    def load(source, target):
        loads.append(pltpu.make_async_copy(source, target, load_sem.at[len(loads)]))
        loads[-1].start()

    for p in range(PARTS):
        load(sums.at[:, p], loaded.at[p])
    load(shifted_hbm, shifted)
    load(back_hbm, back)
    load(keep_hbm, keep)
    load(take_hbm, take)
    stores = []

    def store(source, target):
        stores.append(pltpu.make_async_copy(source, target, store_sem.at[len(stores)]))
        stores[-1].start()

    for p in range(PARTS):
        loads[p].wait()
        wide = slice(p * 512, (p + 1) * 512)
        for i in range(2):
            rows = slice(i * 512, (i + 1) * 512)
            lanes = slice(i * PART_COLS, (i + 1) * PART_COLS)
            up_lanes = slice(p * 512 + i * PART_COLS, p * 512 + (i + 1) * PART_COLS)
            down_grad[wide, lanes] = loaded[p, 1, rows].astype(f32) * scaling
            up_grad[:, up_lanes] = loaded[p, 0, rows].astype(f32) * scaling
        store(down_grad.at[pl.ds(p * 512, 512)], down_hbm.at[pl.ds(p * 512, 512)])
        store(up_grad.at[:, pl.ds(p * 512, 512)], up_hbm.at[:, pl.ds(p * 512, 512)])
    for copy in loads[PARTS:]:
        copy.wait()
    whole = dot(keep[...], shifted[...]) + dot(take[...], back[...])
    output[...] = whole.reshape(SPOTS, LEVELS, WIDTH).astype(bf16)
    store(output, output_hbm)
    for copy in stores:
        copy.wait()


def finish(sums, shifted, back):
    keep, take = final_matrices()
    anywhere = pl.BlockSpec(memory_space=pl.ANY)
    return pl.pallas_call(
        finish_kernel,
        out_shape=(
            jax.ShapeDtypeStruct((SPOTS, LEVELS, WIDTH), bf16),
            jax.ShapeDtypeStruct((WIDTH, FF), f32),
            jax.ShapeDtypeStruct((FF, WIDTH), f32),
        ),
        in_specs=[anywhere] * 5,
        out_specs=(anywhere, anywhere, anywhere),
        scratch_shapes=[
            pltpu.VMEM((PARTS, 2, PART_ROWS, PART_COLS), bf16),
            pltpu.VMEM((WIDTH, FF), f32),
            pltpu.VMEM((FF, WIDTH), f32),
            pltpu.VMEM((TOKENS, WIDTH), bf16),
            pltpu.VMEM((HALF, WIDTH), bf16),
            pltpu.VMEM((TOKENS, TOKENS), bf16),
            pltpu.VMEM((TOKENS, HALF), bf16),
            pltpu.VMEM((SPOTS, LEVELS, WIDTH), bf16),
            pltpu.SemaphoreType.DMA((PARTS + 4,)),
            pltpu.SemaphoreType.DMA((2 * PARTS + 1,)),
        ],
        compiler_params=pltpu.CompilerParams(vmem_limit_bytes=60 * 1024 * 1024),
        name="finish",
    )(
        sums,
        shifted,
        back,
        jnp.asarray(keep, bf16),
        jnp.asarray(take, bf16),
    )


def per_device(
    pixel_field,
    level_ids,
    embed_weight,
    embed_bias,
    latents,
    query_weight,
    key_weight,
    value_weight,
    pool_weight,
    pool_temp,
    first_gain,
    qkv_weight,
    window_temp,
    proj_weight,
    second_gain,
    up_weight,
    down_weight,
    cotangent,
):
    cot = jnp.transpose(cotangent, (1, 2, 0, 3)).reshape(SPOTS, LEVELS, WIDTH)
    shifted, back, sums = main_call(
        jnp.transpose(pixel_field, (0, 3, 1, 2)),
        level_ids,
        embed_weight,
        embed_bias,
        latents,
        query_weight,
        key_weight,
        value_weight,
        pool_weight,
        pool_temp,
        first_gain,
        qkv_weight,
        window_temp,
        proj_weight,
        second_gain,
        up_weight,
        down_weight,
        cot,
    )
    output, up_grad, down_grad = finish(sums, shifted, back)
    output = output.reshape(ROWS, COLS, LEVELS, WIDTH)
    return (jnp.transpose(output, (2, 0, 1, 3)), up_grad, down_grad)


def solution(mesh):
    placed = (P("enc", None, None, "lon"),) + (P(),) * 16 + (P(None, "enc", "lon", None),)
    return jax.shard_map(
        per_device,
        mesh=mesh,
        in_specs=placed,
        out_specs=(P(None, "enc", "lon", None), P(), P()),
        check_vma=False,
    )
```

```python
import itertools
import math

import jax
import jax.numpy as jnp
import numpy as np
from jax import lax
from jax.experimental import pallas as pl
from jax.experimental.pallas import tpu as pltpu
from jax.sharding import PartitionSpec as P

SLOTS = 52
HEADS = 16
HEAD_WIDTH = 32
WIDTH = 512
FF = 2048
LEVELS = 4
ROWS = 6
COLS = 12
SPOTS = ROWS * COLS
TOKENS = LEVELS * SPOTS
HALF = TOKENS // 2
PIXELS = 100
PER = SLOTS // 4
FAR = 7
EPSILON = 1e-05
NTOK = 36864
PARTS = 4
PART_ROWS = 1024
PART_COLS = 256
HALO = HALF // 2
LEAD = 40
STAGES = 3
PHASES = ((0,), (1, 2))
MESH = pl.DeviceIdType.MESH

f32 = jnp.float32
bf16 = jnp.bfloat16


def dot(a, b, contract=((1,), (0,))):
    return lax.dot_general(a, b, (contract, ((), ())), preferred_element_type=f32)


def normed(values, gain):
    mean = jnp.mean(values, axis=-1, keepdims=True)
    centred = values - mean
    variance = jnp.mean(centred * centred, axis=-1, keepdims=True)
    return (centred * lax.rsqrt(variance + EPSILON) * gain).astype(bf16)


def pooled_at(r, c, l):
    spot = c * ROWS + r
    if spot < LEAD:
        return l * LEAD + spot
    return LEVELS * LEAD + l * (SPOTS - LEAD) + spot - LEAD


def piece_at(r, c, l):
    return (r * (COLS // 2) + c) * LEVELS + l


def natural_at(r, c, l):
    return (r * COLS + c) * LEVELS + l


def shifted_at(r, c, l):
    pair, place = ((1, 0), (0, 0), (0, 1), (1, 1))[l]
    return (r // 3) * HALF + pair * HALO + ((r % 3) * COLS + c) * 2 + place


def matrix_of(rows, cols, entries):
    matrix = np.zeros((rows, cols), np.float32)
    for r in range(ROWS):
        for c in range(COLS // 2):
            for l in range(LEVELS):
                matrix[entries(r, c, l)] = 1.0
    return matrix


def order_matrices():
    half = COLS // 2
    return (
        matrix_of(HALF, LEVELS * LEAD, lambda r, c, l: (piece_at(r, c, l), pooled_at(r, c, l))),
        matrix_of(TOKENS, TOKENS, lambda r, c, l: (shifted_at(r, c, l), pooled_at(r, half + c, l))),
        matrix_of(HALF, TOKENS, lambda r, c, l: (piece_at(r, c, l), natural_at(r, c, l))),
        matrix_of(TOKENS, TOKENS, lambda r, c, l: (shifted_at(r, c, l), natural_at(r, half + c, l))),
        matrix_of(TOKENS, HALF, lambda r, c, l: (shifted_at(r, half + c, l), piece_at(r, c, l))),
        matrix_of(HALF, TOKENS, lambda r, c, l: (piece_at(r, c, l), shifted_at(r, half + c, l))),
    )


def final_matrices():
    half = COLS // 2
    return (
        matrix_of(TOKENS, TOKENS, lambda r, c, l: (natural_at(r, half + c, l), shifted_at(r, c, l))),
        matrix_of(TOKENS, HALF, lambda r, c, l: (natural_at(r, c, l), piece_at(r, c, l))),
    )


def pixel_matrix():
    matrix = np.zeros((4 * SPOTS, 4 * SPOTS), np.float32)
    for owner in range(4):
        for c in range(COLS):
            for r in range(ROWS):
                matrix[owner * SPOTS + c * ROWS + r, c * 4 * ROWS + owner * ROWS + r] = 1.0
    return matrix


def head_rows():
    mask = np.zeros((HEADS, WIDTH), np.float32)
    for h in range(HEADS):
        mask[h, h * HEAD_WIDTH : (h + 1) * HEAD_WIDTH] = 1.0
    return mask


def spread_matrix():
    one = np.zeros((LEVELS * HEADS, LEVELS * WIDTH), np.float32)
    for l in range(LEVELS):
        for h in range(HEADS):
            at = l * WIDTH + h * HEAD_WIDTH
            one[l * HEADS + h, at : at + HEAD_WIDTH] = 1.0
    return np.concatenate([one, one], axis=0)


def mesh_id(x, y, z, core):
    return (lax.rem(y, 2) * 2 + core, x * 8 + z * 2 + y // 2)


def split_parts(values):
    first = lax.broadcasted_iota(jnp.int32, values.shape, 1) < 64
    high = values.astype(bf16).astype(f32)
    return jnp.where(first, high, values - high).astype(bf16)


def main_kernel(
    ids,
    pool_temp,
    window_temp,
    pixels,
    pixel_order,
    latents,
    heads,
    first_gain,
    second_gain,
    embed_bias,
    query_hbm,
    key_hbm,
    embed_hbm,
    value_hbm,
    pool_hbm,
    spread_hbm,
    qkv_hbm,
    proj_hbm,
    up_hbm,
    down_hbm,
    cot_hbm,
    mat0_hbm,
    mat1_hbm,
    mat2_hbm,
    mat3_hbm,
    mat4_hbm,
    mat5_hbm,
    output_hbm,
    back_hbm,
    whole,
    output,
    back,
    result,
    query_weight,
    key_weight,
    embed_weight,
    value_weight,
    pool_weight,
    spread,
    qkv_weight,
    proj_weight,
    up_weight,
    down_weight,
    cotangent,
    mat0,
    mat1,
    mat2,
    mat3,
    mat4,
    mat5,
    bias,
    outgoing,
    arrived,
    tokens,
    scores,
    values,
    sums,
    own_cot,
    cot_left,
    cot_east,
    left,
    east,
    wide,
    cot_shifted,
    back_grad,
    qs,
    ks,
    vs,
    masks,
    attended,
    norm2,
    norm2_t,
    total,
    hiddens,
    leave,
    grads,
    pair,
    work,
    got1,
    got2,
    load_sem,
    store_sem,
    send,
    recv,
    ring_send,
    ring_recv,
    pair_send,
    pair_recv,
):
    enc = lax.axis_index("enc")
    lon = lax.axis_index("lon")
    mate = enc + 1 - 2 * lax.rem(enc, 2)
    peers = (mate, lax.rem(enc + 2, 4), lax.rem(mate + 2, 4))
    west_id = (enc, lax.rem(lon + 31, 32))
    east_id = (enc, lax.rem(lon + 1, 32))
    core = lax.rem(enc, 2)
    x_at = lon // 8
    y_at = lax.rem(lon, 2) * 2 + enc // 2
    z_at = lax.rem(lon // 2, 4)

    places = [[lax.rem(at + by, 4) for by in range(4)] for at in (x_at, y_at, z_at)]
    x_part = [place * 8 for place in places[0]]
    y_part = [place // 2 for place in places[1]]
    z_part = [place * 2 for place in places[2]]
    enc_part = [lax.rem(place, 2) * 2 + core for place in places[1]]

    def device_at(step):
        return enc_part[step[1]], x_part[step[0]] + y_part[step[1]] + z_part[step[2]]

    def by_core(first, second):
        return first + core * (second - first)

    def step_of(part, way, phase, by):
        step = [0, 0, 0]
        for dim, count in zip(phase, by):
            step[(part + way + dim) % 3] = count
        return tuple(step)

    def chunk_for(part, way, phase, by):
        chunk = 0
        for dim, count in zip(phase, by):
            chunk = chunk * 4 + places[(part + way + dim) % 3][count % 4]
        return chunk

    def chunk_at(part, phase, by):
        return by_core(*[chunk_for(part, way, phase, by) for way in range(2)])

    combos = [
        sorted(
            [by for by in itertools.product(range(4), repeat=len(phase)) if any(by)],
            key=lambda by: -sum(min(count, 4 - count) for count in by),
        )
        for phase in PHASES
    ]
    others = sorted(
        {
            step_of(turn, 0, phase, by)
            for turn in range(3)
            for phase, bys in zip(PHASES, combos)
            for by in bys
        }
    )
    devices = {step: device_at(step) for step in others}

    def device_for(part, phase, by):
        near, far = [devices[step_of(part, way, phase, by)] for way in range(2)]
        return by_core(near[0], far[0]), by_core(near[1], far[1])

    barrier = pltpu.get_barrier_semaphore()
    for peer in peers:
        pl.semaphore_signal(barrier, inc=1, device_id=(peer, lon), device_id_type=MESH)
    for other in (west_id, east_id):
        pl.semaphore_signal(barrier, inc=1, device_id=other, device_id_type=MESH)
    for step in others:
        pl.semaphore_signal(barrier, inc=1, device_id=devices[step], device_id_type=MESH)

    loads = {}
    for index, (name, source, target) in enumerate(
        (
            ("query", query_hbm, query_weight),
            ("key", key_hbm, key_weight),
            ("cot", cot_hbm, cotangent),
            ("mat2", mat2_hbm, mat2),
            ("embed", embed_hbm, embed_weight),
            ("value", value_hbm, value_weight),
            ("spread", spread_hbm, spread),
            ("pool", pool_hbm, pool_weight),
            ("mat0", mat0_hbm, mat0),
            ("mat1", mat1_hbm, mat1),
            ("mat3", mat3_hbm, mat3),
            ("mat4", mat4_hbm, mat4),
            ("mat5", mat5_hbm, mat5),
            ("down", down_hbm, down_weight),
            ("qkv", qkv_hbm, qkv_weight),
            ("proj", proj_hbm, proj_weight),
            ("up", up_hbm, up_weight),
        )
    ):
        loads[name] = pltpu.make_async_copy(source, target, load_sem.at[index])
        loads[name].start()

    def remote(source, target, index, device):
        copy = pltpu.make_async_remote_copy(
            src_ref=source,
            dst_ref=target,
            send_sem=send.at[index],
            recv_sem=recv.at[index],
            device_id=device,
            device_id_type=MESH,
        )
        copy.start()
        return copy

    def sort_pixels(slot, _):
        block = pixels[slot].astype(f32).reshape(4 * SPOTS, PIXELS).astype(bf16)
        block = dot(pixel_order[...], block).astype(bf16).astype(f32)
        for owner in range(4):
            outgoing[owner, slot] = block[owner * SPOTS : (owner + 1) * SPOTS].astype(bf16)
        return 0

    far_copies = []

    def send_far(k, first, count):
        slots_there = pl.ds(first, count)
        for i in (1, 2):
            far_copies.append(
                remote(
                    outgoing.at[peers[i], slots_there],
                    arrived.at[i, slots_there],
                    7 + 2 * k + i,
                    (peers[i], lon),
                )
            )

    lax.fori_loop(0, FAR, sort_pixels, 0, unroll=True)
    pl.semaphore_wait(barrier, 5 + len(others))
    send_far(0, 0, FAR)
    lax.fori_loop(FAR, PER, sort_pixels, 0, unroll=True)
    copy_mate = remote(outgoing.at[peers[0]], arrived.at[0], 0, (peers[0], lon))
    send_far(1, FAR, PER - FAR)

    bias[...] = embed_bias[...].astype(f32)
    loads["query"].wait()
    loads["key"].wait()
    queries = dot(latents[...], query_weight[...]).astype(bf16).astype(f32)
    blocks = [queries[l : l + 1] * heads[...] for l in range(LEVELS)]
    blocks = jnp.concatenate(blocks, axis=0).astype(bf16)
    head_of = lax.rem(lax.broadcasted_iota(jnp.int32, (LEVELS * HEADS, 1), 0), HEADS)
    temp = jnp.zeros((LEVELS * HEADS, 1), f32)
    for h in range(HEADS):
        temp = jnp.where(head_of == h, pool_temp[h] * (1.0 / math.sqrt(HEAD_WIDTH)), temp)
    folded = dot(blocks, key_weight[...], ((1,), (1,))) * temp
    high = folded.astype(bf16)
    low = (folded - high.astype(f32)).astype(bf16)
    keys = jnp.concatenate([high, high, low, low], axis=0)

    def token_of(block, slot):
        level = ids[slot]
        return dot(block, embed_weight[level]) + bias[pl.ds(level, 1), :]

    def embed_near(i, _):
        near = token_of(outgoing[enc, i], enc * PER + i)
        far = token_of(arrived[0, i], mate * PER + i)
        tokens[i] = jnp.concatenate([near, far], axis=0).astype(bf16)
        return 0

    def embed_far(first):
        def embed(i, _):
            near = token_of(arrived[1, first + i], peers[1] * PER + first + i)
            far = token_of(arrived[2, first + i], peers[2] * PER + first + i)
            tokens[i] = jnp.concatenate([near, far], axis=0).astype(bf16)
            return 0

        return embed

    def project(first, count):
        block = jnp.concatenate([tokens[first + i] for i in range(count)], axis=0)
        projected = dot(block, value_weight[...])
        scored = dot(block, keys, ((1,), (1,)))
        scored = scored[:, :128] + scored[:, 128:]
        for i in range(2 * count):
            values[first * 2 + i] = projected[i * SPOTS : (i + 1) * SPOTS]
            scores[first * 2 + i] = scored[i * SPOTS : (i + 1) * SPOTS]

    def project_two(i, _):
        project(2 * i, 2)
        return 0

    def mix(stage, first, count, lo, hi):
        probs = jnp.concatenate([scores[first + i, lo:hi] for i in range(count)], axis=0)
        split = split_parts(probs)
        size = hi - lo
        for l in range(LEVELS):
            wider = dot(split, spread[:, l * WIDTH : (l + 1) * WIDTH])
            part = sums[stage, l, lo:hi]
            for i in range(count):
                part = part + wider[i * size : (i + 1) * size] * values[first + i, lo:hi]
            sums[stage, l, lo:hi] = part

    def mix_all(stage, pairs, lo, hi):
        def mix_four(i, _):
            mix(stage, 4 * i, 4, lo, hi)
            return 0

        lax.fori_loop(0, pairs // 2, mix_four, 0, unroll=True)
        if pairs % 2:
            mix(stage, 2 * pairs - 2, 2, lo, hi)

    def pool_stage(stage, pairs, embed):
        lax.fori_loop(0, pairs, embed, 0, unroll=True)
        if stage == 0:
            loads["value"].wait()
        lax.fori_loop(0, pairs // 2, project_two, 0, unroll=True)
        if pairs % 2:
            project(pairs - 1, 1)
        peak = scores[0]
        for s in range(1, 2 * pairs):
            peak = jnp.maximum(peak, scores[s])
        weight = jnp.zeros_like(peak)
        for s in range(2 * pairs):
            exponent = jnp.exp(scores[s] - peak)
            scores[s] = exponent
            weight = weight + exponent
        sums[stage] = jnp.zeros((LEVELS, SPOTS, WIDTH), f32)
        return peak, weight

    loads["cot"].wait()
    loads["mat2"].wait()
    own_cot[...] = cotangent[...].astype(f32).reshape(TOKENS, WIDTH).astype(bf16)
    cot_left[...] = dot(mat2[...], own_cot[...]).astype(bf16)
    loads["embed"].wait()
    copy_mate.wait_recv()
    stats = [pool_stage(0, PER, embed_near)]
    loads["spread"].wait()
    mix_all(0, PER, 0, SPOTS)
    far_copies[0].wait_recv()
    far_copies[1].wait_recv()
    stats.append(pool_stage(1, FAR, embed_far(0)))
    mix_all(1, FAR, 0, SPOTS)
    far_copies[2].wait_recv()
    far_copies[3].wait_recv()
    copy_cot = remote(cot_left, cot_east, 3, west_id)
    stats.append(pool_stage(2, PER - FAR, embed_far(FAR)))

    peak = stats[0][0]
    for other, _ in stats[1:]:
        peak = jnp.maximum(peak, other)
    decays = [jnp.exp(top - peak) for top, _ in stats]
    inverse = 1.0 / sum(weight * decay for decay, (_, weight) in zip(decays, stats))
    decays = [decay * inverse for decay in decays]
    loads["pool"].wait()

    def finish_pool(lo, hi):
        shares = split_parts(jnp.concatenate([decay[lo:hi] for decay in decays], axis=0))
        size = hi - lo
        pooled = []
        for l in range(LEVELS):
            share = dot(shares, spread[:, l * WIDTH : (l + 1) * WIDTH])
            level = share[:size] * sums[0, l, lo:hi]
            for k in range(1, STAGES):
                level = level + share[k * size : (k + 1) * size] * sums[k, l, lo:hi]
            pooled.append(level)
        projected = dot(jnp.concatenate(pooled, axis=0).astype(bf16), pool_weight[...])
        rows = [
            projected[l * size : (l + 1) * size] + latents[l : l + 1].astype(f32)
            for l in range(LEVELS)
        ]
        return jnp.concatenate(rows, axis=0).astype(bf16)

    mix_all(2, PER - FAR, 0, LEAD)
    lead = finish_pool(0, LEAD)
    loads["mat0"].wait()
    left[...] = dot(mat0[...], lead).astype(bf16)
    copy_left = remote(left, east, 4, west_id)
    mix_all(2, PER - FAR, LEAD, SPOTS)
    stream = jnp.concatenate([lead, finish_pool(LEAD, SPOTS)], axis=0)
    loads["mat1"].wait()
    kept = dot(mat1[...], stream)
    copy_cot.wait_recv()
    loads["mat3"].wait()
    loads["mat4"].wait()
    cot = (dot(mat3[...], own_cot[...]) + dot(mat4[...], cot_east[...])).astype(bf16)
    cot_shifted[...] = cot
    loads["down"].wait()
    for j in range(4):
        back_grad[j] = dot(cot, down_weight[j * 512 : (j + 1) * 512], ((1,), (1,)))
    copy_left.wait_recv()
    own = (kept + dot(mat4[...], east[...])).astype(bf16)
    wide[HALF : HALF + TOKENS] = own
    copy_up = remote(
        wide.at[pl.ds(HALF, HALF)],
        wide.at[pl.ds(HALF + TOKENS, HALF)],
        5,
        (lax.rem(enc + 3, 4), lon),
    )
    copy_down = remote(
        wide.at[pl.ds(TOKENS, HALF)], wide.at[pl.ds(0, HALF)], 6, (lax.rem(enc + 1, 4), lon)
    )

    loads["qkv"].wait()
    norm = normed(own.astype(f32), first_gain[...])
    own_q = dot(norm, qkv_weight[:, :WIDTH])
    own_k = dot(norm, qkv_weight[:, WIDTH : 2 * WIDTH])
    own_v = dot(norm, qkv_weight[:, 2 * WIDTH :])
    row = lax.broadcasted_iota(jnp.int32, (HALO, HALF), 0)
    col = lax.broadcasted_iota(jnp.int32, (HALO, HALF), 1)
    same = lax.rem(row, 2) == lax.rem(col, 2)
    first_key = jnp.where(enc == 0, HALO, 0)
    last_key = jnp.where(enc == 3, HALO, HALF)
    ones = jnp.ones((HALF, 128), f32)
    for win in range(2):
        inside = (col >= first_key) if win == 0 else (col < last_key)
        masks[win * 2] = jnp.where(inside, 0.0, -1e30)
        masks[win * 2 + 1] = jnp.where(inside & same, 0.0, -1e30)
    copy_up.wait_recv()
    copy_down.wait_recv()
    halo = jnp.concatenate([wide[:HALF], wide[HALF + TOKENS :]], axis=0).astype(f32)
    norm = normed(halo, first_gain[...])
    halo_k = dot(norm, qkv_weight[:, WIDTH : 2 * WIDTH])
    halo_v = dot(norm, qkv_weight[:, 2 * WIDTH :])
    for win in range(2):
        for two in range(2):
            at = win * HALF + two * HALO
            rows = slice(at, at + HALO)
            for g in range(4):
                lanes = slice(g * 128, (g + 1) * 128)
                index = (win * 2 + two) * 4 + g
                qs[index] = own_q[rows, lanes]
                key = (halo_k[rows, lanes], own_k[rows, lanes])
                value = (halo_v[rows, lanes], own_v[rows, lanes])
                if win == 1:
                    key, value = key[::-1], value[::-1]
                ks[index] = jnp.concatenate(key, axis=0).astype(bf16)
                value = jnp.concatenate(value, axis=0)
                vs[index] = jnp.concatenate([value, ones], axis=1).astype(bf16)

    lane = lax.broadcasted_iota(jnp.int32, (HALO, 128), 1) // HEAD_WIDTH

    def attend(index, _):
        group = lax.rem(index, 4)
        query = qs[index]
        mask = masks[index // 4]
        stacked = [jnp.where(lane == h, query, 0.0) for h in range(4)]
        raw = dot(jnp.concatenate(stacked, axis=0).astype(bf16), ks[index], ((1,), (1,)))
        exponents = []
        for h in range(4):
            masked = raw[h * HALO : (h + 1) * HALO] + mask
            top = jnp.max(masked, axis=-1, keepdims=True)
            factor = window_temp[group * 4 + h] * (1.0 / math.sqrt(HEAD_WIDTH))
            exponents.append(jnp.exp((masked - top) * factor).astype(bf16).astype(f32))
        exponent = jnp.concatenate(exponents, axis=0).astype(bf16)
        mixed = dot(exponent, vs[index])
        above = mixed[:HALO, :128]
        under = mixed[:HALO, 128:]
        for h in range(1, 4):
            rows = slice(h * HALO, (h + 1) * HALO)
            above = jnp.where(lane == h, mixed[rows, :128], above)
            under = jnp.where(lane == h, mixed[rows, 128:], under)
        attended[index] = above / under
        return 0

    lax.fori_loop(0, 16, attend, 0, unroll=True)

    rows = [
        jnp.concatenate([attended[block * 4 + g] for g in range(4)], axis=1) for block in range(4)
    ]
    loads["proj"].wait()
    mixed = dot(jnp.concatenate(rows, axis=0).astype(bf16), proj_weight[...])
    middle = (own.astype(f32) + mixed).astype(bf16).astype(f32)
    norm = normed(middle, second_gain[...])
    norm2[...] = norm
    norm2_t[...] = norm.T
    total[...] = middle

    got = (got1, got2)
    sizes = [PART_ROWS // 4, PART_ROWS // 64]
    offsets = [0, len(combos[0])]
    starts = []
    for p in range(PARTS):
        at = [0]
        for phase in range(len(PHASES)):
            at.append(at[-1] + chunk_at(p, PHASES[phase], (0, 0)) * sizes[phase])
        starts.append(at)
    pair_id = (mate, lon)
    pair_copies = []
    stores = []
    copies = {}

    def give_pair(index, source, target):
        copy = pltpu.make_async_remote_copy(
            src_ref=source,
            dst_ref=target,
            send_sem=pair_send.at[index],
            recv_sem=pair_recv.at[index],
            device_id=pair_id,
            device_id_type=MESH,
        )
        copy.start()
        pair_copies.append(copy)
        return copy

    def ring_copy(way, p, phase, k, source, target):
        at = offsets[phase] + k
        return pltpu.make_async_remote_copy(
            src_ref=source,
            dst_ref=target,
            send_sem=ring_send.at[way, p, at],
            recv_sem=ring_recv.at[way, p, at],
            device_id=device_for(p, PHASES[phase], combos[phase][k]),
            device_id_type=MESH,
        )

    def scatter(p, phase, make=None):
        size = sizes[phase]
        for k, by in enumerate(combos[phase]):
            target = chunk_at(p, PHASES[phase], by)
            first = pl.multiple_of(starts[p][phase] + target * size, 16)
            if make is not None:
                make(pl.ds(first, size))
            source = work.at[p, pl.ds(first, size)]
            copy = ring_copy(0, p, phase, k, source, got[phase].at[p, k])
            copy.start()
            copies[0, p, phase, k] = copy

    def add_up(p, phase):
        for k in range(len(combos[phase])):
            copies[0, p, phase, k].wait_recv()
        size = sizes[phase]
        first = pl.multiple_of(starts[p][phase + 1], 16)
        held = work[p, pl.ds(first, size), :].astype(f32)
        for k in range(len(combos[phase])):
            held = held + got[phase][p, k].astype(f32)
        if phase == 0:
            work[p, pl.ds(first, size), :] = held.astype(bf16)
            scatter(p, 1)
        else:
            result[core, p, pl.ds(first, size), :] = held.astype(bf16)
            gather(p, 1)

    def gather(p, phase):
        first = pl.multiple_of(starts[p][phase + 1], 16)
        piece = result.at[core, p, pl.ds(first, sizes[phase])]
        for k in range(len(combos[phase])):
            copy = ring_copy(1, p, phase, k, piece, piece)
            copy.start()
            copies[1, p, phase, k] = copy

    def gathered(p, phase):
        for k, by in enumerate(combos[phase]):
            source = chunk_at(p, PHASES[phase], [4 - step for step in by])
            first = pl.multiple_of(starts[p][phase] + source * sizes[phase], 16)
            piece = result.at[core, p, pl.ds(first, sizes[phase])]
            ring_copy(1, p, phase, k, piece, piece).wait_recv()
            if phase == 0:
                give_pair(PARTS + 4 * p + 1 + k, piece, piece)
        if phase == 1:
            gather(p, 0)
            first = pl.multiple_of(starts[p][1], 16)
            piece = result.at[core, p, pl.ds(first, sizes[0])]
            give_pair(PARTS + 4 * p, piece, piece)
        else:
            store(result.at[core, p], whole.at[core, p])

    def store(source, target):
        copy = pltpu.make_async_copy(source, target, store_sem.at[len(stores)])
        copy.start()
        stores.append(copy)

    def paired(p):
        for k in range(4):
            piece = result.at[1 - core, p, pl.ds(0, sizes[0])]
            pltpu.make_async_remote_copy(
                src_ref=piece,
                dst_ref=piece,
                send_sem=pair_send.at[PARTS + 4 * p + k],
                recv_sem=pair_recv.at[PARTS + 4 * p + k],
                device_id=pair_id,
                device_id_type=MESH,
            ).wait_recv()
        store(result.at[1 - core, p], whole.at[1 - core, p])

    def mlp(j):
        columns = slice(j * 512, (j + 1) * 512)
        x = dot(norm2[...], up_weight[:, columns])
        cubic = 0.044715 * (x * x)
        scale = math.sqrt(2.0 / math.pi)
        bend = jnp.tanh(scale * (x * (1.0 + cubic)))
        hidden = (0.5 * x * (1.0 + bend)).astype(bf16)
        hiddens[j] = hidden
        slope = 0.5 * (1.0 + bend) + 0.5 * x * (1.0 - bend * bend) * (scale * (1.0 + 3.0 * cubic))
        slope = (slope * back_grad[j]).astype(bf16)
        down_grad = dot(hidden, cot_shifted[...], ((0,), (0,))).astype(bf16)
        up_grad = dot(norm2_t[...], slope).astype(bf16)
        for i in range(2):
            lanes = slice(i * PART_COLS, (i + 1) * PART_COLS)
            grads[0, j, i * 512 : (i + 1) * 512] = up_grad[:, lanes]
            grads[1, j, i * 512 : (i + 1) * 512] = down_grad[:, lanes]

    def reduce_pair(p):
        pair_copies[p].wait_recv()

        def both(rows):
            work[p, rows, :] = (grads[core, p, rows, :].astype(f32) + pair[p, rows, :].astype(f32)).astype(bf16)

        scatter(p, 0, both)
        both(pl.ds(pl.multiple_of(starts[p][1], 16), sizes[0]))

    loads["up"].wait()
    for j in range(PARTS):
        mlp(j)
        give_pair(j, grads.at[1 - core, j], pair.at[j])
        if j > 1:
            reduce_pair(j - 2)
    reduce_pair(PARTS - 2)
    reduce_pair(PARTS - 1)
    done = total[...]
    for j in range(PARTS):
        done = done + dot(hiddens[j], down_weight[j * 512 : (j + 1) * 512])
    done = done.astype(bf16)
    output[...] = done
    store(output, output_hbm)
    loads["mat5"].wait()
    leave[...] = dot(mat5[...], done).astype(bf16)
    for p in range(PARTS):
        add_up(p, 0)
    copy_back = remote(leave, back, 7, east_id)
    for p in range(PARTS):
        add_up(p, 1)
    for p in range(PARTS):
        gathered(p, 1)
    copy_back.wait_recv()
    store(back, back_hbm)
    for p in range(PARTS):
        gathered(p, 0)
    for p in range(PARTS):
        paired(p)
    for copy in (copy_mate, copy_cot, copy_left, copy_up, copy_down, copy_back, *far_copies):
        copy.wait_send()
    for copy in pair_copies:
        copy.wait_send()
    for copy in copies.values():
        copy.wait_send()
    for copy in stores:
        copy.wait()


def main_call(
    pixels,
    ids,
    embed_weight,
    embed_bias,
    latents,
    query_weight,
    key_weight,
    value_weight,
    pool_weight,
    pool_temp,
    first_gain,
    qkv_weight,
    window_temp,
    proj_weight,
    second_gain,
    up_weight,
    down_weight,
    cot,
):
    vmem = pl.BlockSpec(memory_space=pltpu.VMEM)
    smem = pl.BlockSpec(memory_space=pltpu.SMEM)
    anywhere = pl.BlockSpec(memory_space=pl.ANY)
    matrices = [jnp.asarray(matrix, bf16) for matrix in order_matrices()]
    spread = jnp.asarray(spread_matrix(), bf16)
    loaded = (
        query_weight,
        key_weight,
        embed_weight,
        value_weight,
        pool_weight,
        spread,
        qkv_weight,
        proj_weight,
        up_weight,
        down_weight,
        cot,
        *matrices,
    )
    piece = pltpu.VMEM((HALF, WIDTH), bf16)
    part = pltpu.VMEM((PARTS, PART_ROWS, PART_COLS), bf16)
    return pl.pallas_call(
        main_kernel,
        out_shape=(
            jax.ShapeDtypeStruct((TOKENS, WIDTH), bf16),
            jax.ShapeDtypeStruct((HALF, WIDTH), bf16),
            jax.ShapeDtypeStruct((2, PARTS, PART_ROWS, PART_COLS), bf16),
        ),
        in_specs=[smem] * 3 + [vmem] * 7 + [anywhere] * len(loaded),
        out_specs=(anywhere, anywhere, anywhere),
        scratch_shapes=[
            pltpu.VMEM((TOKENS, WIDTH), bf16),
            pltpu.VMEM((HALF, WIDTH), bf16),
            pltpu.VMEM((2, PARTS, PART_ROWS, PART_COLS), bf16),
        ]
        + [pltpu.VMEM(value.shape, bf16) for value in loaded]
        + [
            pltpu.VMEM((SLOTS, WIDTH), f32),
            pltpu.VMEM((4, PER, SPOTS, PIXELS), bf16),
            pltpu.VMEM((3, PER, SPOTS, PIXELS), bf16),
            pltpu.VMEM((PER, 2 * SPOTS, WIDTH), bf16),
            pltpu.VMEM((2 * PER, SPOTS, 128), f32),
            pltpu.VMEM((2 * PER, SPOTS, WIDTH), f32),
            pltpu.VMEM((STAGES, LEVELS, SPOTS, WIDTH), f32),
            pltpu.VMEM((TOKENS, WIDTH), bf16),
            piece,
            piece,
            piece,
            piece,
            pltpu.VMEM((2 * TOKENS, WIDTH), bf16),
            pltpu.VMEM((TOKENS, WIDTH), bf16),
            pltpu.VMEM((4, TOKENS, 512), f32),
            pltpu.VMEM((16, HALO, 128), f32),
            pltpu.VMEM((16, HALF, 128), bf16),
            pltpu.VMEM((16, HALF, 256), bf16),
            pltpu.VMEM((4, HALO, HALF), f32),
            pltpu.VMEM((16, HALO, 128), f32),
            pltpu.VMEM((TOKENS, WIDTH), bf16),
            pltpu.VMEM((WIDTH, TOKENS), bf16),
            pltpu.VMEM((TOKENS, WIDTH), f32),
            pltpu.VMEM((PARTS, TOKENS, 512), bf16),
            piece,
            pltpu.VMEM((2, PARTS, PART_ROWS, PART_COLS), bf16),
            part,
            part,
            pltpu.VMEM((PARTS, 3, PART_ROWS // 4, PART_COLS), bf16),
            pltpu.VMEM((PARTS, 15, PART_ROWS // 64, PART_COLS), bf16),
            pltpu.SemaphoreType.DMA((len(loaded),)),
            pltpu.SemaphoreType.DMA((2 * PARTS + 2,)),
            pltpu.SemaphoreType.DMA((12,)),
            pltpu.SemaphoreType.DMA((12,)),
            pltpu.SemaphoreType.DMA((2, PARTS, 18)),
            pltpu.SemaphoreType.DMA((2, PARTS, 18)),
            pltpu.SemaphoreType.DMA((5 * PARTS,)),
            pltpu.SemaphoreType.DMA((5 * PARTS,)),
        ],
        compiler_params=pltpu.CompilerParams(
            collective_id=1, has_side_effects=True, vmem_limit_bytes=60 * 1024 * 1024
        ),
        name="main",
    )(
        ids,
        pool_temp,
        window_temp,
        pixels,
        jnp.asarray(pixel_matrix(), bf16),
        latents,
        jnp.asarray(head_rows(), f32),
        first_gain[None, :],
        second_gain[None, :],
        embed_bias,
        *loaded,
    )


def finish_kernel(
    sums,
    shifted_hbm,
    back_hbm,
    keep_hbm,
    take_hbm,
    output_hbm,
    up_hbm,
    down_hbm,
    loaded,
    up_grad,
    down_grad,
    shifted,
    back,
    keep,
    take,
    output,
    load_sem,
    store_sem,
):
    scaling = 1.0 / math.sqrt(NTOK)
    loads = []

    def load(source, target):
        loads.append(pltpu.make_async_copy(source, target, load_sem.at[len(loads)]))
        loads[-1].start()

    for p in range(PARTS):
        load(sums.at[:, p], loaded.at[p])
    load(shifted_hbm, shifted)
    load(back_hbm, back)
    load(keep_hbm, keep)
    load(take_hbm, take)
    stores = []

    def store(source, target):
        stores.append(pltpu.make_async_copy(source, target, store_sem.at[len(stores)]))
        stores[-1].start()

    for p in range(PARTS):
        loads[p].wait()
        wide = slice(p * 512, (p + 1) * 512)
        for i in range(2):
            rows = slice(i * 512, (i + 1) * 512)
            lanes = slice(i * PART_COLS, (i + 1) * PART_COLS)
            up_lanes = slice(p * 512 + i * PART_COLS, p * 512 + (i + 1) * PART_COLS)
            down_grad[wide, lanes] = loaded[p, 1, rows].astype(f32) * scaling
            up_grad[:, up_lanes] = loaded[p, 0, rows].astype(f32) * scaling
        store(down_grad.at[pl.ds(p * 512, 512)], down_hbm.at[pl.ds(p * 512, 512)])
        store(up_grad.at[:, pl.ds(p * 512, 512)], up_hbm.at[:, pl.ds(p * 512, 512)])
    for copy in loads[PARTS:]:
        copy.wait()
    whole = dot(keep[...], shifted[...]) + dot(take[...], back[...])
    output[...] = whole.reshape(SPOTS, LEVELS, WIDTH).astype(bf16)
    store(output, output_hbm)
    for copy in stores:
        copy.wait()


def finish(sums, shifted, back):
    keep, take = final_matrices()
    anywhere = pl.BlockSpec(memory_space=pl.ANY)
    return pl.pallas_call(
        finish_kernel,
        out_shape=(
            jax.ShapeDtypeStruct((SPOTS, LEVELS, WIDTH), bf16),
            jax.ShapeDtypeStruct((WIDTH, FF), f32),
            jax.ShapeDtypeStruct((FF, WIDTH), f32),
        ),
        in_specs=[anywhere] * 5,
        out_specs=(anywhere, anywhere, anywhere),
        scratch_shapes=[
            pltpu.VMEM((PARTS, 2, PART_ROWS, PART_COLS), bf16),
            pltpu.VMEM((WIDTH, FF), f32),
            pltpu.VMEM((FF, WIDTH), f32),
            pltpu.VMEM((TOKENS, WIDTH), bf16),
            pltpu.VMEM((HALF, WIDTH), bf16),
            pltpu.VMEM((TOKENS, TOKENS), bf16),
            pltpu.VMEM((TOKENS, HALF), bf16),
            pltpu.VMEM((SPOTS, LEVELS, WIDTH), bf16),
            pltpu.SemaphoreType.DMA((PARTS + 4,)),
            pltpu.SemaphoreType.DMA((2 * PARTS + 1,)),
        ],
        compiler_params=pltpu.CompilerParams(vmem_limit_bytes=60 * 1024 * 1024),
        name="finish",
    )(
        sums,
        shifted,
        back,
        jnp.asarray(keep, bf16),
        jnp.asarray(take, bf16),
    )


def per_device(
    pixel_field,
    level_ids,
    embed_weight,
    embed_bias,
    latents,
    query_weight,
    key_weight,
    value_weight,
    pool_weight,
    pool_temp,
    first_gain,
    qkv_weight,
    window_temp,
    proj_weight,
    second_gain,
    up_weight,
    down_weight,
    cotangent,
):
    cot = jnp.transpose(cotangent, (1, 2, 0, 3)).reshape(SPOTS, LEVELS, WIDTH)
    shifted, back, sums = main_call(
        jnp.transpose(pixel_field, (0, 3, 1, 2)),
        level_ids,
        embed_weight,
        embed_bias,
        latents,
        query_weight,
        key_weight,
        value_weight,
        pool_weight,
        pool_temp,
        first_gain,
        qkv_weight,
        window_temp,
        proj_weight,
        second_gain,
        up_weight,
        down_weight,
        cot,
    )
    output, up_grad, down_grad = finish(sums, shifted, back)
    output = output.reshape(ROWS, COLS, LEVELS, WIDTH)
    return (jnp.transpose(output, (2, 0, 1, 3)), up_grad, down_grad)


def solution(mesh):
    placed = (P("enc", None, None, "lon"),) + (P(),) * 16 + (P(None, "enc", "lon", None),)
    return jax.shard_map(
        per_device,
        mesh=mesh,
        in_specs=placed,
        out_specs=(P(None, "enc", "lon", None), P(), P()),
        check_vma=False,
    )
```
